128 devices in a mesh: gx: 8 (over x, y_hi), gy: 16 (over z, y_lo, core).
Axes of the slice: x: 4, y: 4 (y_hi: 2, y_lo: 2; y = y_hi * 2 + y_lo), z: 4, core: 2. Of those that a mesh axis runs over, the one named last changes fastest.
Arguments:
- ensemble: bfloat16 [128, 512, 48, 128], P('gx', 'gy'), may hold values from -6 to 6
- obs_cell: int32 [8, 16, 2048], P('gx', 'gy'), may hold values from 0 to 24575
- obs_value: float32 [8, 16, 2048], P('gx', 'gy'), may hold values from -8 to 8
- obs_weight: float32 [8, 16, 2048], P('gx', 'gy'), may hold values from 0.05 to 0.5
- obs_count: int32 [8, 16], replicated, may hold values from 1 to 2048, as said below
Outputs:
- analysis: bfloat16 [128, 512, 48, 128], P('gx', 'gy')
The draws below stay inside these ranges and needn't reach their ends.
Inputs may be any that keep to these rules, and one draw needn't show every extreme that they name: `obs_cell`: each observation lies in its own block's cells. `obs_count`: some block has all 2048 slots live.
All inputs are finite; a program needn't handle non-finite values.
Results may differ from the reference program's by a relative error of at most 0.007.
Values may be sent and summed in bfloat16 or wider, within the bound.
A program may use at most 128 MiB of HBM per device.

```python
import math
import jax
import jax.numpy as jnp
from jax import lax

K = 128
CX = 16
CY = 32
LEV = 48
OBS = 2048
NEWTON = 6
ITERS = 2
BX = 8
BY = 16
NX = 128
NY = 512


def draw_obs_count(key, part):
    key = jax.random.fold_in(key, 7)
    level_key, fill_key, pick_key = jax.random.split(key, 3)
    levels = jax.random.randint(level_key, (BX, BY), 0, 3).astype(jnp.int32)
    ceiling = jnp.right_shift(jnp.full((BX, BY), OBS, jnp.int32), levels)
    raw_draw = jax.random.randint(fill_key, (BX, BY), 0, 1 << 20).astype(jnp.int32)
    counts = 1 + raw_draw % ceiling
    chosen = jax.random.randint(pick_key, (), 0, BX * BY).astype(jnp.int32)
    flat_index = jnp.arange(BX * BY, dtype=jnp.int32).reshape(BX, BY)
    return jnp.where(flat_index == chosen, jnp.int32(OBS), counts).astype(jnp.int32)


def with_ends(values, stream_key, least, high):
    shape = values.shape
    index_at = [jax.random.randint(jax.random.fold_in(stream_key, axis), (), 0, shape[axis]) for axis in range(len(shape))]
    values = values.at[tuple(index_at)].set(least)
    longest = shape.index(max(shape))
    index_at[longest] = (index_at[longest] + 1) % shape[longest]
    return values.at[tuple(index_at)].set(high)


def steps_of(key, extent, cuts, low, top_value):
    def one(axis_at, parts):
        heights = jax.random.uniform(jax.random.fold_in(jax.random.fold_in(key, 6), axis_at), (parts,), jnp.float32, low / len(cuts), top_value / len(cuts))
        return jnp.repeat(jnp.exp(heights), extent[axis_at] // parts).reshape((-1,) + (1,) * (len(extent) - axis_at - 1))

    level = one(*cuts[0])
    for cut in cuts[1:]:
        level = level * one(*cut)
    return level


def centred(stream_key, shape, scale, reach, shards=(), kind=jnp.bfloat16):
    values = jax.random.normal(stream_key, shape, jnp.float32) * scale
    if len(shards) > 0:
        values = steps_of(stream_key, shape, shards, -0.22, 0.18) * values
    return jnp.clip(values, min=-reach, max=reach).astype(kind)


def setup_inputs(seed: int = 0) -> dict:
    key_of = jax.random.split(jax.random.key(seed), 6)
    return {
        "ensemble": centred(key_of[0], (NX, NY, LEV, K), 1.0, 6.0, ((0, 8), (1, 16))),
        "obs_cell": with_ends(jax.random.randint(key_of[1], (BX, BY, OBS), 0, CX * CY * LEV), jax.random.fold_in(key_of[1], 1), 0, (CX * CY * LEV) - 1).astype(jnp.int32),
        "obs_value": centred(key_of[2], (BX, BY, OBS), 3.0, 8.0, ((0, 8), (1, 16)), jnp.float32),
        "obs_weight": jnp.clip(jnp.exp(math.log(0.5) - 2.3025851 * jax.random.uniform(key_of[3], (BX, BY, OBS), jnp.float32) ** steps_of(key_of[3], (BX, BY, OBS), ((0, 8), (1, 16)), -0.2, 0.2)), 0.05, 0.5),
        "obs_count": draw_obs_count(jax.random.fold_in(key_of[5], 71), 0),
    }


RADIUS_WEIGHTS = (0.5, 0.75, 1.0, 0.75, 0.5)
HIGHEST_PRECISION = lax.Precision.HIGHEST

def transform(local_sum):
    order = local_sum.shape[1]
    gram_part = local_sum[:order]
    projected = local_sum[order]
    identity = jnp.eye(order, dtype=jnp.float32)
    system = gram_part + (order - 1) * identity
    frobenius = jnp.sqrt(jnp.sum(system * system))
    root_iter = system / frobenius
    inverse_iter = identity
    for newton_step in range(NEWTON):
        correction = 1.5 * identity - 0.5 * jnp.dot(inverse_iter, root_iter, precision=HIGHEST_PRECISION)
        root_iter = jnp.dot(root_iter, correction, precision=HIGHEST_PRECISION)
        inverse_iter = jnp.dot(correction, inverse_iter, precision=HIGHEST_PRECISION)
    inner = jnp.dot(inverse_iter, projected, precision=HIGHEST_PRECISION)
    mean_weights = jnp.dot(inverse_iter, inner, precision=HIGHEST_PRECISION) / frobenius
    spread = jnp.sqrt((order - 1) / frobenius) * inverse_iter
    return (mean_weights[:, None] + spread).astype(jnp.bfloat16)

def hat_weights(count):
    position = (jnp.arange(count, dtype=jnp.float32) + 0.5) / count
    lower = jnp.maximum(0.0, 0.5 - position)
    upper = jnp.maximum(0.0, position - 0.5)
    return jnp.stack([lower, 1.0 - lower - upper, upper], axis=1)

def apply_block(ensemble_block, centre, nearby):
    size_x, size_y, levels, members = ensemble_block.shape
    deviation = (ensemble_block.astype(jnp.float32) - centre[..., None]).astype(jnp.bfloat16)
    weights_x = hat_weights(size_x)
    weights_y = hat_weights(size_y)
    ranges_x = (slice(0, size_x // 2), slice(0, size_x), slice(size_x // 2, size_x))
    ranges_y = (slice(0, size_y // 2), slice(0, size_y), slice(size_y // 2, size_y))
    total = jnp.zeros(ensemble_block.shape, jnp.float32)
    for index_x in range(3):
        for index_y in range(3):
            portion = deviation[ranges_x[index_x], ranges_y[index_y]]
            product = jnp.dot(portion.reshape(-1, members), nearby[index_x, index_y], preferred_element_type=jnp.float32)
            product = product.reshape(portion.shape)
            factor = weights_x[ranges_x[index_x], index_x][:, None, None, None] * weights_y[ranges_y[index_y], index_y][None, :, None, None]
            total = total.at[ranges_x[index_x], ranges_y[index_y]].add(factor * product)
    return (centre[..., None] + total).astype(jnp.bfloat16)

def block_statistics(arguments):
    flat_rows, centre, obs_cells, values, weights, count = arguments
    capacity = obs_cells.shape[0]
    is_valid = jnp.arange(capacity, dtype=jnp.int32) < count
    scaled = jnp.where(is_valid, weights, jnp.zeros_like(weights))
    picked = flat_rows[obs_cells]
    picked_mean = centre[obs_cells]
    anomaly = (scaled[:, None] * (picked.astype(jnp.float32) - picked_mean[:, None])).astype(jnp.bfloat16)
    innovation = (scaled * (values - picked_mean)).astype(jnp.bfloat16)
    gram_sum = lax.dot_general(anomaly, anomaly, (((0,), (0,)), ((), ())), preferred_element_type=jnp.float32)
    proj_sum = jnp.dot(innovation, anomaly, preferred_element_type=jnp.float32)
    return jnp.concatenate([gram_sum, proj_sum[None]], 0)

def apply_packed(arguments):
    ensemble_block, centre, nearby = arguments
    return apply_block(ensemble_block, centre, nearby)

def reference(ensemble, obs_cell, obs_value, obs_weight, obs_count):
    members = ensemble.shape[3]
    block_data = ensemble.reshape(BX, CX, BY, CY, LEV, members).transpose(0, 2, 1, 3, 4, 5)
    block_data = block_data.reshape(BX * BY, CX, CY, LEV, members)
    for iteration in range(ITERS):
        flat_rows = block_data.reshape(BX * BY, CX * CY * LEV, members)
        centre = lax.optimization_barrier(jnp.mean(flat_rows, axis=2, dtype=jnp.float32))
        packed = lax.map(block_statistics, (flat_rows, centre, obs_cell.reshape(BX * BY, OBS), obs_value.reshape(BX * BY, OBS), obs_weight.reshape(BX * BY, OBS), obs_count.reshape(BX * BY)))
        packed = packed.reshape(BX, BY, members + 1, members)
        local_sum = jnp.zeros_like(packed)
        for offset_x in range(5):
            for offset_y in range(5):
                factor = RADIUS_WEIGHTS[offset_x] * RADIUS_WEIGHTS[offset_y]
                local_sum = local_sum + factor * jnp.roll(packed, (2 - offset_x, 2 - offset_y), (0, 1))
        matrices = jax.vmap(transform)(local_sum.reshape(BX * BY, members + 1, members))
        matrices = matrices.reshape(BX, BY, members, members)
        nearby = jnp.stack([jnp.stack([jnp.roll(matrices, (1 - offset_x, 1 - offset_y), (0, 1)) for offset_y in range(3)], 2) for offset_x in range(3)], 2)
        block_data = lax.map(apply_packed, (block_data, centre.reshape(BX * BY, CX, CY, LEV), nearby.reshape(BX * BY, 3, 3, members, members)))
    result = block_data.reshape(BX, BY, CX, CY, LEV, members).transpose(0, 2, 1, 3, 4, 5)
    return result.reshape(NX, NY, LEV, members)
```

```python
import jax
import jax.numpy as jnp
from jax import lax
from jax.experimental import pallas as pl
from jax.experimental.pallas import tpu as pltpu
from jax.sharding import PartitionSpec as P

K = 128
CX = 16
CY = 32
LEV = 48
ROWS = CX * CY * LEV
XROWS = CY * LEV
OBS = 2048
NEWTON = 6
ITERS = 2
PACK = 72
QUART = 256
GROUP = 4

MESH = pl.DeviceIdType.MESH
F32 = jnp.float32
BF16 = jnp.bfloat16
STAT_STEPS = (-2, -1, 1, 2)
STAT_WEIGHTS = (0.5, 0.75, 0.75, 0.5)
BLEND_STEPS = tuple((a, b) for a in (-1, 0, 1) for b in (-1, 0, 1) if (a, b) != (0, 0))


def slot_of(a, b):
    return (a + 1) * 3 + (b + 1)


def mm(a, b):
    return jnp.dot(a, b, preferred_element_type=F32)


def mm_nt(a, b):
    return lax.dot_general(a, b, (((1,), (1,)), ((), ())), preferred_element_type=F32)


def split(x):
    high = x.astype(BF16)
    low = (x - high.astype(F32)).astype(BF16)
    return high, low


def wide(x):
    high, low = split(x)
    return jnp.concatenate([high, low], axis=1)


def times(a, b):
    both = wide(b)
    out = mm(wide(a), jnp.concatenate([both, both], axis=0))
    return out[:, :K] + out[:, K:]


def iotas(shape):
    return lax.broadcasted_iota(jnp.int32, shape, 0), lax.broadcasted_iota(jnp.int32, shape, 1)


def centring():
    row, col = iotas((K, K))
    return jnp.where(row == col, (K - 1.0) / K, -1.0 / K).astype(BF16)


def pack_stats(total):
    half = K // 2
    row, lane = iotas((half, K))
    top = total[:half]
    turned = pltpu.roll(total[half:K], half, 1)
    body = jnp.where(lane < row, turned, top)
    diagonal = jnp.sum(jnp.where(lane == row, turned, 0.0), axis=0, keepdims=True)
    tail_row, _ = iotas((8, K))
    projected = total[K : K + 1]
    tail = jnp.where(tail_row == 0, diagonal, projected)
    return jnp.concatenate([body, tail], axis=0)


def unpack_stats(packed):
    half = K // 2
    row, lane = iotas((half, K))
    body = packed[:half]
    diagonal = packed[half : half + 1]
    projected = packed[half + 1 : half + 2]
    flipped = jnp.concatenate([body, jnp.zeros((half, K), F32)], axis=0).T
    top = jnp.where(lane < row, flipped[:half], body)
    lower = jnp.where(lane < row, body, jnp.where(lane == row, diagonal, flipped[:half]))
    bottom = jnp.where(lane < half, flipped[half:], pltpu.roll(lower, half, 1))
    return jnp.concatenate([top, bottom], axis=0), projected


def transposed_transform(packed):
    gram, projected = unpack_stats(packed)
    row, col = iotas((K, K))
    identity = jnp.where(row == col, 1.0, 0.0).astype(F32)
    system = gram + (K - 1) * identity
    squares = jnp.sum(system * system, axis=0, keepdims=True)
    frobenius = jnp.sqrt(jnp.sum(squares, axis=1, keepdims=True))
    root = system / frobenius
    carried = jnp.broadcast_to(projected, (16, K))
    correction = 1.5 * identity - 0.5 * root
    out = times(jnp.concatenate([root, carried], axis=0), correction)
    root, carried, inverse = out[:K], out[K:], correction
    for step in range(1, NEWTON):
        correction = 1.5 * identity - 0.5 * times(inverse, root)
        if step < NEWTON - 1:
            out = times(jnp.concatenate([inverse, carried, root], axis=0), correction)
            root = out[K + 16 :]
        else:
            out = times(jnp.concatenate([inverse, carried], axis=0), correction)
        inverse, carried = out[:K], out[K : K + 16]
    weights = times(carried, inverse)[0:1] / frobenius
    return (weights + jnp.sqrt((K - 1) / frobenius) * inverse).astype(BF16)


def hats(position):
    below = jnp.maximum(0.0, 0.5 - position)
    above = jnp.maximum(0.0, position - 0.5)
    return below, 1.0 - below - above, above


def hat_of(j, count):
    position = (j + 0.5) / count
    below, above = max(0.0, 0.5 - position), max(0.0, position - 0.5)
    return below, 1.0 - below - above, above


def apply_column(i, matrix_ref, read, write):
    position = (i.astype(F32) + 0.5) / CX
    weights = hats(position)
    sides = []
    for b in range(3):
        blend = weights[0] * matrix_ref[b * K : (b + 1) * K]
        for a in (1, 2):
            at = (a * 3 + b) * K
            blend = blend + weights[a] * matrix_ref[at : at + K]
        sides.append(wide(blend))
    for half in range(2):
        stationary = jnp.concatenate([sides[half], sides[half + 1]], axis=0)
        for group in range(CY // 2 // GROUP):
            first = half * (CY // 2) + group * GROUP
            block = read(first * LEV, GROUP * LEV)
            out = mm_nt(jnp.concatenate([block, block], axis=1), stationary)
            parts = []
            for j in range(GROUP):
                hat = hat_of(first + j, CY)
                piece = out[j * LEV : (j + 1) * LEV]
                parts.append(hat[half] * piece[:, :K] + hat[half + 1] * piece[:, K:])
            write(first * LEV, GROUP * LEV, jnp.concatenate(parts, axis=0).astype(BF16))


def full_matrices(transforms):
    return mm(transforms, centring()) + 1.0 / K


def first_kernel(
    count_ref, cell_ref, cells_ref, value_ref, weight_ref, ens_ref,
    next_ref, blend_ref,
    ens, ens32, picked, rows, matrices, matrices2, stat_x, stat_y, got_x, got_y, nearby,
    load_sem, store_sem, send_x, recv_x, send_y, recv_y, send_t, recv_t,
):
    gx, gy = lax.axis_index("gx"), lax.axis_index("gy")
    nx, ny = lax.axis_size("gx"), lax.axis_size("gy")

    def at(a, b):
        return (lax.rem(gx + a + nx, nx), lax.rem(gy + b + ny, ny))

    partners = [(s, 0) for s in STAT_STEPS] + [(0, s) for s in STAT_STEPS]
    partners += [(a, b) for a in (-1, 1) for b in (-1, 1)]
    barrier = pltpu.get_barrier_semaphore()
    for a, b in partners:
        pl.semaphore_signal(barrier, inc=1, device_id=at(a, b), device_id_type=MESH)

    def column(ref, i):
        return ref.at[pl.ds(pl.multiple_of(i * XROWS, XROWS), XROWS)]

    @pl.loop(0, CX)
    def _(i):
        pltpu.make_async_copy(column(ens_ref, i), column(ens, i), load_sem.at[i]).start()

    count = count_ref[gx, gy]
    cells = cells_ref[...].astype(F32)
    slot = lax.broadcasted_iota(jnp.int32, (1, OBS), 1)
    rows[0:1] = jnp.where(slot < count, weight_ref[...], 0.0)
    rows[1:2] = value_ref[...]
    east = jnp.floor((cells + 0.5) * (1.0 / XROWS))
    north = jnp.floor((cells - XROWS * east + 0.5) * (1.0 / LEV))
    for first, hat in ((2, hats((east + 0.5) / CX)), (5, hats((north + 0.5) / CY))):
        for k in range(3):
            rows[first + k : first + k + 1] = hat[k]

    @pl.loop(0, CX)
    def _(i):
        pltpu.make_async_copy(column(ens_ref, i), column(ens, i), load_sem.at[i]).wait()
        start = pl.multiple_of(i * XROWS, XROWS)
        ens32[pl.ds(start, XROWS)] = ens[pl.ds(start, XROWS)].astype(F32)

    @pl.loop(0, OBS // 16)
    def _(g):
        for r in range(16):
            o = g * 16 + r
            picked[pl.ds(o, 1)] = ens32[pl.ds(cell_ref[0, o], 1)]

    def accumulate(total, q, deviation, centre):
        lanes = slice(q * QUART, (q + 1) * QUART)
        scale, value = rows[0:1, lanes], rows[1:2, lanes]
        anomaly = (scale * deviation).astype(BF16)
        innovation = jnp.broadcast_to(scale * (value - centre), (16, QUART)).astype(BF16)
        return total + mm_nt(jnp.concatenate([anomaly, innovation], axis=0), anomaly)

    def exchange(t, sent, got, send_sem, recv_sem, shift):
        copies = []
        for k, step in enumerate(STAT_STEPS):
            there = STAT_STEPS.index(-step)
            copies.append(
                pltpu.make_async_remote_copy(
                    src_ref=sent.at[t],
                    dst_ref=got.at[t, there],
                    send_sem=send_sem.at[t, k],
                    recv_sem=recv_sem.at[t, there],
                    device_id=at(*shift(step)),
                    device_id_type=MESH,
                )
            )
        return copies

    def finish(copies):
        for copy in copies:
            copy.wait_recv()
        for copy in copies:
            copy.wait_send()

    def weighted(t, sent, got):
        total = sent[t]
        for k in range(4):
            total = total + STAT_WEIGHTS[k] * got[t, k]
        return total

    def apply_some(first, last):
        @pl.loop(first, last)
        def _(i):
            base = i * XROWS

            def read(start, size):
                return ens[pl.ds(pl.multiple_of(base + start, 16), size)]

            def write(start, size, value):
                ens[pl.ds(pl.multiple_of(base + start, 16), size)] = value

            apply_column(i, matrices, read, write)
            pltpu.make_async_copy(column(ens, i), column(next_ref, i), store_sem.at[i]).start()

    for t in range(ITERS):
        total = jnp.zeros((K + 16, K), F32)
        if t == 0:
            row, col = iotas((K + 16, K))
            centre_rows = jnp.where(row == col, (K - 1.0) / K, jnp.where(row < K, -1.0 / K, 1.0 / K))
            centre_rows = centre_rows.astype(BF16)
            for q in range(OBS // QUART):
                block = picked[q * QUART : (q + 1) * QUART].astype(BF16)
                moved = mm_nt(centre_rows, block)
                total = accumulate(total, q, moved[:K], moved[K : K + 1])
        else:
            matrices2[...] = wide(matrices[...])
            for q in range(OBS // QUART):
                lanes = slice(q * QUART, (q + 1) * QUART)
                block = picked[q * QUART : (q + 1) * QUART].astype(BF16)
                block = jnp.concatenate([block, block], axis=1)
                fresh = jnp.zeros((K, QUART), F32)
                for a in range(3):
                    out = mm_nt(matrices2[a * 3 * K : (a + 1) * 3 * K], block)
                    part = rows[5:6, lanes] * out[:K]
                    part = part + rows[6:7, lanes] * out[K : 2 * K]
                    part = part + rows[7:8, lanes] * out[2 * K :]
                    fresh = fresh + rows[2 + a : 3 + a, lanes] * part
                fresh = fresh.astype(BF16).astype(F32)
                centre = jnp.sum(fresh, axis=0, keepdims=True) * (1.0 / K)
                total = accumulate(total, q, fresh - centre, centre)
        stat_x[t] = pack_stats(total)

        if t == 0:
            pl.semaphore_wait(barrier, len(partners))
        copies = exchange(t, stat_x, got_x, send_x, recv_x, lambda step: (step, 0))
        for copy in copies:
            copy.start()
        if t == 1:
            apply_some(0, 5)
        finish(copies)
        stat_y[t] = weighted(t, stat_x, got_x)
        copies = exchange(t, stat_y, got_y, send_y, recv_y, lambda step: (0, step))
        for copy in copies:
            copy.start()
        if t == 1:
            apply_some(5, 10)
        finish(copies)
        own = slot_of(0, 0) * K
        nearby[t, own : own + K] = transposed_transform(weighted(t, stat_y, got_y))
        copies = []
        for k, (a, b) in enumerate(BLEND_STEPS):
            there = slot_of(-a, -b)
            copies.append(
                pltpu.make_async_remote_copy(
                    src_ref=nearby.at[t, pl.ds(own, K)],
                    dst_ref=nearby.at[t, pl.ds(there * K, K)],
                    send_sem=send_t.at[t, k],
                    recv_sem=recv_t.at[t, there],
                    device_id=at(a, b),
                    device_id_type=MESH,
                )
            )
        for copy in copies:
            copy.start()
        if t == 1:
            apply_some(10, 16)
        finish(copies)
        if t == 0:
            matrices[...] = full_matrices(nearby[t])

    blend_ref[...] = nearby[1]

    @pl.loop(0, CX)
    def _(i):
        pltpu.make_async_copy(column(ens, i), column(next_ref, i), store_sem.at[i]).wait()


def last_kernel(blend_ref, ens_ref, out_ref, matrices):
    i = pl.program_id(0)

    @pl.when(i == 0)
    def _():
        matrices[...] = full_matrices(blend_ref[...])

    def read(start, size):
        return ens_ref[start : start + size]

    def write(start, size, value):
        out_ref[start : start + size] = value

    apply_column(i, matrices, read, write)


def shards(ensemble, obs_cell, obs_value, obs_weight, obs_count):
    flat = ensemble.reshape(ROWS, K)
    cells = obs_cell.reshape(1, OBS)
    vmem = pl.BlockSpec(memory_space=pltpu.VMEM)
    smem = pl.BlockSpec(memory_space=pltpu.SMEM)
    anywhere = pl.BlockSpec(memory_space=pl.ANY)
    dma = pltpu.SemaphoreType.DMA
    following, blend = pl.pallas_call(
        first_kernel,
        out_shape=(
            jax.ShapeDtypeStruct((ROWS, K), BF16),
            jax.ShapeDtypeStruct((9 * K, K), BF16),
        ),
        in_specs=[smem, smem, vmem, vmem, vmem, anywhere],
        out_specs=(anywhere, vmem),
        scratch_shapes=[
            pltpu.VMEM((ROWS, K), BF16),
            pltpu.VMEM((ROWS, K), F32),
            pltpu.VMEM((OBS, K), F32),
            pltpu.VMEM((8, OBS), F32),
            pltpu.VMEM((9 * K, K), F32),
            pltpu.VMEM((9 * K, 2 * K), BF16),
            pltpu.VMEM((ITERS, PACK, K), F32),
            pltpu.VMEM((ITERS, PACK, K), F32),
            pltpu.VMEM((ITERS, 4, PACK, K), F32),
            pltpu.VMEM((ITERS, 4, PACK, K), F32),
            pltpu.VMEM((ITERS, 9 * K, K), BF16),
            dma((CX,)),
            dma((CX,)),
            dma((ITERS, 4)),
            dma((ITERS, 4)),
            dma((ITERS, 4)),
            dma((ITERS, 4)),
            dma((ITERS, 8)),
            dma((ITERS, 9)),
        ],
        compiler_params=pltpu.CompilerParams(
            collective_id=0, has_side_effects=True, vmem_limit_bytes=40 * 1024 * 1024
        ),
        name="analyse",
    )(obs_count, cells, cells, obs_value.reshape(1, OBS), obs_weight.reshape(1, OBS), flat)
    out = pl.pallas_call(
        last_kernel,
        grid=(CX,),
        out_shape=jax.ShapeDtypeStruct((ROWS, K), BF16),
        in_specs=[
            pl.BlockSpec((9 * K, K), lambda i: (0, 0)),
            pl.BlockSpec((XROWS, K), lambda i: (i, 0)),
        ],
        out_specs=pl.BlockSpec((XROWS, K), lambda i: (i, 0)),
        scratch_shapes=[pltpu.VMEM((9 * K, K), F32)],
        compiler_params=pltpu.CompilerParams(vmem_limit_bytes=32 * 1024 * 1024),
        name="blend",
    )(blend, following)
    return out.reshape(ensemble.shape)


def solution(mesh):
    placed = (
        P("gx", "gy", None, None),
        P("gx", "gy", None),
        P("gx", "gy", None),
        P("gx", "gy", None),
        P(),
    )
    return jax.shard_map(
        shards, mesh=mesh, in_specs=placed, out_specs=P("gx", "gy", None, None), check_vma=False
    )
```

```python
import jax
import jax.numpy as jnp
from jax import lax
from jax.experimental import pallas as pl
from jax.experimental.pallas import tpu as pltpu
from jax.sharding import PartitionSpec as P

K = 128
CX = 16
CY = 32
LEV = 48
ROWS = CX * CY * LEV
XROWS = CY * LEV
OBS = 2048
NEWTON = 6
ITERS = 2
PACK = 72
QUART = 256
GROUP = 8
BX = 8
BY = 16

MESH = pl.DeviceIdType.MESH
F32 = jnp.float32
BF16 = jnp.bfloat16
STAT_STEPS = (-1, 1, -2, 2)
STAT_WEIGHTS = (0.75, 0.75, 0.5, 0.5)
BLEND_STEPS = tuple((a, b) for a in (-1, 1, 0) for b in (-1, 1, 0) if (a, b) != (0, 0))


def slot_of(a, b):
    return (a + 1) * 3 + (b + 1)


def mm(a, b):
    return jnp.dot(a, b, preferred_element_type=F32)


def mm_nt(a, b):
    return lax.dot_general(a, b, (((1,), (1,)), ((), ())), preferred_element_type=F32)


def split(x):
    high = x.astype(BF16)
    low = (x - high.astype(F32)).astype(BF16)
    return high, low


def wide(x):
    high, low = split(x)
    return jnp.concatenate([high, low], axis=1)


def times(a, b):
    both = wide(b)
    out = mm(wide(a), jnp.concatenate([both, both], axis=0))
    return out[:, :K] + out[:, K:]


def iotas(shape):
    return lax.broadcasted_iota(jnp.int32, shape, 0), lax.broadcasted_iota(jnp.int32, shape, 1)


def centring():
    row, col = iotas((K, K))
    return jnp.where(row == col, (K - 1.0) / K, -1.0 / K).astype(BF16)


def pack_stats(total):
    half = K // 2
    row, lane = iotas((half, K))
    top = total[:half]
    turned = pltpu.roll(total[half:K], half, 1)
    body = jnp.where(lane < row, turned, top)
    diagonal = jnp.sum(jnp.where(lane == row, turned, 0.0), axis=0, keepdims=True)
    tail_row, _ = iotas((8, K))
    projected = total[K : K + 1]
    tail = jnp.where(tail_row == 0, diagonal, projected)
    return jnp.concatenate([body, tail], axis=0)


def unpack_stats(packed):
    half = K // 2
    row, lane = iotas((half, K))
    body = packed[:half]
    diagonal = packed[half : half + 1]
    projected = packed[half + 1 : half + 2]
    flipped = jnp.concatenate([body, jnp.zeros((half, K), F32)], axis=0).T
    top = jnp.where(lane < row, flipped[:half], body)
    lower = jnp.where(lane < row, body, jnp.where(lane == row, diagonal, flipped[:half]))
    bottom = jnp.where(lane < half, flipped[half:], pltpu.roll(lower, half, 1))
    return jnp.concatenate([top, bottom], axis=0), projected


def transposed_transform(packed):
    gram, projected = unpack_stats(packed)
    row, col = iotas((K, K))
    identity = jnp.where(row == col, 1.0, 0.0).astype(F32)
    system = gram + (K - 1) * identity
    squares = jnp.sum(system * system, axis=0, keepdims=True)
    frobenius = jnp.sqrt(jnp.sum(squares, axis=1, keepdims=True))
    root = system / frobenius
    carried = jnp.broadcast_to(projected, (16, K))
    correction = 1.5 * identity - 0.5 * root
    out = times(jnp.concatenate([root, carried], axis=0), correction)
    root, carried, inverse = out[:K], out[K:], correction
    for step in range(1, NEWTON):
        correction = 1.5 * identity - 0.5 * times(inverse, root)
        if step < NEWTON - 1:
            out = times(jnp.concatenate([inverse, carried, root], axis=0), correction)
            root = out[K + 16 :]
        else:
            out = times(jnp.concatenate([inverse, carried], axis=0), correction)
        inverse, carried = out[:K], out[K : K + 16]
    weights = times(carried, inverse)[0:1] / frobenius
    return (weights + jnp.sqrt((K - 1) / frobenius) * inverse).astype(BF16)


def hats(position):
    below = jnp.maximum(0.0, 0.5 - position)
    above = jnp.maximum(0.0, position - 0.5)
    return below, 1.0 - below - above, above


def hat_of(j, count):
    position = (j + 0.5) / count
    below, above = max(0.0, 0.5 - position), max(0.0, position - 0.5)
    return below, 1.0 - below - above, above


def blend_column(i, slot, matrices, stationary):
    weights = hats((i.astype(F32) + 0.5) / CX)
    for b in range(3):
        blend = weights[0] * matrices[b * K : (b + 1) * K]
        for a in (1, 2):
            at = (a * 3 + b) * K
            blend = blend + weights[a] * matrices[at : at + K]
        stationary[slot, b * K : (b + 1) * K] = wide(blend)


def apply_column(i, slot, ens, stationary):
    for half in range(2):
        matrix = stationary[slot, half * K : half * K + 2 * K]
        for group in range(CY // 2 // GROUP):
            first = half * (CY // 2) + group * GROUP
            here = pl.ds(pl.multiple_of(i * XROWS + first * LEV, 16), GROUP * LEV)
            block = ens[here]
            out = mm_nt(jnp.concatenate([block, block], axis=1), matrix)
            parts = []
            for j in range(GROUP):
                hat = hat_of(first + j, CY)
                piece = out[j * LEV : (j + 1) * LEV]
                parts.append(hat[half] * piece[:, :K] + hat[half + 1] * piece[:, K:])
            ens[here] = jnp.concatenate(parts, axis=0).astype(BF16)


def apply_columns(first, last, matrices, stationary, ens, before, after):
    blend_column(jnp.int32(first), 0, matrices, stationary)

    @pl.loop(first // 2, last // 2)
    def _(pair):
        for slot in range(2):
            before(pair * 2 + slot)
        for slot in range(2):
            i = pair * 2 + slot
            apply_column(i, slot, ens, stationary)
            blend_column(jnp.minimum(i + 1, CX - 1), 1 - slot, matrices, stationary)
        for slot in range(2):
            after(pair * 2 + slot)


def full_matrices(transforms):
    return mm(transforms, centring()) + 1.0 / K


def column(ref, i):
    return ref.at[pl.ds(pl.multiple_of(i * XROWS, XROWS), XROWS)]


def first_kernel(
    count_any, cell_any, value_any, weight_any, ens_any,
    next_ref, blend_ref,
    count_ref, cell_ref, given, cells_ref, ens, ens32, picked, rows, matrices, matrices2, stationary,
    stat_x, stat_y, got_x, got_y, nearby, own_ref,
    small_sem, load_sem, store_sem, own_sem, send_x, recv_x, send_y, recv_y, send_t, recv_t,
):
    gx, gy = lax.axis_index("gx"), lax.axis_index("gy")
    nx, ny = lax.axis_size("gx"), lax.axis_size("gy")

    def at(a, b):
        return (lax.rem(gx + a + nx, nx), lax.rem(gy + b + ny, ny))

    small = [
        pltpu.make_async_copy(count_any, count_ref, small_sem.at[0]),
        pltpu.make_async_copy(cell_any, cell_ref, small_sem.at[1]),
        pltpu.make_async_copy(cell_any, cells_ref, small_sem.at[2]),
        pltpu.make_async_copy(value_any, given.at[0], small_sem.at[3]),
        pltpu.make_async_copy(weight_any, given.at[1], small_sem.at[4]),
    ]
    for copy in small:
        copy.start()

    @pl.loop(0, CX)
    def _(i):
        pltpu.make_async_copy(column(ens_any, i), column(ens, i), load_sem.at[i]).start()

    partners = [(s, 0) for s in STAT_STEPS] + [(0, s) for s in STAT_STEPS]
    partners += [(a, b) for a in (-1, 1) for b in (-1, 1)]
    barrier = pltpu.get_barrier_semaphore()
    for a, b in partners:
        pl.semaphore_signal(barrier, inc=1, device_id=at(a, b), device_id_type=MESH)

    for copy in small:
        copy.wait()
    count = count_ref[gx, gy]
    cells = cells_ref[...].astype(F32)
    slot = lax.broadcasted_iota(jnp.int32, (1, OBS), 1)
    rows[0:1] = jnp.where(slot < count, given[1], 0.0)
    rows[1:2] = given[0]
    east = jnp.floor((cells + 0.5) * (1.0 / XROWS))
    north = jnp.floor((cells - XROWS * east + 0.5) * (1.0 / LEV))
    for first, hat in ((2, hats((east + 0.5) / CX)), (5, hats((north + 0.5) / CY))):
        for k in range(3):
            rows[first + k : first + k + 1] = hat[k]

    @pl.loop(0, CX)
    def _(i):
        pltpu.make_async_copy(column(ens_any, i), column(ens, i), load_sem.at[i]).wait()
        start = pl.multiple_of(i * XROWS, XROWS)
        ens32[pl.ds(start, XROWS)] = ens[pl.ds(start, XROWS)].astype(F32)

    @pl.loop(0, OBS // 16)
    def _(g):
        for r in range(16):
            o = g * 16 + r
            picked[pl.ds(o, 1)] = ens32[pl.ds(cell_ref[0, o], 1)]

    def accumulate(total, q, deviation, centre):
        lanes = slice(q * QUART, (q + 1) * QUART)
        scale, value = rows[0:1, lanes], rows[1:2, lanes]
        anomaly = (scale * deviation).astype(BF16)
        innovation = jnp.broadcast_to(scale * (value - centre), (16, QUART)).astype(BF16)
        return total + mm_nt(jnp.concatenate([anomaly, innovation], axis=0), anomaly)

    def exchange(t, sent, got, send_sem, recv_sem, shift):
        copies = []
        for k, step in enumerate(STAT_STEPS):
            there = STAT_STEPS.index(-step)
            copies.append(
                pltpu.make_async_remote_copy(
                    src_ref=sent.at[t],
                    dst_ref=got.at[t, there],
                    send_sem=send_sem.at[t, k],
                    recv_sem=recv_sem.at[t, there],
                    device_id=at(*shift(step)),
                    device_id_type=MESH,
                )
            )
        return copies

    def finish(copies):
        for copy in copies:
            copy.wait_recv()
        for copy in copies:
            copy.wait_send()

    def weighted(t, sent, got):
        total = sent[t]
        for k in range(4):
            total = total + STAT_WEIGHTS[k] * got[t, k]
        return total

    def nothing(i):
        pass

    def store(i):
        pltpu.make_async_copy(column(ens, i), column(next_ref, i), store_sem.at[i]).start()

    def apply_some(first, last):
        apply_columns(first, last, matrices, stationary, ens, nothing, store)

    for t in range(ITERS):
        total = jnp.zeros((K + 16, K), F32)
        if t == 0:
            row, col = iotas((K + 16, K))
            centre_rows = jnp.where(row == col, (K - 1.0) / K, jnp.where(row < K, -1.0 / K, 1.0 / K))
            centre_rows = centre_rows.astype(BF16)
            for q in range(OBS // QUART):
                block = picked[q * QUART : (q + 1) * QUART].astype(BF16)
                moved = mm_nt(centre_rows, block)
                total = accumulate(total, q, moved[:K], moved[K : K + 1])
        else:
            matrices2[...] = wide(matrices[...])
            for q in range(OBS // QUART):
                lanes = slice(q * QUART, (q + 1) * QUART)
                block = picked[q * QUART : (q + 1) * QUART].astype(BF16)
                block = jnp.concatenate([block, block], axis=1)
                fresh = jnp.zeros((K, QUART), F32)
                for a in range(3):
                    out = mm_nt(matrices2[a * 3 * K : (a + 1) * 3 * K], block)
                    part = rows[5:6, lanes] * out[:K]
                    part = part + rows[6:7, lanes] * out[K : 2 * K]
                    part = part + rows[7:8, lanes] * out[2 * K :]
                    fresh = fresh + rows[2 + a : 3 + a, lanes] * part
                fresh = fresh.astype(BF16).astype(F32)
                centre = jnp.sum(fresh, axis=0, keepdims=True) * (1.0 / K)
                total = accumulate(total, q, fresh - centre, centre)
        stat_x[t] = pack_stats(total)

        if t == 0:
            pl.semaphore_wait(barrier, len(partners))
        copies = exchange(t, stat_x, got_x, send_x, recv_x, lambda step: (step, 0))
        for copy in copies:
            copy.start()
        if t == 1:
            apply_some(0, CX // 2)
        finish(copies)
        stat_y[t] = weighted(t, stat_x, got_x)
        copies = exchange(t, stat_y, got_y, send_y, recv_y, lambda step: (0, step))
        for copy in copies:
            copy.start()
        if t == 1:
            apply_some(CX // 2, CX)
        finish(copies)
        own_ref[t] = transposed_transform(weighted(t, stat_y, got_y))
        landing = nearby if t == 0 else blend_ref
        copies = []
        for k, (a, b) in enumerate(BLEND_STEPS):
            there = slot_of(-a, -b)
            copies.append(
                pltpu.make_async_remote_copy(
                    src_ref=own_ref.at[t],
                    dst_ref=landing.at[pl.ds(there * K, K)],
                    send_sem=send_t.at[t, k],
                    recv_sem=recv_t.at[t, there],
                    device_id=at(a, b),
                    device_id_type=MESH,
                )
            )
        for copy in copies:
            copy.start()
        own = slot_of(0, 0) * K
        mine = pltpu.make_async_copy(own_ref.at[t], landing.at[pl.ds(own, K)], own_sem.at[t])
        mine.start()
        finish(copies)
        mine.wait()
        if t == 0:
            matrices[...] = full_matrices(nearby[...])

    @pl.loop(0, CX)
    def _(i):
        pltpu.make_async_copy(column(ens, i), column(next_ref, i), store_sem.at[i]).wait()


def last_kernel(blend_any, ens_any, out_any, nearby, ens, matrices, stationary, blend_sem, load_sem, store_sem):
    get = pltpu.make_async_copy(blend_any, nearby, blend_sem)
    get.start()

    @pl.loop(0, CX)
    def _(i):
        pltpu.make_async_copy(column(ens_any, i), column(ens, i), load_sem.at[i]).start()

    get.wait()
    matrices[...] = full_matrices(nearby[...])

    def load(i):
        pltpu.make_async_copy(column(ens_any, i), column(ens, i), load_sem.at[i]).wait()

    def store(i):
        pltpu.make_async_copy(column(ens, i), column(out_any, i), store_sem.at[i]).start()

    apply_columns(0, CX, matrices, stationary, ens, load, store)

    @pl.loop(0, CX)
    def _(i):
        pltpu.make_async_copy(column(ens, i), column(out_any, i), store_sem.at[i]).wait()


def shards(ensemble, obs_cell, obs_value, obs_weight, obs_count):
    flat = ensemble.reshape(ROWS, K)
    anywhere = pl.BlockSpec(memory_space=pl.ANY)
    dma = pltpu.SemaphoreType.DMA
    following, blend = pl.pallas_call(
        first_kernel,
        out_shape=(
            jax.ShapeDtypeStruct((ROWS, K), BF16),
            jax.ShapeDtypeStruct((9 * K, K), BF16),
        ),
        in_specs=[anywhere] * 5,
        out_specs=(anywhere, anywhere),
        scratch_shapes=[
            pltpu.SMEM((BX, BY), jnp.int32),
            pltpu.SMEM((1, OBS), jnp.int32),
            pltpu.VMEM((2, 1, OBS), F32),
            pltpu.VMEM((1, OBS), jnp.int32),
            pltpu.VMEM((ROWS, K), BF16),
            pltpu.VMEM((ROWS, K), F32),
            pltpu.VMEM((OBS, K), F32),
            pltpu.VMEM((8, OBS), F32),
            pltpu.VMEM((9 * K, K), F32),
            pltpu.VMEM((9 * K, 2 * K), BF16),
            pltpu.VMEM((2, 3 * K, 2 * K), BF16),
            pltpu.VMEM((ITERS, PACK, K), F32),
            pltpu.VMEM((ITERS, PACK, K), F32),
            pltpu.VMEM((ITERS, 4, PACK, K), F32),
            pltpu.VMEM((ITERS, 4, PACK, K), F32),
            pltpu.VMEM((9 * K, K), BF16),
            pltpu.VMEM((ITERS, K, K), BF16),
            dma((5,)),
            dma((CX,)),
            dma((CX,)),
            dma((ITERS,)),
            dma((ITERS, 4)),
            dma((ITERS, 4)),
            dma((ITERS, 4)),
            dma((ITERS, 4)),
            dma((ITERS, 8)),
            dma((ITERS, 9)),
        ],
        compiler_params=pltpu.CompilerParams(
            collective_id=0, has_side_effects=True, vmem_limit_bytes=58 * 1024 * 1024
        ),
        name="analyse",
    )(
        obs_count,
        obs_cell.reshape(1, OBS),
        obs_value.reshape(1, OBS),
        obs_weight.reshape(1, OBS),
        flat,
    )
    out = pl.pallas_call(
        last_kernel,
        out_shape=jax.ShapeDtypeStruct((ROWS, K), BF16),
        in_specs=[anywhere] * 2,
        out_specs=anywhere,
        scratch_shapes=[
            pltpu.VMEM((9 * K, K), BF16),
            pltpu.VMEM((ROWS, K), BF16),
            pltpu.VMEM((9 * K, K), F32),
            pltpu.VMEM((2, 3 * K, 2 * K), BF16),
            dma(()),
            dma((CX,)),
            dma((CX,)),
        ],
        compiler_params=pltpu.CompilerParams(vmem_limit_bytes=58 * 1024 * 1024),
        name="blend",
    )(blend, following)
    return out.reshape(ensemble.shape)


def solution(mesh):
    placed = (
        P("gx", "gy", None, None),
        P("gx", "gy", None),
        P("gx", "gy", None),
        P("gx", "gy", None),
        P(),
    )
    return jax.shard_map(
        shards, mesh=mesh, in_specs=placed, out_specs=P("gx", "gy", None, None), check_vma=False
    )
```

```python
import jax
import jax.numpy as jnp
from jax import lax
from jax.experimental import pallas as pl
from jax.experimental.pallas import tpu as pltpu
from jax.sharding import PartitionSpec as P

K = 128
CX = 16
CY = 32
LEV = 48
ROWS = CX * CY * LEV
XROWS = CY * LEV
OBS = 2048
NEWTON = 6
ITERS = 2
PACK = 72
QUART = 256
GROUP = 8
BX = 8
BY = 16

MESH = pl.DeviceIdType.MESH
F32 = jnp.float32
BF16 = jnp.bfloat16
STAT_STEPS = (-1, 1, -2, 2)
STAT_WEIGHTS = (0.75, 0.75, 0.5, 0.5)
BLEND_STEPS = tuple((a, b) for a in (-1, 1, 0) for b in (-1, 1, 0) if (a, b) != (0, 0))


def slot_of(a, b):
    return (a + 1) * 3 + (b + 1)


def mm(a, b):
    return jnp.dot(a, b, preferred_element_type=F32)


def mm_nt(a, b):
    return lax.dot_general(a, b, (((1,), (1,)), ((), ())), preferred_element_type=F32)


def split(x):
    high = x.astype(BF16)
    low = (x - high.astype(F32)).astype(BF16)
    return high, low


def wide(x):
    high, low = split(x)
    return jnp.concatenate([high, low], axis=1)


def times(a, b):
    both = wide(b)
    out = mm(wide(a), jnp.concatenate([both, both], axis=0))
    return out[:, :K] + out[:, K:]


def iotas(shape):
    return lax.broadcasted_iota(jnp.int32, shape, 0), lax.broadcasted_iota(jnp.int32, shape, 1)


def centring():
    row, col = iotas((K, K))
    return jnp.where(row == col, (K - 1.0) / K, -1.0 / K).astype(BF16)


def pack_stats(total):
    half = K // 2
    row, lane = iotas((half, K))
    top = total[:half]
    turned = pltpu.roll(total[half:K], half, 1)
    body = jnp.where(lane < row, turned, top)
    diagonal = jnp.sum(jnp.where(lane == row, turned, 0.0), axis=0, keepdims=True)
    tail_row, _ = iotas((8, K))
    projected = total[K : K + 1]
    tail = jnp.where(tail_row == 0, diagonal, projected)
    return jnp.concatenate([body, tail], axis=0)


def unpack_stats(packed):
    half = K // 2
    row, lane = iotas((half, K))
    body = packed[:half]
    diagonal = packed[half : half + 1]
    projected = packed[half + 1 : half + 2]
    flipped = jnp.concatenate([body, jnp.zeros((half, K), F32)], axis=0).T
    top = jnp.where(lane < row, flipped[:half], body)
    lower = jnp.where(lane < row, body, jnp.where(lane == row, diagonal, flipped[:half]))
    bottom = jnp.where(lane < half, flipped[half:], pltpu.roll(lower, half, 1))
    return jnp.concatenate([top, bottom], axis=0), projected


def transposed_transform(packed):
    gram, projected = unpack_stats(packed)
    row, col = iotas((K, K))
    identity = jnp.where(row == col, 1.0, 0.0).astype(F32)
    system = gram + (K - 1) * identity
    squares = jnp.sum(system * system, axis=0, keepdims=True)
    frobenius = jnp.sqrt(jnp.sum(squares, axis=1, keepdims=True))
    root = system / frobenius
    carried = jnp.broadcast_to(projected, (16, K))
    correction = 1.5 * identity - 0.5 * root
    out = times(jnp.concatenate([root, carried], axis=0), correction)
    root, carried, inverse = out[:K], out[K:], correction
    for step in range(1, NEWTON):
        correction = 1.5 * identity - 0.5 * times(inverse, root)
        if step < NEWTON - 1:
            out = times(jnp.concatenate([inverse, carried, root], axis=0), correction)
            root = out[K + 16 :]
        else:
            out = times(jnp.concatenate([inverse, carried], axis=0), correction)
        inverse, carried = out[:K], out[K : K + 16]
    weights = times(carried, inverse)[0:1] / frobenius
    return (weights + jnp.sqrt((K - 1) / frobenius) * inverse).astype(BF16)


def hats(position):
    below = jnp.maximum(0.0, 0.5 - position)
    above = jnp.maximum(0.0, position - 0.5)
    return below, 1.0 - below - above, above


def hat_of(j, count):
    position = (j + 0.5) / count
    below, above = max(0.0, 0.5 - position), max(0.0, position - 0.5)
    return below, 1.0 - below - above, above


def blend_column(i, slot, matrices, stationary):
    weights = hats((i.astype(F32) + 0.5) / CX)
    for b in range(3):
        blend = weights[0] * matrices[b * K : (b + 1) * K]
        for a in (1, 2):
            at = (a * 3 + b) * K
            blend = blend + weights[a] * matrices[at : at + K]
        stationary[slot, b * K : (b + 1) * K] = wide(blend)


def apply_column(i, slot, ens, fresh, stationary):
    for half in range(2):
        matrix = stationary[slot, half * K : half * K + 2 * K]
        for group in range(CY // 2 // GROUP):
            first = half * (CY // 2) + group * GROUP
            here = pl.ds(pl.multiple_of(i * XROWS + first * LEV, 16), GROUP * LEV)
            block = ens[here]
            out = mm_nt(jnp.concatenate([block, block], axis=1), matrix)
            parts = []
            for j in range(GROUP):
                hat = hat_of(first + j, CY)
                piece = out[j * LEV : (j + 1) * LEV]
                parts.append(hat[half] * piece[:, :K] + hat[half + 1] * piece[:, K:])
            fresh[here] = jnp.concatenate(parts, axis=0).astype(BF16)


def apply_columns(first, last, matrices, stationary, ens, fresh, before, after):
    blend_column(jnp.int32(first), 0, matrices, stationary)

    @pl.loop(first // 2, last // 2)
    def _(pair):
        for slot in range(2):
            before(pair * 2 + slot)
        for slot in range(2):
            i = pair * 2 + slot
            apply_column(i, slot, ens, fresh, stationary)
            blend_column(jnp.minimum(i + 1, CX - 1), 1 - slot, matrices, stationary)
        for slot in range(2):
            after(pair * 2 + slot)


def full_matrices(transforms):
    return mm(transforms, centring()) + 1.0 / K


def column(ref, i):
    return ref.at[pl.ds(pl.multiple_of(i * XROWS, XROWS), XROWS)]


def first_kernel(
    count_any, cell_any, value_any, weight_any, ens_any,
    next_ref, blend_ref,
    count_ref, cell_ref, given, cells_ref, ens, applied, ens32, picked, rows, matrices, matrices2, stationary,
    stat_x, stat_y, got_x, got_y, nearby, own_ref,
    small_sem, load_sem, store_sem, own_sem, send_x, recv_x, send_y, recv_y, send_t, recv_t,
):
    gx, gy = lax.axis_index("gx"), lax.axis_index("gy")
    nx, ny = lax.axis_size("gx"), lax.axis_size("gy")

    def at(a, b):
        return (lax.rem(gx + a + nx, nx), lax.rem(gy + b + ny, ny))

    small = [
        pltpu.make_async_copy(count_any, count_ref, small_sem.at[0]),
        pltpu.make_async_copy(cell_any, cell_ref, small_sem.at[1]),
        pltpu.make_async_copy(cell_any, cells_ref, small_sem.at[2]),
        pltpu.make_async_copy(value_any, given.at[0], small_sem.at[3]),
        pltpu.make_async_copy(weight_any, given.at[1], small_sem.at[4]),
    ]
    for copy in small:
        copy.start()

    @pl.loop(0, CX)
    def _(i):
        pltpu.make_async_copy(column(ens_any, i), column(ens, i), load_sem.at[i]).start()

    partners = [(s, 0) for s in STAT_STEPS] + [(0, s) for s in STAT_STEPS]
    partners += [(a, b) for a in (-1, 1) for b in (-1, 1)]
    barrier = pltpu.get_barrier_semaphore()
    for a, b in partners:
        pl.semaphore_signal(barrier, inc=1, device_id=at(a, b), device_id_type=MESH)

    for copy in small:
        copy.wait()
    count = count_ref[gx, gy]
    cells = cells_ref[...].astype(F32)
    slot = lax.broadcasted_iota(jnp.int32, (1, OBS), 1)
    rows[0:1] = jnp.where(slot < count, given[1], 0.0)
    rows[1:2] = given[0]
    east = jnp.floor((cells + 0.5) * (1.0 / XROWS))
    north = jnp.floor((cells - XROWS * east + 0.5) * (1.0 / LEV))
    for first, hat in ((2, hats((east + 0.5) / CX)), (5, hats((north + 0.5) / CY))):
        for k in range(3):
            rows[first + k : first + k + 1] = hat[k]

    @pl.loop(0, CX)
    def _(i):
        pltpu.make_async_copy(column(ens_any, i), column(ens, i), load_sem.at[i]).wait()
        start = pl.multiple_of(i * XROWS, XROWS)
        ens32[pl.ds(start, XROWS)] = ens[pl.ds(start, XROWS)].astype(F32)

    @pl.loop(0, OBS // 16)
    def _(g):
        for r in range(16):
            o = g * 16 + r
            picked[pl.ds(o, 1)] = ens32[pl.ds(cell_ref[0, o], 1)]

    def accumulate(total, q, deviation, centre):
        lanes = slice(q * QUART, (q + 1) * QUART)
        scale, value = rows[0:1, lanes], rows[1:2, lanes]
        anomaly = (scale * deviation).astype(BF16)
        innovation = jnp.broadcast_to(scale * (value - centre), (16, QUART)).astype(BF16)
        return total + mm_nt(jnp.concatenate([anomaly, innovation], axis=0), anomaly)

    def exchange(t, sent, got, send_sem, recv_sem, shift):
        copies = []
        for k, step in enumerate(STAT_STEPS):
            there = STAT_STEPS.index(-step)
            copies.append(
                pltpu.make_async_remote_copy(
                    src_ref=sent.at[t],
                    dst_ref=got.at[t, there],
                    send_sem=send_sem.at[t, k],
                    recv_sem=recv_sem.at[t, there],
                    device_id=at(*shift(step)),
                    device_id_type=MESH,
                )
            )
        return copies

    def finish(copies):
        for copy in copies:
            copy.wait_recv()
        for copy in copies:
            copy.wait_send()

    def weighted(t, sent, got):
        total = sent[t]
        for k in range(4):
            total = total + STAT_WEIGHTS[k] * got[t, k]
        return total

    def nothing(i):
        pass

    def store(i):
        pltpu.make_async_copy(column(applied, i), column(next_ref, i), store_sem.at[i]).start()

    def apply_some(first, last):
        apply_columns(first, last, matrices, stationary, ens, applied, nothing, store)

    for t in range(ITERS):
        total = jnp.zeros((K + 16, K), F32)
        if t == 0:
            row, col = iotas((K + 16, K))
            centre_rows = jnp.where(row == col, (K - 1.0) / K, jnp.where(row < K, -1.0 / K, 1.0 / K))
            centre_rows = centre_rows.astype(BF16)
            for q in range(OBS // QUART):
                block = picked[q * QUART : (q + 1) * QUART].astype(BF16)
                moved = mm_nt(centre_rows, block)
                total = accumulate(total, q, moved[:K], moved[K : K + 1])
        else:
            matrices2[...] = wide(matrices[...])
            for q in range(OBS // QUART):
                lanes = slice(q * QUART, (q + 1) * QUART)
                block = picked[q * QUART : (q + 1) * QUART].astype(BF16)
                block = jnp.concatenate([block, block], axis=1)
                fresh = jnp.zeros((K, QUART), F32)
                for a in range(3):
                    out = mm_nt(matrices2[a * 3 * K : (a + 1) * 3 * K], block)
                    part = rows[5:6, lanes] * out[:K]
                    part = part + rows[6:7, lanes] * out[K : 2 * K]
                    part = part + rows[7:8, lanes] * out[2 * K :]
                    fresh = fresh + rows[2 + a : 3 + a, lanes] * part
                fresh = fresh.astype(BF16).astype(F32)
                centre = jnp.sum(fresh, axis=0, keepdims=True) * (1.0 / K)
                total = accumulate(total, q, fresh - centre, centre)
        stat_x[t] = pack_stats(total)

        if t == 0:
            pl.semaphore_wait(barrier, len(partners))
        copies = exchange(t, stat_x, got_x, send_x, recv_x, lambda step: (step, 0))
        for copy in copies:
            copy.start()
        if t == 1:
            apply_some(0, CX // 2)
        finish(copies)
        stat_y[t] = weighted(t, stat_x, got_x)
        copies = exchange(t, stat_y, got_y, send_y, recv_y, lambda step: (0, step))
        for copy in copies:
            copy.start()
        if t == 1:
            apply_some(CX // 2, CX)
        finish(copies)
        own_ref[t] = transposed_transform(weighted(t, stat_y, got_y))
        landing = nearby if t == 0 else blend_ref
        copies = []
        for k, (a, b) in enumerate(BLEND_STEPS):
            there = slot_of(-a, -b)
            copies.append(
                pltpu.make_async_remote_copy(
                    src_ref=own_ref.at[t],
                    dst_ref=landing.at[pl.ds(there * K, K)],
                    send_sem=send_t.at[t, k],
                    recv_sem=recv_t.at[t, there],
                    device_id=at(a, b),
                    device_id_type=MESH,
                )
            )
        for copy in copies:
            copy.start()
        own = slot_of(0, 0) * K
        mine = pltpu.make_async_copy(own_ref.at[t], landing.at[pl.ds(own, K)], own_sem.at[t])
        mine.start()
        finish(copies)
        mine.wait()
        if t == 0:
            matrices[...] = full_matrices(nearby[...])

    @pl.loop(0, CX)
    def _(i):
        pltpu.make_async_copy(column(applied, i), column(next_ref, i), store_sem.at[i]).wait()


def last_kernel(blend_any, ens_any, out_any, nearby, ens, applied, matrices, stationary, blend_sem, load_sem, store_sem):
    get = pltpu.make_async_copy(blend_any, nearby, blend_sem)
    get.start()

    @pl.loop(0, CX)
    def _(i):
        pltpu.make_async_copy(column(ens_any, i), column(ens, i), load_sem.at[i]).start()

    get.wait()
    matrices[...] = full_matrices(nearby[...])

    def load(i):
        pltpu.make_async_copy(column(ens_any, i), column(ens, i), load_sem.at[i]).wait()

    def store(i):
        pltpu.make_async_copy(column(applied, i), column(out_any, i), store_sem.at[i]).start()

    apply_columns(0, CX, matrices, stationary, ens, applied, load, store)

    @pl.loop(0, CX)
    def _(i):
        pltpu.make_async_copy(column(applied, i), column(out_any, i), store_sem.at[i]).wait()


def shards(ensemble, obs_cell, obs_value, obs_weight, obs_count):
    flat = ensemble.reshape(ROWS, K)
    anywhere = pl.BlockSpec(memory_space=pl.ANY)
    dma = pltpu.SemaphoreType.DMA
    following, blend = pl.pallas_call(
        first_kernel,
        out_shape=(
            jax.ShapeDtypeStruct((ROWS, K), BF16),
            jax.ShapeDtypeStruct((9 * K, K), BF16),
        ),
        in_specs=[anywhere] * 5,
        out_specs=(anywhere, anywhere),
        scratch_shapes=[
            pltpu.SMEM((BX, BY), jnp.int32),
            pltpu.SMEM((1, OBS), jnp.int32),
            pltpu.VMEM((2, 1, OBS), F32),
            pltpu.VMEM((1, OBS), jnp.int32),
            pltpu.VMEM((ROWS, K), BF16),
            pltpu.VMEM((ROWS, K), BF16),
            pltpu.VMEM((ROWS, K), F32),
            pltpu.VMEM((OBS, K), F32),
            pltpu.VMEM((8, OBS), F32),
            pltpu.VMEM((9 * K, K), F32),
            pltpu.VMEM((9 * K, 2 * K), BF16),
            pltpu.VMEM((2, 3 * K, 2 * K), BF16),
            pltpu.VMEM((ITERS, PACK, K), F32),
            pltpu.VMEM((ITERS, PACK, K), F32),
            pltpu.VMEM((ITERS, 4, PACK, K), F32),
            pltpu.VMEM((ITERS, 4, PACK, K), F32),
            pltpu.VMEM((9 * K, K), BF16),
            pltpu.VMEM((ITERS, K, K), BF16),
            dma((5,)),
            dma((CX,)),
            dma((CX,)),
            dma((ITERS,)),
            dma((ITERS, 4)),
            dma((ITERS, 4)),
            dma((ITERS, 4)),
            dma((ITERS, 4)),
            dma((ITERS, 8)),
            dma((ITERS, 9)),
        ],
        compiler_params=pltpu.CompilerParams(
            collective_id=0, has_side_effects=True, vmem_limit_bytes=58 * 1024 * 1024
        ),
        name="analyse",
    )(
        obs_count,
        obs_cell.reshape(1, OBS),
        obs_value.reshape(1, OBS),
        obs_weight.reshape(1, OBS),
        flat,
    )
    out = pl.pallas_call(
        last_kernel,
        out_shape=jax.ShapeDtypeStruct((ROWS, K), BF16),
        in_specs=[anywhere] * 2,
        out_specs=anywhere,
        scratch_shapes=[
            pltpu.VMEM((9 * K, K), BF16),
            pltpu.VMEM((ROWS, K), BF16),
            pltpu.VMEM((ROWS, K), BF16),
            pltpu.VMEM((9 * K, K), F32),
            pltpu.VMEM((2, 3 * K, 2 * K), BF16),
            dma(()),
            dma((CX,)),
            dma((CX,)),
        ],
        compiler_params=pltpu.CompilerParams(vmem_limit_bytes=58 * 1024 * 1024),
        name="blend",
    )(blend, following)
    return out.reshape(ensemble.shape)


def solution(mesh):
    placed = (
        P("gx", "gy", None, None),
        P("gx", "gy", None),
        P("gx", "gy", None),
        P("gx", "gy", None),
        P(),
    )
    return jax.shard_map(
        shards, mesh=mesh, in_specs=placed, out_specs=P("gx", "gy", None, None), check_vma=False
    )
```

```python
import jax
import jax.numpy as jnp
from jax import lax
from jax.experimental import pallas as pl
from jax.experimental.pallas import tpu as pltpu
from jax.sharding import PartitionSpec as P

K = 128
CX = 16
CY = 32
LEV = 48
ROWS = CX * CY * LEV
XROWS = CY * LEV
OBS = 2048
NEWTON = 6
ITERS = 2
PACK = 72
QUART = 256
GROUP = 8
UNROLL = 4
GATHER = 64
PACKED = 80
BX = 8
BY = 16

MESH = pl.DeviceIdType.MESH
F32 = jnp.float32
BF16 = jnp.bfloat16
STAT_STEPS = (-1, 1, -2, 2)
STAT_WEIGHTS = (0.75, 0.75, 0.5, 0.5)
BLEND_STEPS = tuple((a, b) for a in (-1, 1, 0) for b in (-1, 1, 0) if (a, b) != (0, 0))


def slot_of(a, b):
    return (a + 1) * 3 + (b + 1)


def mm(a, b):
    return jnp.dot(a, b, preferred_element_type=F32)


def mm_nt(a, b):
    return lax.dot_general(a, b, (((1,), (1,)), ((), ())), preferred_element_type=F32)


def split(x):
    high = x.astype(BF16)
    low = (x - high.astype(F32)).astype(BF16)
    return high, low


def wide(x):
    high, low = split(x)
    return jnp.concatenate([high, low], axis=1)


def times(a, b):
    both = wide(b)
    out = mm(wide(a), jnp.concatenate([both, both], axis=0))
    return out[:, :K] + out[:, K:]


def iotas(shape):
    return lax.broadcasted_iota(jnp.int32, shape, 0), lax.broadcasted_iota(jnp.int32, shape, 1)


def centring():
    row, col = iotas((K, K))
    return jnp.where(row == col, (K - 1.0) / K, -1.0 / K).astype(BF16)


def fold(matrix):
    half = K // 2
    row, lane = iotas((half, K))
    return jnp.where(lane < row, pltpu.roll(matrix[half:], half, 1), matrix[:half])


def unfold(body, diagonal):
    half = K // 2
    row, lane = iotas((half, K))
    flipped = jnp.concatenate([body, jnp.zeros((half, K), F32)], axis=0).T
    top = jnp.where(lane < row, flipped[:half], body)
    lower = jnp.where(lane < row, body, flipped[:half])
    bottom = jnp.where(lane < half, flipped[half:], pltpu.roll(lower, half, 1))
    row, col = iotas((K, K))
    return jnp.where(row == col, diagonal, jnp.concatenate([top, bottom], axis=0))


def diagonal_of(matrix):
    row, col = iotas((K, K))
    return jnp.sum(jnp.where(row == col, matrix, 0.0), axis=0, keepdims=True)


def pack_stats(total):
    gram = total[:K]
    tail_row, _ = iotas((PACK - K // 2, K))
    tail = jnp.where(tail_row == 0, diagonal_of(gram), total[K : K + 1])
    return jnp.concatenate([fold(gram), tail], axis=0)


def unpack_stats(packed):
    half = K // 2
    return unfold(packed[:half], packed[half : half + 1]), packed[half + 1 : half + 2]


def pack_transform(spread, weights):
    tail_row, _ = iotas((PACKED - K // 2, K))
    tail = jnp.zeros((PACKED - K // 2, K), F32)
    for k, line in enumerate((diagonal_of(spread), weights)):
        high, low = split(line)
        tail = jnp.where(tail_row == 2 * k, high.astype(F32), tail)
        tail = jnp.where(tail_row == 2 * k + 1, low.astype(F32), tail)
    return jnp.concatenate([fold(spread), tail], axis=0).astype(BF16)


def unpack_transform(packed):
    half = K // 2
    packed = packed.astype(F32)
    diagonal = packed[half : half + 1] + packed[half + 1 : half + 2]
    weights = packed[half + 2 : half + 3] + packed[half + 3 : half + 4]
    return (weights + unfold(packed[:half], diagonal)).astype(BF16)


def transform_parts(packed):
    gram, projected = unpack_stats(packed)
    row, col = iotas((K, K))
    identity = jnp.where(row == col, 1.0, 0.0).astype(F32)
    system = gram + (K - 1) * identity
    squares = jnp.sum(system * system, axis=0, keepdims=True)
    frobenius = jnp.sqrt(jnp.sum(squares, axis=1, keepdims=True))
    root = system / frobenius
    carried = jnp.broadcast_to(projected, (16, K))
    correction = 1.5 * identity - 0.5 * root
    root, carried, inverse = times(root, correction), times(carried, correction), correction
    for step in range(1, NEWTON):
        correction = 1.5 * identity - 0.5 * times(inverse, root)
        out = times(jnp.concatenate([inverse, carried], axis=0), correction)
        if step < NEWTON - 1:
            root = times(root, correction)
        inverse, carried = out[:K], out[K:]
    weights = times(carried, inverse)[0:1] / frobenius
    return jnp.sqrt((K - 1) / frobenius) * inverse, weights


def hats(position):
    below = jnp.maximum(0.0, 0.5 - position)
    above = jnp.maximum(0.0, position - 0.5)
    return below, 1.0 - below - above, above


def hat_of(j, count):
    position = (j + 0.5) / count
    below, above = max(0.0, 0.5 - position), max(0.0, position - 0.5)
    return below, 1.0 - below - above, above


def blend_column(i, slot, matrices, stationary):
    weights = hats((i.astype(F32) + 0.5) / CX)
    for b in range(3):
        blend = weights[0] * matrices[b * K : (b + 1) * K]
        for a in (1, 2):
            at = (a * 3 + b) * K
            blend = blend + weights[a] * matrices[at : at + K]
        stationary[slot, b * K : (b + 1) * K] = wide(blend)


def apply_column(i, slot, ens, fresh, stationary):
    for half in range(2):
        matrix = stationary[slot, half * K : half * K + 2 * K]
        for group in range(CY // 2 // GROUP):
            first = half * (CY // 2) + group * GROUP
            here = pl.ds(pl.multiple_of(i * XROWS + first * LEV, 16), GROUP * LEV)
            block = ens[here]
            out = mm_nt(jnp.concatenate([block, block], axis=1), matrix)
            parts = []
            for j in range(GROUP):
                hat = hat_of(first + j, CY)
                piece = out[j * LEV : (j + 1) * LEV]
                parts.append(hat[half] * piece[:, :K] + hat[half + 1] * piece[:, K:])
            fresh[here] = jnp.concatenate(parts, axis=0).astype(BF16)


def apply_columns(first, last, matrices, stationary, ens, fresh, before, after):
    blend_column(jnp.int32(first), 0, matrices, stationary)

    @pl.loop(first // UNROLL, last // UNROLL)
    def _(step):
        for k in range(UNROLL):
            before(step * UNROLL + k)
        for k in range(UNROLL):
            i = step * UNROLL + k
            apply_column(i, k % 2, ens, fresh, stationary)
            blend_column(jnp.minimum(i + 1, CX - 1), 1 - k % 2, matrices, stationary)
        for k in range(UNROLL):
            after(step * UNROLL + k)


def full_matrices(transforms):
    return mm(transforms, centring()) + 1.0 / K


def column(ref, i):
    return ref.at[pl.ds(pl.multiple_of(i * XROWS, XROWS), XROWS)]


def first_kernel(
    count_any, cell_any, value_any, weight_any, ens_any,
    next_ref, blend_ref,
    count_ref, cell_ref, given, cells_ref, ens, applied, ens32, picked, rows, deviations, matrices, stationary,
    stat_x, stat_y, got_x, got_y, nearby, transforms, own_ref,
    small_sem, load_sem, store_sem, own_sem, send_x, recv_x, send_y, recv_y, send_t, recv_t,
):
    gx, gy = lax.axis_index("gx"), lax.axis_index("gy")
    nx, ny = lax.axis_size("gx"), lax.axis_size("gy")

    def at(a, b):
        return (lax.rem(gx + a + nx, nx), lax.rem(gy + b + ny, ny))

    small = [
        pltpu.make_async_copy(count_any, count_ref, small_sem.at[0]),
        pltpu.make_async_copy(cell_any, cell_ref, small_sem.at[1]),
        pltpu.make_async_copy(cell_any, cells_ref, small_sem.at[2]),
        pltpu.make_async_copy(value_any, given.at[0], small_sem.at[3]),
        pltpu.make_async_copy(weight_any, given.at[1], small_sem.at[4]),
    ]
    for copy in small:
        copy.start()

    @pl.loop(0, CX)
    def _(i):
        pltpu.make_async_copy(column(ens_any, i), column(ens, i), load_sem.at[i]).start()

    partners = [(s, 0) for s in STAT_STEPS] + [(0, s) for s in STAT_STEPS]
    partners += [(a, b) for a in (-1, 1) for b in (-1, 1)]
    barrier = pltpu.get_barrier_semaphore()
    for a, b in partners:
        pl.semaphore_signal(barrier, inc=1, device_id=at(a, b), device_id_type=MESH)

    for copy in small:
        copy.wait()
    count = count_ref[gx, gy]
    cells = cells_ref[...].astype(F32)
    slot = lax.broadcasted_iota(jnp.int32, (1, OBS), 1)
    rows[0:1] = jnp.where(slot < count, given[1], 0.0)
    rows[1:2] = given[0]
    east = jnp.floor((cells + 0.5) * (1.0 / XROWS))
    north = jnp.floor((cells - XROWS * east + 0.5) * (1.0 / LEV))
    for first, hat in ((2, hats((east + 0.5) / CX)), (5, hats((north + 0.5) / CY))):
        for k in range(3):
            rows[first + k : first + k + 1] = hat[k]

    @pl.loop(0, CX)
    def _(i):
        pltpu.make_async_copy(column(ens_any, i), column(ens, i), load_sem.at[i]).wait()
        start = pl.multiple_of(i * XROWS, XROWS)
        ens32[pl.ds(start, XROWS)] = ens[pl.ds(start, XROWS)].astype(F32)

    @pl.loop(0, OBS // GATHER)
    def _(g):
        for r in range(GATHER):
            o = g * GATHER + r
            picked[pl.ds(o, 1)] = ens32[pl.ds(cell_ref[0, o], 1)]

    def accumulate(total, lanes, deviation, centre):
        scale, value = rows[0:1, lanes], rows[1:2, lanes]
        anomaly = (scale * deviation).astype(BF16)
        innovation = jnp.broadcast_to(scale * (value - centre), (16, QUART)).astype(BF16)
        return total + mm_nt(jnp.concatenate([anomaly, innovation], axis=0), anomaly)

    def exchange(t, sent, got, send_sem, recv_sem, shift):
        copies = []
        for k, step in enumerate(STAT_STEPS):
            there = STAT_STEPS.index(-step)
            copies.append(
                pltpu.make_async_remote_copy(
                    src_ref=sent.at[t],
                    dst_ref=got.at[t, there],
                    send_sem=send_sem.at[t, k],
                    recv_sem=recv_sem.at[t, there],
                    device_id=at(*shift(step)),
                    device_id_type=MESH,
                )
            )
        return copies

    def finish(copies):
        for copy in copies:
            copy.wait_recv()
        for copy in copies:
            copy.wait_send()

    def weighted(t, sent, got):
        total = sent[t]
        for k in range(4):
            total = total + STAT_WEIGHTS[k] * got[t, k]
        return total

    def nothing(i):
        pass

    def store(i):
        pltpu.make_async_copy(column(applied, i), column(next_ref, i), store_sem.at[i]).start()

    def apply_some(first, last):
        apply_columns(first, last, matrices, stationary, ens, applied, nothing, store)

    for t in range(ITERS):
        total = jnp.zeros((K + 16, K), F32)
        if t == 0:
            row, col = iotas((K + 16, K))
            centre_rows = jnp.where(row == col, (K - 1.0) / K, jnp.where(row < K, -1.0 / K, 1.0 / K))
            centre_rows = centre_rows.astype(BF16)
            for q in range(OBS // QUART):
                lanes = slice(q * QUART, (q + 1) * QUART)
                moved = mm_nt(centre_rows, picked[lanes].astype(BF16))
                total = accumulate(total, lanes, moved[:K], moved[K : K + 1])
                deviations[:, lanes] = moved[:K].astype(BF16)
                rows[8:9, lanes] = moved[K : K + 1]
        else:
            for q in range(OBS // QUART):
                lanes = slice(q * QUART, (q + 1) * QUART)
                out = mm(transforms[...], deviations[:, lanes])
                fresh = rows[8:9, lanes]
                for a in range(3):
                    at_a = a * 3 * K
                    part = rows[5:6, lanes] * out[at_a : at_a + K]
                    part = part + rows[6:7, lanes] * out[at_a + K : at_a + 2 * K]
                    part = part + rows[7:8, lanes] * out[at_a + 2 * K : at_a + 3 * K]
                    fresh = fresh + rows[2 + a : 3 + a, lanes] * part
                fresh = fresh.astype(BF16).astype(F32)
                centre = jnp.sum(fresh, axis=0, keepdims=True) * (1.0 / K)
                total = accumulate(total, lanes, fresh - centre, centre)
        stat_x[t] = pack_stats(total)

        if t == 0:
            pl.semaphore_wait(barrier, len(partners))
        copies = exchange(t, stat_x, got_x, send_x, recv_x, lambda step: (step, 0))
        for copy in copies:
            copy.start()
        if t == 1:
            matrices[...] = full_matrices(transforms[...])
            apply_some(0, CX // 2)
        finish(copies)
        stat_y[t] = weighted(t, stat_x, got_x)
        copies = exchange(t, stat_y, got_y, send_y, recv_y, lambda step: (0, step))
        for copy in copies:
            copy.start()
        if t == 1:
            apply_some(CX // 2, CX)
        finish(copies)
        spread, weights = transform_parts(weighted(t, stat_y, got_y))
        own_ref[t] = pack_transform(spread, weights)
        landing = nearby if t == 0 else blend_ref
        copies = {}
        for k, (a, b) in enumerate(BLEND_STEPS):
            there = slot_of(-a, -b)
            copies[(-a, -b)] = pltpu.make_async_remote_copy(
                src_ref=own_ref.at[t],
                dst_ref=landing.at[there],
                send_sem=send_t.at[t, k],
                recv_sem=recv_t.at[t, there],
                device_id=at(a, b),
                device_id_type=MESH,
            )
        for copy in copies.values():
            copy.start()
        own = slot_of(0, 0)
        if t == 0:
            transforms[own * K : (own + 1) * K] = (weights + spread).astype(BF16)
        else:
            mine = pltpu.make_async_copy(own_ref.at[t], landing.at[own], own_sem)
            mine.start()
        for step in reversed(BLEND_STEPS):
            copies[step].wait_recv()
            if t == 0:
                slot = slot_of(*step)
                transforms[slot * K : (slot + 1) * K] = unpack_transform(nearby[slot])
        if t == 1:
            mine.wait()
        for copy in copies.values():
            copy.wait_send()

    @pl.loop(0, CX)
    def _(i):
        pltpu.make_async_copy(column(applied, i), column(next_ref, i), store_sem.at[i]).wait()


def last_kernel(blend_any, ens_any, out_any, nearby, ens, applied, transforms, matrices, stationary, blend_sem, load_sem, store_sem):
    get = pltpu.make_async_copy(blend_any, nearby, blend_sem)
    get.start()

    @pl.loop(0, CX)
    def _(i):
        pltpu.make_async_copy(column(ens_any, i), column(ens, i), load_sem.at[i]).start()

    get.wait()
    for slot in range(9):
        transforms[slot * K : (slot + 1) * K] = unpack_transform(nearby[slot])
    matrices[...] = full_matrices(transforms[...])

    def load(i):
        pltpu.make_async_copy(column(ens_any, i), column(ens, i), load_sem.at[i]).wait()

    def store(i):
        pltpu.make_async_copy(column(applied, i), column(out_any, i), store_sem.at[i]).start()

    apply_columns(0, CX, matrices, stationary, ens, applied, load, store)

    @pl.loop(0, CX)
    def _(i):
        pltpu.make_async_copy(column(applied, i), column(out_any, i), store_sem.at[i]).wait()


def shards(ensemble, obs_cell, obs_value, obs_weight, obs_count):
    flat = ensemble.reshape(ROWS, K)
    anywhere = pl.BlockSpec(memory_space=pl.ANY)
    dma = pltpu.SemaphoreType.DMA
    following, blend = pl.pallas_call(
        first_kernel,
        out_shape=(
            jax.ShapeDtypeStruct((ROWS, K), BF16),
            jax.ShapeDtypeStruct((9, PACKED, K), BF16),
        ),
        in_specs=[anywhere] * 5,
        out_specs=(anywhere, anywhere),
        scratch_shapes=[
            pltpu.SMEM((BX, BY), jnp.int32),
            pltpu.SMEM((1, OBS), jnp.int32),
            pltpu.VMEM((2, 1, OBS), F32),
            pltpu.VMEM((1, OBS), jnp.int32),
            pltpu.VMEM((ROWS, K), BF16),
            pltpu.VMEM((ROWS, K), BF16),
            pltpu.VMEM((ROWS, K), F32),
            pltpu.VMEM((OBS, K), F32),
            pltpu.VMEM((16, OBS), F32),
            pltpu.VMEM((K, OBS), BF16),
            pltpu.VMEM((9 * K, K), F32),
            pltpu.VMEM((2, 3 * K, 2 * K), BF16),
            pltpu.VMEM((ITERS, PACK, K), F32),
            pltpu.VMEM((ITERS, PACK, K), F32),
            pltpu.VMEM((ITERS, 4, PACK, K), F32),
            pltpu.VMEM((ITERS, 4, PACK, K), F32),
            pltpu.VMEM((9, PACKED, K), BF16),
            pltpu.VMEM((9 * K, K), BF16),
            pltpu.VMEM((ITERS, PACKED, K), BF16),
            dma((5,)),
            dma((CX,)),
            dma((CX,)),
            dma(()),
            dma((ITERS, 4)),
            dma((ITERS, 4)),
            dma((ITERS, 4)),
            dma((ITERS, 4)),
            dma((ITERS, 8)),
            dma((ITERS, 9)),
        ],
        compiler_params=pltpu.CompilerParams(
            collective_id=0, has_side_effects=True, vmem_limit_bytes=58 * 1024 * 1024
        ),
        name="analyse",
    )(
        obs_count,
        obs_cell.reshape(1, OBS),
        obs_value.reshape(1, OBS),
        obs_weight.reshape(1, OBS),
        flat,
    )
    out = pl.pallas_call(
        last_kernel,
        out_shape=jax.ShapeDtypeStruct((ROWS, K), BF16),
        in_specs=[anywhere] * 2,
        out_specs=anywhere,
        scratch_shapes=[
            pltpu.VMEM((9, PACKED, K), BF16),
            pltpu.VMEM((ROWS, K), BF16),
            pltpu.VMEM((ROWS, K), BF16),
            pltpu.VMEM((9 * K, K), BF16),
            pltpu.VMEM((9 * K, K), F32),
            pltpu.VMEM((2, 3 * K, 2 * K), BF16),
            dma(()),
            dma((CX,)),
            dma((CX,)),
        ],
        compiler_params=pltpu.CompilerParams(vmem_limit_bytes=58 * 1024 * 1024),
        name="blend",
    )(blend, following)
    return out.reshape(ensemble.shape)


def solution(mesh):
    placed = (
        P("gx", "gy", None, None),
        P("gx", "gy", None),
        P("gx", "gy", None),
        P("gx", "gy", None),
        P(),
    )
    return jax.shard_map(
        shards, mesh=mesh, in_specs=placed, out_specs=P("gx", "gy", None, None), check_vma=False
    )
```

```python
import jax
import jax.numpy as jnp
from jax import lax
from jax.experimental import pallas as pl
from jax.experimental.pallas import tpu as pltpu
from jax.sharding import PartitionSpec as P

K = 128
CX = 16
CY = 32
LEV = 48
ROWS = CX * CY * LEV
XROWS = CY * LEV
OBS = 2048
NEWTON = 6
ITERS = 2
PACK = 72
QUART = 512
GROUP = 8
UNROLL = 4
GATHER = 64
PACKED = 80
BX = 8
BY = 16

MESH = pl.DeviceIdType.MESH
F32 = jnp.float32
BF16 = jnp.bfloat16
STAT_STEPS = (-1, 1, -2, 2)
STAT_WEIGHTS = (0.75, 0.75, 0.5, 0.5)
BLEND_STEPS = tuple((a, b) for a in (-1, 1, 0) for b in (-1, 1, 0) if (a, b) != (0, 0))


def slot_of(a, b):
    return (a + 1) * 3 + (b + 1)


def mm(a, b):
    return jnp.dot(a, b, preferred_element_type=F32)


def mm_nt(a, b):
    return lax.dot_general(a, b, (((1,), (1,)), ((), ())), preferred_element_type=F32)


def split(x):
    high = x.astype(BF16)
    low = (x - high.astype(F32)).astype(BF16)
    return high, low


def wide(x):
    high, low = split(x)
    return jnp.concatenate([high, low], axis=1)


def times(a, b):
    both = wide(b)
    out = mm(wide(a), jnp.concatenate([both, both], axis=0))
    return out[:, :K] + out[:, K:]


def iotas(shape):
    return lax.broadcasted_iota(jnp.int32, shape, 0), lax.broadcasted_iota(jnp.int32, shape, 1)


def centring():
    row, col = iotas((K, K))
    return jnp.where(row == col, (K - 1.0) / K, -1.0 / K).astype(BF16)


def fold(matrix):
    half = K // 2
    row, lane = iotas((half, K))
    return jnp.where(lane < row, pltpu.roll(matrix[half:], half, 1), matrix[:half])


def unfold(body, diagonal):
    half = K // 2
    row, lane = iotas((half, K))
    flipped = jnp.concatenate([body, jnp.zeros((half, K), F32)], axis=0).T
    top = jnp.where(lane < row, flipped[:half], body)
    lower = jnp.where(lane < row, body, flipped[:half])
    bottom = jnp.where(lane < half, flipped[half:], pltpu.roll(lower, half, 1))
    row, col = iotas((K, K))
    return jnp.where(row == col, diagonal, jnp.concatenate([top, bottom], axis=0))


def diagonal_of(matrix):
    row, col = iotas((K, K))
    return jnp.sum(jnp.where(row == col, matrix, 0.0), axis=0, keepdims=True)


def pack_stats(total):
    gram = total[:K]
    tail_row, _ = iotas((PACK - K // 2, K))
    tail = jnp.where(tail_row == 0, diagonal_of(gram), total[K : K + 1])
    return jnp.concatenate([fold(gram), tail], axis=0)


def unpack_stats(packed):
    half = K // 2
    return unfold(packed[:half], packed[half : half + 1]), packed[half + 1 : half + 2]


def pack_transform(spread, weights):
    tail_row, _ = iotas((PACKED - K // 2, K))
    tail = jnp.zeros((PACKED - K // 2, K), F32)
    for k, line in enumerate((diagonal_of(spread), weights)):
        high, low = split(line)
        tail = jnp.where(tail_row == 2 * k, high.astype(F32), tail)
        tail = jnp.where(tail_row == 2 * k + 1, low.astype(F32), tail)
    return jnp.concatenate([fold(spread), tail], axis=0).astype(BF16)


def unpack_transform(packed):
    half = K // 2
    packed = packed.astype(F32)
    diagonal = packed[half : half + 1] + packed[half + 1 : half + 2]
    weights = packed[half + 2 : half + 3] + packed[half + 3 : half + 4]
    return (weights + unfold(packed[:half], diagonal)).astype(BF16)


def transform_parts(packed):
    gram, projected = unpack_stats(packed)
    row, col = iotas((K, K))
    identity = jnp.where(row == col, 1.0, 0.0).astype(F32)
    system = gram + (K - 1) * identity
    squares = jnp.sum(system * system, axis=0, keepdims=True)
    frobenius = jnp.sqrt(jnp.sum(squares, axis=1, keepdims=True))
    root = system / frobenius
    correction = 1.5 * identity - 0.5 * root
    root, inverse = times(correction, root), correction
    for step in range(1, NEWTON - 1):
        correction = 1.5 * identity - 0.5 * times(inverse, root)
        root, inverse = times(correction, root), times(correction, inverse)
    correction = 1.5 * identity - 0.5 * times(inverse, root)
    carried = times(jnp.broadcast_to(projected, (16, K)), inverse)
    carried, inverse = times(carried, correction), times(correction, inverse)
    weights = times(carried, inverse)[0:1] / frobenius
    return jnp.sqrt((K - 1) / frobenius) * inverse, weights


def hats(position):
    below = jnp.maximum(0.0, 0.5 - position)
    above = jnp.maximum(0.0, position - 0.5)
    return below, 1.0 - below - above, above


def hat_of(j, count):
    position = (j + 0.5) / count
    below, above = max(0.0, 0.5 - position), max(0.0, position - 0.5)
    return below, 1.0 - below - above, above


def blend_column(i, slot, matrices, stationary):
    weights = hats((i.astype(F32) + 0.5) / CX)
    for b in range(3):
        blend = weights[0] * matrices[b * K : (b + 1) * K]
        for a in (1, 2):
            at = (a * 3 + b) * K
            blend = blend + weights[a] * matrices[at : at + K]
        stationary[slot, b * K : (b + 1) * K] = wide(blend)


def apply_column(i, slot, ens, fresh, stationary):
    for half in range(2):
        matrix = stationary[slot, half * K : half * K + 2 * K]
        for group in range(CY // 2 // GROUP):
            first = half * (CY // 2) + group * GROUP
            here = pl.ds(pl.multiple_of(i * XROWS + first * LEV, 16), GROUP * LEV)
            block = ens[here]
            out = mm_nt(jnp.concatenate([block, block], axis=1), matrix)
            parts = []
            for j in range(GROUP):
                hat = hat_of(first + j, CY)
                piece = out[j * LEV : (j + 1) * LEV]
                parts.append(hat[half] * piece[:, :K] + hat[half + 1] * piece[:, K:])
            fresh[here] = jnp.concatenate(parts, axis=0).astype(BF16)


def apply_columns(first, last, matrices, stationary, ens, fresh, before, after):
    blend_column(jnp.int32(first), 0, matrices, stationary)

    @pl.loop(first // UNROLL, last // UNROLL)
    def _(step):
        for k in range(UNROLL):
            before(step * UNROLL + k)
        for k in range(UNROLL):
            i = step * UNROLL + k
            apply_column(i, k % 2, ens, fresh, stationary)
            after(i)
            blend_column(jnp.minimum(i + 1, CX - 1), 1 - k % 2, matrices, stationary)


def full_matrices(transforms):
    return mm(transforms, centring()) + 1.0 / K


def column(ref, i):
    return ref.at[pl.ds(pl.multiple_of(i * XROWS, XROWS), XROWS)]


def first_kernel(
    count_any, cell_any, value_any, weight_any, ens_any,
    next_ref, blend_ref,
    count_ref, cell_ref, given, cells_ref, ens, applied, ens32, picked, rows, deviations, matrices, stationary,
    stat_x, stat_y, got_x, got_y, nearby, transforms, own_ref,
    small_sem, load_sem, store_sem, own_sem, send_x, recv_x, send_y, recv_y, send_t, recv_t,
):
    gx, gy = lax.axis_index("gx"), lax.axis_index("gy")
    nx, ny = lax.axis_size("gx"), lax.axis_size("gy")

    def at(a, b):
        return (lax.rem(gx + a + nx, nx), lax.rem(gy + b + ny, ny))

    small = [
        pltpu.make_async_copy(count_any, count_ref, small_sem.at[0]),
        pltpu.make_async_copy(cell_any, cell_ref, small_sem.at[1]),
        pltpu.make_async_copy(cell_any, cells_ref, small_sem.at[2]),
        pltpu.make_async_copy(value_any, given.at[0], small_sem.at[3]),
        pltpu.make_async_copy(weight_any, given.at[1], small_sem.at[4]),
    ]
    for copy in small:
        copy.start()

    @pl.loop(0, CX)
    def _(i):
        pltpu.make_async_copy(column(ens_any, i), column(ens, i), load_sem.at[i]).start()

    partners = [(s, 0) for s in STAT_STEPS] + [(0, s) for s in STAT_STEPS]
    partners += [(a, b) for a in (-1, 1) for b in (-1, 1)]
    barrier = pltpu.get_barrier_semaphore()
    for a, b in partners:
        pl.semaphore_signal(barrier, inc=1, device_id=at(a, b), device_id_type=MESH)

    for copy in small:
        copy.wait()
    count = count_ref[gx, gy]
    cells = cells_ref[...].astype(F32)
    slot = lax.broadcasted_iota(jnp.int32, (1, OBS), 1)
    rows[0:1] = jnp.where(slot < count, given[1], 0.0)
    rows[1:2] = given[0]
    east = jnp.floor((cells + 0.5) * (1.0 / XROWS))
    north = jnp.floor((cells - XROWS * east + 0.5) * (1.0 / LEV))
    for first, hat in ((2, hats((east + 0.5) / CX)), (5, hats((north + 0.5) / CY))):
        for k in range(3):
            rows[first + k : first + k + 1] = hat[k]

    @pl.loop(0, CX)
    def _(i):
        pltpu.make_async_copy(column(ens_any, i), column(ens, i), load_sem.at[i]).wait()
        start = pl.multiple_of(i * XROWS, XROWS)
        ens32[pl.ds(start, XROWS)] = ens[pl.ds(start, XROWS)].astype(F32)

    @pl.loop(0, OBS // GATHER)
    def _(g):
        for r in range(GATHER):
            o = g * GATHER + r
            picked[pl.ds(o, 1)] = ens32[pl.ds(cell_ref[0, o], 1)]

    def accumulate(total, lanes, deviation, centre):
        scale, value = rows[0:1, lanes], rows[1:2, lanes]
        anomaly = (scale * deviation).astype(BF16)
        innovation = jnp.broadcast_to(scale * (value - centre), (16, QUART)).astype(BF16)
        return total + mm_nt(jnp.concatenate([anomaly, innovation], axis=0), anomaly)

    def exchange(t, sent, got, send_sem, recv_sem, shift):
        copies = []
        for k, step in enumerate(STAT_STEPS):
            there = STAT_STEPS.index(-step)
            copies.append(
                pltpu.make_async_remote_copy(
                    src_ref=sent.at[t],
                    dst_ref=got.at[t, there],
                    send_sem=send_sem.at[t, k],
                    recv_sem=recv_sem.at[t, there],
                    device_id=at(*shift(step)),
                    device_id_type=MESH,
                )
            )
        return copies

    pending = []

    def settle():
        while pending:
            pending.pop().wait_send()

    def weighted(t, sent, got, copies):
        total = sent[t]
        for k in reversed(range(4)):
            copies[STAT_STEPS.index(-STAT_STEPS[k])].wait_recv()
            total = total + STAT_WEIGHTS[k] * got[t, k]
        pending.extend(copies)
        return total

    def nothing(i):
        pass

    def store(i):
        pltpu.make_async_copy(column(applied, i), column(next_ref, i), store_sem.at[i]).start()

    def apply_some(first, last):
        apply_columns(first, last, matrices, stationary, ens, applied, nothing, store)

    for t in range(ITERS):
        total = jnp.zeros((K + 16, K), F32)
        if t == 0:
            row, col = iotas((K + 16, K))
            centre_rows = jnp.where(row == col, (K - 1.0) / K, jnp.where(row < K, -1.0 / K, 1.0 / K))
            centre_rows = centre_rows.astype(BF16)
            for q in range(OBS // QUART):
                lanes = slice(q * QUART, (q + 1) * QUART)
                moved = mm_nt(centre_rows, picked[lanes].astype(BF16))
                total = accumulate(total, lanes, moved[:K], moved[K : K + 1])
                deviations[:, lanes] = moved[:K].astype(BF16)
                rows[8:9, lanes] = moved[K : K + 1]
        else:
            for q in range(OBS // QUART):
                lanes = slice(q * QUART, (q + 1) * QUART)
                out = mm(transforms[...], deviations[:, lanes])
                fresh = rows[8:9, lanes]
                for a in range(3):
                    at_a = a * 3 * K
                    part = rows[5:6, lanes] * out[at_a : at_a + K]
                    part = part + rows[6:7, lanes] * out[at_a + K : at_a + 2 * K]
                    part = part + rows[7:8, lanes] * out[at_a + 2 * K : at_a + 3 * K]
                    fresh = fresh + rows[2 + a : 3 + a, lanes] * part
                fresh = fresh.astype(BF16).astype(F32)
                centre = jnp.sum(fresh, axis=0, keepdims=True) * (1.0 / K)
                total = accumulate(total, lanes, fresh - centre, centre)
        stat_x[t] = pack_stats(total)

        if t == 0:
            pl.semaphore_wait(barrier, len(partners))
        copies = exchange(t, stat_x, got_x, send_x, recv_x, lambda step: (step, 0))
        for copy in copies:
            copy.start()
        if t == 1:
            matrices[...] = full_matrices(transforms[...])
            apply_some(0, CX // 2)
            settle()
        stat_y[t] = weighted(t, stat_x, got_x, copies)
        copies = exchange(t, stat_y, got_y, send_y, recv_y, lambda step: (0, step))
        for copy in copies:
            copy.start()
        if t == 1:
            apply_some(CX // 2, CX)
        spread, weights = transform_parts(weighted(t, stat_y, got_y, copies))
        own_ref[t] = pack_transform(spread, weights)
        landing = nearby if t == 0 else blend_ref
        copies = {}
        for k, (a, b) in enumerate(BLEND_STEPS):
            there = slot_of(-a, -b)
            copies[(-a, -b)] = pltpu.make_async_remote_copy(
                src_ref=own_ref.at[t],
                dst_ref=landing.at[there],
                send_sem=send_t.at[t, k],
                recv_sem=recv_t.at[t, there],
                device_id=at(a, b),
                device_id_type=MESH,
            )
        for copy in copies.values():
            copy.start()
        own = slot_of(0, 0)
        if t == 0:
            transforms[own * K : (own + 1) * K] = (weights + spread).astype(BF16)
        else:
            mine = pltpu.make_async_copy(own_ref.at[t], landing.at[own], own_sem)
            mine.start()
            settle()
        for step in reversed(BLEND_STEPS):
            copies[step].wait_recv()
            if t == 0:
                slot = slot_of(*step)
                transforms[slot * K : (slot + 1) * K] = unpack_transform(nearby[slot])
        if t == 1:
            mine.wait()
        pending.extend(copies.values())
    settle()

    @pl.loop(0, CX)
    def _(i):
        pltpu.make_async_copy(column(applied, i), column(next_ref, i), store_sem.at[i]).wait()


def last_kernel(blend_any, ens_any, out_any, nearby, ens, applied, transforms, matrices, stationary, blend_sem, load_sem, store_sem):
    get = pltpu.make_async_copy(blend_any, nearby, blend_sem)
    get.start()

    @pl.loop(0, CX)
    def _(i):
        pltpu.make_async_copy(column(ens_any, i), column(ens, i), load_sem.at[i]).start()

    get.wait()
    for slot in range(9):
        transforms[slot * K : (slot + 1) * K] = unpack_transform(nearby[slot])
    matrices[...] = full_matrices(transforms[...])

    def load(i):
        pltpu.make_async_copy(column(ens_any, i), column(ens, i), load_sem.at[i]).wait()

    def store(i):
        pltpu.make_async_copy(column(applied, i), column(out_any, i), store_sem.at[i]).start()

    apply_columns(0, CX, matrices, stationary, ens, applied, load, store)

    @pl.loop(0, CX)
    def _(i):
        pltpu.make_async_copy(column(applied, i), column(out_any, i), store_sem.at[i]).wait()


def shards(ensemble, obs_cell, obs_value, obs_weight, obs_count):
    flat = ensemble.reshape(ROWS, K)
    anywhere = pl.BlockSpec(memory_space=pl.ANY)
    dma = pltpu.SemaphoreType.DMA
    following, blend = pl.pallas_call(
        first_kernel,
        out_shape=(
            jax.ShapeDtypeStruct((ROWS, K), BF16),
            jax.ShapeDtypeStruct((9, PACKED, K), BF16),
        ),
        in_specs=[anywhere] * 5,
        out_specs=(anywhere, anywhere),
        scratch_shapes=[
            pltpu.SMEM((BX, BY), jnp.int32),
            pltpu.SMEM((1, OBS), jnp.int32),
            pltpu.VMEM((2, 1, OBS), F32),
            pltpu.VMEM((1, OBS), jnp.int32),
            pltpu.VMEM((ROWS, K), BF16),
            pltpu.VMEM((ROWS, K), BF16),
            pltpu.VMEM((ROWS, K), F32),
            pltpu.VMEM((OBS, K), F32),
            pltpu.VMEM((16, OBS), F32),
            pltpu.VMEM((K, OBS), BF16),
            pltpu.VMEM((9 * K, K), F32),
            pltpu.VMEM((2, 3 * K, 2 * K), BF16),
            pltpu.VMEM((ITERS, PACK, K), F32),
            pltpu.VMEM((ITERS, PACK, K), F32),
            pltpu.VMEM((ITERS, 4, PACK, K), F32),
            pltpu.VMEM((ITERS, 4, PACK, K), F32),
            pltpu.VMEM((9, PACKED, K), BF16),
            pltpu.VMEM((9 * K, K), BF16),
            pltpu.VMEM((ITERS, PACKED, K), BF16),
            dma((5,)),
            dma((CX,)),
            dma((CX,)),
            dma(()),
            dma((ITERS, 4)),
            dma((ITERS, 4)),
            dma((ITERS, 4)),
            dma((ITERS, 4)),
            dma((ITERS, 8)),
            dma((ITERS, 9)),
        ],
        compiler_params=pltpu.CompilerParams(
            collective_id=0, has_side_effects=True, vmem_limit_bytes=58 * 1024 * 1024
        ),
        name="analyse",
    )(
        obs_count,
        obs_cell.reshape(1, OBS),
        obs_value.reshape(1, OBS),
        obs_weight.reshape(1, OBS),
        flat,
    )
    out = pl.pallas_call(
        last_kernel,
        out_shape=jax.ShapeDtypeStruct((ROWS, K), BF16),
        in_specs=[anywhere] * 2,
        out_specs=anywhere,
        scratch_shapes=[
            pltpu.VMEM((9, PACKED, K), BF16),
            pltpu.VMEM((ROWS, K), BF16),
            pltpu.VMEM((ROWS, K), BF16),
            pltpu.VMEM((9 * K, K), BF16),
            pltpu.VMEM((9 * K, K), F32),
            pltpu.VMEM((2, 3 * K, 2 * K), BF16),
            dma(()),
            dma((CX,)),
            dma((CX,)),
        ],
        compiler_params=pltpu.CompilerParams(vmem_limit_bytes=58 * 1024 * 1024),
        name="blend",
    )(blend, following)
    return out.reshape(ensemble.shape)


def solution(mesh):
    placed = (
        P("gx", "gy", None, None),
        P("gx", "gy", None),
        P("gx", "gy", None),
        P("gx", "gy", None),
        P(),
    )
    return jax.shard_map(
        shards, mesh=mesh, in_specs=placed, out_specs=P("gx", "gy", None, None), check_vma=False
    )
```

```python
import jax
import jax.numpy as jnp
from jax import lax
from jax.experimental import pallas as pl
from jax.experimental.pallas import tpu as pltpu
from jax.sharding import PartitionSpec as P

K = 128
CX = 16
CY = 32
LEV = 48
ROWS = CX * CY * LEV
XROWS = CY * LEV
OBS = 2048
NEWTON = 6
ITERS = 2
QUART = 512
GROUP = 8
UNROLL = 4
GATHER = 64
PACKED = 80
BX = 8
BY = 16

MESH = pl.DeviceIdType.MESH
F32 = jnp.float32
BF16 = jnp.bfloat16
STAT_STEPS = (-1, 1, -2, 2)
STAT_WEIGHTS = (0.75, 0.75, 0.5, 0.5)
BLEND_STEPS = tuple((a, b) for a in (-1, 1, 0) for b in (-1, 1, 0) if (a, b) != (0, 0))


def slot_of(a, b):
    return (a + 1) * 3 + (b + 1)


def mm(a, b):
    return jnp.dot(a, b, preferred_element_type=F32)


def mm_nt(a, b):
    return lax.dot_general(a, b, (((1,), (1,)), ((), ())), preferred_element_type=F32)


def split(x):
    high = x.astype(BF16)
    low = (x - high.astype(F32)).astype(BF16)
    return high, low


def wide(x):
    high, low = split(x)
    return jnp.concatenate([high, low], axis=1)


def times(a, b):
    both = wide(b)
    out = mm(wide(a), jnp.concatenate([both, both], axis=0))
    return out[:, :K] + out[:, K:]


def iotas(shape):
    return lax.broadcasted_iota(jnp.int32, shape, 0), lax.broadcasted_iota(jnp.int32, shape, 1)


def centring():
    row, col = iotas((K, K))
    return jnp.where(row == col, (K - 1.0) / K, -1.0 / K).astype(BF16)


def fold(matrix):
    half = K // 2
    row, lane = iotas((half, K))
    return jnp.where(lane < row, pltpu.roll(matrix[half:], half, 1), matrix[:half])


def unfold(body, diagonal):
    half = K // 2
    row, lane = iotas((half, K))
    flipped = jnp.concatenate([body, jnp.zeros((half, K), F32)], axis=0).T
    top = jnp.where(lane < row, flipped[:half], body)
    lower = jnp.where(lane < row, body, flipped[:half])
    bottom = jnp.where(lane < half, flipped[half:], pltpu.roll(lower, half, 1))
    row, col = iotas((K, K))
    return jnp.where(row == col, diagonal, jnp.concatenate([top, bottom], axis=0))


def diagonal_of(matrix):
    row, col = iotas((K, K))
    return jnp.sum(jnp.where(row == col, matrix, 0.0), axis=0, keepdims=True)


def opened(symmetric, line):
    tail_row, _ = iotas((PACKED - K // 2, K))
    tail = jnp.where(tail_row == 0, diagonal_of(symmetric), jnp.where(tail_row == 2, line, 0.0))
    return jnp.concatenate([fold(symmetric), tail], axis=0)


def lines_of(packed):
    half = K // 2
    diagonal = packed[half : half + 1] + packed[half + 1 : half + 2]
    return diagonal, packed[half + 2 : half + 3] + packed[half + 3 : half + 4]


def closed(packed):
    tail_row, _ = iotas((PACKED - K // 2, K))
    tail = jnp.zeros((PACKED - K // 2, K), F32)
    for k, line in enumerate(lines_of(packed)):
        high, low = split(line)
        tail = jnp.where(tail_row == 2 * k, high.astype(F32), tail)
        tail = jnp.where(tail_row == 2 * k + 1, low.astype(F32), tail)
    return jnp.concatenate([packed[: K // 2], tail], axis=0).astype(BF16)


def unpack(packed):
    diagonal, line = lines_of(packed)
    return unfold(packed[: K // 2], diagonal), line


def unpack_transform(packed):
    spread, weights = unpack(packed.astype(F32))
    return (weights + spread).astype(BF16)


def transform_parts(packed):
    gram, projected = unpack(packed)
    row, col = iotas((K, K))
    identity = jnp.where(row == col, 1.0, 0.0).astype(F32)
    system = gram + (K - 1) * identity
    squares = jnp.sum(system * system, axis=0, keepdims=True)
    frobenius = jnp.sqrt(jnp.sum(squares, axis=1, keepdims=True))
    root = system / frobenius
    correction = 1.5 * identity - 0.5 * root
    root, inverse = times(correction, root), correction
    for step in range(1, NEWTON - 1):
        correction = 1.5 * identity - 0.5 * times(inverse, root)
        root, inverse = times(correction, root), times(correction, inverse)
    correction = 1.5 * identity - 0.5 * times(inverse, root)
    carried = times(jnp.broadcast_to(projected, (16, K)), inverse)
    carried, inverse = times(carried, correction), times(correction, inverse)
    weights = times(carried, inverse)[0:1] / frobenius
    return jnp.sqrt((K - 1) / frobenius) * inverse, weights


def hats(position):
    below = jnp.maximum(0.0, 0.5 - position)
    above = jnp.maximum(0.0, position - 0.5)
    return below, 1.0 - below - above, above


def hat_of(j, count):
    position = (j + 0.5) / count
    below, above = max(0.0, 0.5 - position), max(0.0, position - 0.5)
    return below, 1.0 - below - above, above


def blend_column(i, slot, matrices, stationary):
    weights = hats((i.astype(F32) + 0.5) / CX)
    for b in range(3):
        blend = weights[0] * matrices[b * K : (b + 1) * K]
        for a in (1, 2):
            at = (a * 3 + b) * K
            blend = blend + weights[a] * matrices[at : at + K]
        stationary[slot, b * K : (b + 1) * K] = wide(blend)


def apply_column(i, slot, ens, fresh, stationary):
    for half in range(2):
        matrix = stationary[slot, half * K : half * K + 2 * K]
        for group in range(CY // 2 // GROUP):
            first = half * (CY // 2) + group * GROUP
            here = pl.ds(pl.multiple_of(i * XROWS + first * LEV, 16), GROUP * LEV)
            block = ens[here]
            out = mm_nt(jnp.concatenate([block, block], axis=1), matrix)
            parts = []
            for j in range(GROUP):
                hat = hat_of(first + j, CY)
                piece = out[j * LEV : (j + 1) * LEV]
                parts.append(hat[half] * piece[:, :K] + hat[half + 1] * piece[:, K:])
            fresh[here] = jnp.concatenate(parts, axis=0).astype(BF16)


def apply_columns(first, last, matrices, stationary, ens, fresh, before, after):
    blend_column(jnp.int32(first), 0, matrices, stationary)

    @pl.loop(first // UNROLL, last // UNROLL)
    def _(step):
        for k in range(UNROLL):
            before(step * UNROLL + k)
        for k in range(UNROLL):
            i = step * UNROLL + k
            apply_column(i, k % 2, ens, fresh, stationary)
            after(i)
            blend_column(jnp.minimum(i + 1, CX - 1), 1 - k % 2, matrices, stationary)


def full_matrices(transforms):
    return mm(transforms, centring()) + 1.0 / K


def column(ref, i):
    return ref.at[pl.ds(pl.multiple_of(i * XROWS, XROWS), XROWS)]


def first_kernel(
    count_any, cell_any, value_any, weight_any, ens_any,
    next_ref, blend_ref,
    count_ref, cell_ref, given, cells_ref, ens, applied, ens32, picked, rows, deviations, matrices, stationary,
    stat_x, stat_y, got_x, got_y, nearby, transforms, own_ref,
    small_sem, load_sem, store_sem, own_sem, send_x, recv_x, send_y, recv_y, send_t, recv_t,
):
    gx, gy = lax.axis_index("gx"), lax.axis_index("gy")
    nx, ny = lax.axis_size("gx"), lax.axis_size("gy")

    def at(a, b):
        return (lax.rem(gx + a + nx, nx), lax.rem(gy + b + ny, ny))

    small = [
        pltpu.make_async_copy(count_any, count_ref, small_sem.at[0]),
        pltpu.make_async_copy(cell_any, cell_ref, small_sem.at[1]),
        pltpu.make_async_copy(cell_any, cells_ref, small_sem.at[2]),
        pltpu.make_async_copy(value_any, given.at[0], small_sem.at[3]),
        pltpu.make_async_copy(weight_any, given.at[1], small_sem.at[4]),
    ]
    for copy in small:
        copy.start()

    @pl.loop(0, CX)
    def _(i):
        pltpu.make_async_copy(column(ens_any, i), column(ens, i), load_sem.at[i]).start()

    partners = [(s, 0) for s in STAT_STEPS] + [(0, s) for s in STAT_STEPS]
    partners += [(a, b) for a in (-1, 1) for b in (-1, 1)]
    barrier = pltpu.get_barrier_semaphore()
    for a, b in partners:
        pl.semaphore_signal(barrier, inc=1, device_id=at(a, b), device_id_type=MESH)

    for copy in small:
        copy.wait()
    count = count_ref[gx, gy]
    cells = cells_ref[...].astype(F32)
    slot = lax.broadcasted_iota(jnp.int32, (1, OBS), 1)
    rows[0:1] = jnp.where(slot < count, given[1], 0.0)
    rows[1:2] = given[0]
    east = jnp.floor((cells + 0.5) * (1.0 / XROWS))
    north = jnp.floor((cells - XROWS * east + 0.5) * (1.0 / LEV))
    for first, hat in ((2, hats((east + 0.5) / CX)), (5, hats((north + 0.5) / CY))):
        for k in range(3):
            rows[first + k : first + k + 1] = hat[k]

    @pl.loop(0, CX)
    def _(i):
        pltpu.make_async_copy(column(ens_any, i), column(ens, i), load_sem.at[i]).wait()
        start = pl.multiple_of(i * XROWS, XROWS)
        ens32[pl.ds(start, XROWS)] = ens[pl.ds(start, XROWS)].astype(F32)

    @pl.loop(0, OBS // GATHER)
    def _(g):
        for r in range(GATHER):
            o = g * GATHER + r
            picked[pl.ds(o, 1)] = ens32[pl.ds(cell_ref[0, o], 1)]

    def accumulate(total, lanes, deviation, centre):
        scale, value = rows[0:1, lanes], rows[1:2, lanes]
        anomaly = (scale * deviation).astype(BF16)
        innovation = jnp.broadcast_to(scale * (value - centre), (16, QUART)).astype(BF16)
        return total + mm_nt(jnp.concatenate([anomaly, innovation], axis=0), anomaly)

    def exchange(t, sent, got, send_sem, recv_sem, shift):
        copies = []
        for k, step in enumerate(STAT_STEPS):
            there = STAT_STEPS.index(-step)
            copies.append(
                pltpu.make_async_remote_copy(
                    src_ref=sent.at[t],
                    dst_ref=got.at[t, there],
                    send_sem=send_sem.at[t, k],
                    recv_sem=recv_sem.at[t, there],
                    device_id=at(*shift(step)),
                    device_id_type=MESH,
                )
            )
        return copies

    pending = []

    def settle():
        while pending:
            pending.pop().wait_send()

    def weighted(t, total, got, copies):
        for k in reversed(range(4)):
            copies[STAT_STEPS.index(-STAT_STEPS[k])].wait_recv()
            total = total + STAT_WEIGHTS[k] * got[t, k].astype(F32)
        pending.extend(copies)
        return total

    def nothing(i):
        pass

    def store(i):
        pltpu.make_async_copy(column(applied, i), column(next_ref, i), store_sem.at[i]).start()

    def apply_some(first, last):
        apply_columns(first, last, matrices, stationary, ens, applied, nothing, store)

    for t in range(ITERS):
        total = jnp.zeros((K + 16, K), F32)
        if t == 0:
            row, col = iotas((K + 16, K))
            centre_rows = jnp.where(row == col, (K - 1.0) / K, jnp.where(row < K, -1.0 / K, 1.0 / K))
            centre_rows = centre_rows.astype(BF16)
            for q in range(OBS // QUART):
                lanes = slice(q * QUART, (q + 1) * QUART)
                moved = mm_nt(centre_rows, picked[lanes].astype(BF16))
                total = accumulate(total, lanes, moved[:K], moved[K : K + 1])
                deviations[:, lanes] = moved[:K].astype(BF16)
                rows[8:9, lanes] = moved[K : K + 1]
        else:
            for q in range(OBS // QUART):
                lanes = slice(q * QUART, (q + 1) * QUART)
                out = mm(transforms[...], deviations[:, lanes])
                fresh = rows[8:9, lanes]
                for a in range(3):
                    at_a = a * 3 * K
                    part = rows[5:6, lanes] * out[at_a : at_a + K]
                    part = part + rows[6:7, lanes] * out[at_a + K : at_a + 2 * K]
                    part = part + rows[7:8, lanes] * out[at_a + 2 * K : at_a + 3 * K]
                    fresh = fresh + rows[2 + a : 3 + a, lanes] * part
                fresh = fresh.astype(BF16).astype(F32)
                centre = jnp.sum(fresh, axis=0, keepdims=True) * (1.0 / K)
                total = accumulate(total, lanes, fresh - centre, centre)
        own = opened(total[:K], total[K : K + 1])
        stat_x[t] = closed(own)

        if t == 0:
            pl.semaphore_wait(barrier, len(partners))
        copies = exchange(t, stat_x, got_x, send_x, recv_x, lambda step: (step, 0))
        for copy in copies:
            copy.start()
        if t == 1:
            matrices[...] = full_matrices(transforms[...])
            apply_some(0, CX // 2)
            settle()
        own = weighted(t, own, got_x, copies)
        stat_y[t] = closed(own)
        copies = exchange(t, stat_y, got_y, send_y, recv_y, lambda step: (0, step))
        for copy in copies:
            copy.start()
        if t == 1:
            apply_some(CX // 2, CX)
        spread, weights = transform_parts(weighted(t, own, got_y, copies))
        own_ref[t] = closed(opened(spread, weights))
        landing = nearby if t == 0 else blend_ref
        copies = {}
        for k, (a, b) in enumerate(BLEND_STEPS):
            there = slot_of(-a, -b)
            copies[(-a, -b)] = pltpu.make_async_remote_copy(
                src_ref=own_ref.at[t],
                dst_ref=landing.at[there],
                send_sem=send_t.at[t, k],
                recv_sem=recv_t.at[t, there],
                device_id=at(a, b),
                device_id_type=MESH,
            )
        for copy in copies.values():
            copy.start()
        own = slot_of(0, 0)
        if t == 0:
            transforms[own * K : (own + 1) * K] = (weights + spread).astype(BF16)
        else:
            mine = pltpu.make_async_copy(own_ref.at[t], landing.at[own], own_sem)
            mine.start()
            settle()
        for step in reversed(BLEND_STEPS):
            copies[step].wait_recv()
            if t == 0:
                slot = slot_of(*step)
                transforms[slot * K : (slot + 1) * K] = unpack_transform(nearby[slot])
        if t == 1:
            mine.wait()
        pending.extend(copies.values())
    settle()

    @pl.loop(0, CX)
    def _(i):
        pltpu.make_async_copy(column(applied, i), column(next_ref, i), store_sem.at[i]).wait()


def last_kernel(blend_any, ens_any, out_any, nearby, ens, applied, transforms, matrices, stationary, blend_sem, load_sem, store_sem):
    get = pltpu.make_async_copy(blend_any, nearby, blend_sem)
    get.start()

    @pl.loop(0, CX)
    def _(i):
        pltpu.make_async_copy(column(ens_any, i), column(ens, i), load_sem.at[i]).start()

    get.wait()
    for slot in range(9):
        transforms[slot * K : (slot + 1) * K] = unpack_transform(nearby[slot])
    matrices[...] = full_matrices(transforms[...])

    def load(i):
        pltpu.make_async_copy(column(ens_any, i), column(ens, i), load_sem.at[i]).wait()

    def store(i):
        pltpu.make_async_copy(column(applied, i), column(out_any, i), store_sem.at[i]).start()

    apply_columns(0, CX, matrices, stationary, ens, applied, load, store)

    @pl.loop(0, CX)
    def _(i):
        pltpu.make_async_copy(column(applied, i), column(out_any, i), store_sem.at[i]).wait()


def shards(ensemble, obs_cell, obs_value, obs_weight, obs_count):
    flat = ensemble.reshape(ROWS, K)
    anywhere = pl.BlockSpec(memory_space=pl.ANY)
    dma = pltpu.SemaphoreType.DMA
    following, blend = pl.pallas_call(
        first_kernel,
        out_shape=(
            jax.ShapeDtypeStruct((ROWS, K), BF16),
            jax.ShapeDtypeStruct((9, PACKED, K), BF16),
        ),
        in_specs=[anywhere] * 5,
        out_specs=(anywhere, anywhere),
        scratch_shapes=[
            pltpu.SMEM((BX, BY), jnp.int32),
            pltpu.SMEM((1, OBS), jnp.int32),
            pltpu.VMEM((2, 1, OBS), F32),
            pltpu.VMEM((1, OBS), jnp.int32),
            pltpu.VMEM((ROWS, K), BF16),
            pltpu.VMEM((ROWS, K), BF16),
            pltpu.VMEM((ROWS, K), F32),
            pltpu.VMEM((OBS, K), F32),
            pltpu.VMEM((16, OBS), F32),
            pltpu.VMEM((K, OBS), BF16),
            pltpu.VMEM((9 * K, K), F32),
            pltpu.VMEM((2, 3 * K, 2 * K), BF16),
            pltpu.VMEM((ITERS, PACKED, K), BF16),
            pltpu.VMEM((ITERS, PACKED, K), BF16),
            pltpu.VMEM((ITERS, 4, PACKED, K), BF16),
            pltpu.VMEM((ITERS, 4, PACKED, K), BF16),
            pltpu.VMEM((9, PACKED, K), BF16),
            pltpu.VMEM((9 * K, K), BF16),
            pltpu.VMEM((ITERS, PACKED, K), BF16),
            dma((5,)),
            dma((CX,)),
            dma((CX,)),
            dma(()),
            dma((ITERS, 4)),
            dma((ITERS, 4)),
            dma((ITERS, 4)),
            dma((ITERS, 4)),
            dma((ITERS, 8)),
            dma((ITERS, 9)),
        ],
        compiler_params=pltpu.CompilerParams(
            collective_id=0, has_side_effects=True, vmem_limit_bytes=58 * 1024 * 1024
        ),
        name="analyse",
    )(
        obs_count,
        obs_cell.reshape(1, OBS),
        obs_value.reshape(1, OBS),
        obs_weight.reshape(1, OBS),
        flat,
    )
    out = pl.pallas_call(
        last_kernel,
        out_shape=jax.ShapeDtypeStruct((ROWS, K), BF16),
        in_specs=[anywhere] * 2,
        out_specs=anywhere,
        scratch_shapes=[
            pltpu.VMEM((9, PACKED, K), BF16),
            pltpu.VMEM((ROWS, K), BF16),
            pltpu.VMEM((ROWS, K), BF16),
            pltpu.VMEM((9 * K, K), BF16),
            pltpu.VMEM((9 * K, K), F32),
            pltpu.VMEM((2, 3 * K, 2 * K), BF16),
            dma(()),
            dma((CX,)),
            dma((CX,)),
        ],
        compiler_params=pltpu.CompilerParams(vmem_limit_bytes=58 * 1024 * 1024),
        name="blend",
    )(blend, following)
    return out.reshape(ensemble.shape)


def solution(mesh):
    placed = (
        P("gx", "gy", None, None),
        P("gx", "gy", None),
        P("gx", "gy", None),
        P("gx", "gy", None),
        P(),
    )
    return jax.shard_map(
        shards, mesh=mesh, in_specs=placed, out_specs=P("gx", "gy", None, None), check_vma=False
    )
```

```python
import jax
import jax.numpy as jnp
from jax import lax
from jax.experimental import pallas as pl
from jax.experimental.pallas import tpu as pltpu
from jax.sharding import PartitionSpec as P

K = 128
CX = 16
CY = 32
LEV = 48
ROWS = CX * CY * LEV
XROWS = CY * LEV
OBS = 2048
NEWTON = 6
ITERS = 2
QUART = 512
GROUP = 8
UNROLL = 4
GATHER = 64
PACKED = 80
BX = 8
BY = 16

MESH = pl.DeviceIdType.MESH
F32 = jnp.float32
BF16 = jnp.bfloat16
STAT_STEPS = (-1, 1, -2, 2)
STAT_WEIGHTS = (0.75, 0.75, 0.5, 0.5)
BLEND_STEPS = tuple((a, b) for a in (-1, 1, 0) for b in (-1, 1, 0) if (a, b) != (0, 0))


def slot_of(a, b):
    return (a + 1) * 3 + (b + 1)


def mm(a, b):
    return jnp.dot(a, b, preferred_element_type=F32)


def mm_nt(a, b):
    return lax.dot_general(a, b, (((1,), (1,)), ((), ())), preferred_element_type=F32)


def split(x):
    high = x.astype(BF16)
    low = (x - high.astype(F32)).astype(BF16)
    return high, low


def wide(x):
    high, low = split(x)
    return jnp.concatenate([high, low], axis=1)


def times(a, b):
    both = wide(b)
    out = mm(wide(a), jnp.concatenate([both, both], axis=0))
    return out[:, :K] + out[:, K:]


def iotas(shape):
    return lax.broadcasted_iota(jnp.int32, shape, 0), lax.broadcasted_iota(jnp.int32, shape, 1)


def centring():
    row, col = iotas((K, K))
    return jnp.where(row == col, (K - 1.0) / K, -1.0 / K).astype(BF16)


def fold(matrix):
    half = K // 2
    row, lane = iotas((half, K))
    return jnp.where(lane < row, pltpu.roll(matrix[half:], half, 1), matrix[:half])


def unfold(body, diagonal):
    half = K // 2
    row, lane = iotas((half, K))
    flipped = jnp.concatenate([body, jnp.zeros((half, K), F32)], axis=0).T
    top = jnp.where(lane < row, flipped[:half], body)
    lower = jnp.where(lane < row, body, flipped[:half])
    bottom = jnp.where(lane < half, flipped[half:], pltpu.roll(lower, half, 1))
    row, col = iotas((K, K))
    return jnp.where(row == col, diagonal, jnp.concatenate([top, bottom], axis=0))


def diagonal_of(matrix):
    row, col = iotas((K, K))
    return jnp.sum(jnp.where(row == col, matrix, 0.0), axis=0, keepdims=True)


def opened(symmetric, line):
    tail_row, _ = iotas((PACKED - K // 2, K))
    tail = jnp.where(tail_row == 0, diagonal_of(symmetric), jnp.where(tail_row == 2, line, 0.0))
    return jnp.concatenate([fold(symmetric), tail], axis=0)


def lines_of(packed):
    half = K // 2
    diagonal = packed[half : half + 1] + packed[half + 1 : half + 2]
    return diagonal, packed[half + 2 : half + 3] + packed[half + 3 : half + 4]


def closed(packed):
    tail_row, _ = iotas((PACKED - K // 2, K))
    tail = jnp.zeros((PACKED - K // 2, K), F32)
    for k, line in enumerate(lines_of(packed)):
        high, low = split(line)
        tail = jnp.where(tail_row == 2 * k, high.astype(F32), tail)
        tail = jnp.where(tail_row == 2 * k + 1, low.astype(F32), tail)
    return jnp.concatenate([packed[: K // 2], tail], axis=0).astype(BF16)


def unpack(packed):
    diagonal, line = lines_of(packed)
    return unfold(packed[: K // 2], diagonal), line


def unpack_transform(packed):
    spread, weights = unpack(packed.astype(F32))
    return (weights + spread).astype(BF16)


def transform_parts(packed):
    gram, projected = unpack(packed)
    row, col = iotas((K, K))
    identity = jnp.where(row == col, 1.0, 0.0).astype(F32)
    system = gram + (K - 1) * identity
    squares = jnp.sum(system * system, axis=0, keepdims=True)
    frobenius = jnp.sqrt(jnp.sum(squares, axis=1, keepdims=True))
    root = system / frobenius
    correction = 1.5 * identity - 0.5 * root
    root, inverse = times(correction, root), correction
    for step in range(1, NEWTON - 1):
        correction = 1.5 * identity - 0.5 * times(inverse, root)
        root, inverse = times(correction, root), times(correction, inverse)
    correction = 1.5 * identity - 0.5 * times(inverse, root)
    carried = times(jnp.broadcast_to(projected, (16, K)), inverse)
    carried, inverse = times(carried, correction), times(correction, inverse)
    weights = times(carried, inverse)[0:1] / frobenius
    return jnp.sqrt((K - 1) / frobenius) * inverse, weights


def hats(position):
    below = jnp.maximum(0.0, 0.5 - position)
    above = jnp.maximum(0.0, position - 0.5)
    return below, 1.0 - below - above, above


def hat_of(j, count):
    position = (j + 0.5) / count
    below, above = max(0.0, 0.5 - position), max(0.0, position - 0.5)
    return below, 1.0 - below - above, above


def blend_column(i, slot, matrices, stationary):
    weights = hats((i.astype(F32) + 0.5) / CX)
    for b in range(3):
        blend = weights[0] * matrices[b * K : (b + 1) * K]
        for a in (1, 2):
            at = (a * 3 + b) * K
            blend = blend + weights[a] * matrices[at : at + K]
        stationary[slot, b * K : (b + 1) * K] = wide(blend)


def apply_column(i, slot, ens, fresh, stationary):
    for half in range(2):
        matrix = stationary[slot, half * K : half * K + 2 * K]
        for group in range(CY // 2 // GROUP):
            first = half * (CY // 2) + group * GROUP
            here = pl.ds(pl.multiple_of(i * XROWS + first * LEV, 16), GROUP * LEV)
            block = ens[here]
            out = mm_nt(jnp.concatenate([block, block], axis=1), matrix)
            parts = []
            for j in range(GROUP):
                hat = hat_of(first + j, CY)
                piece = out[j * LEV : (j + 1) * LEV]
                parts.append(hat[half] * piece[:, :K] + hat[half + 1] * piece[:, K:])
            fresh[here] = jnp.concatenate(parts, axis=0).astype(BF16)


def apply_columns(first, last, matrices, stationary, ens, fresh, before, after):
    blend_column(jnp.int32(first), 0, matrices, stationary)

    @pl.loop(first // UNROLL, last // UNROLL)
    def _(step):
        for k in range(UNROLL):
            before(step * UNROLL + k)
        for k in range(UNROLL):
            i = step * UNROLL + k
            apply_column(i, k % 2, ens, fresh, stationary)
            after(i)
            blend_column(jnp.minimum(i + 1, CX - 1), 1 - k % 2, matrices, stationary)


def full_matrices(transforms):
    return mm(transforms, centring()) + 1.0 / K


def column(ref, i):
    return ref.at[pl.ds(pl.multiple_of(i * XROWS, XROWS), XROWS)]


def first_kernel(
    count_any, cell_any, value_any, weight_any, ens_any,
    applied, blend_ref,
    count_ref, cell_ref, given, cells_ref, ens, ens32, picked, rows, deviations, matrices, stationary,
    stat_x, stat_y, got_x, got_y, nearby, transforms, own_ref,
    small_sem, load_sem, own_sem, send_x, recv_x, send_y, recv_y, send_t, recv_t,
):
    gx, gy = lax.axis_index("gx"), lax.axis_index("gy")
    nx, ny = lax.axis_size("gx"), lax.axis_size("gy")

    def at(a, b):
        return (lax.rem(gx + a + nx, nx), lax.rem(gy + b + ny, ny))

    small = [
        pltpu.make_async_copy(count_any, count_ref, small_sem.at[0]),
        pltpu.make_async_copy(cell_any, cell_ref, small_sem.at[1]),
        pltpu.make_async_copy(cell_any, cells_ref, small_sem.at[2]),
        pltpu.make_async_copy(value_any, given.at[0], small_sem.at[3]),
        pltpu.make_async_copy(weight_any, given.at[1], small_sem.at[4]),
    ]
    for copy in small:
        copy.start()

    @pl.loop(0, CX)
    def _(i):
        pltpu.make_async_copy(column(ens_any, i), column(ens, i), load_sem.at[i]).start()

    partners = [(s, 0) for s in STAT_STEPS] + [(0, s) for s in STAT_STEPS]
    partners += [(a, b) for a in (-1, 1) for b in (-1, 1)]
    barrier = pltpu.get_barrier_semaphore()
    for a, b in partners:
        pl.semaphore_signal(barrier, inc=1, device_id=at(a, b), device_id_type=MESH)

    for copy in small:
        copy.wait()
    count = count_ref[gx, gy]
    cells = cells_ref[...].astype(F32)
    slot = lax.broadcasted_iota(jnp.int32, (1, OBS), 1)
    rows[0:1] = jnp.where(slot < count, given[1], 0.0)
    rows[1:2] = given[0]
    east = jnp.floor((cells + 0.5) * (1.0 / XROWS))
    north = jnp.floor((cells - XROWS * east + 0.5) * (1.0 / LEV))
    for first, hat in ((2, hats((east + 0.5) / CX)), (5, hats((north + 0.5) / CY))):
        for k in range(3):
            rows[first + k : first + k + 1] = hat[k]

    @pl.loop(0, CX)
    def _(i):
        pltpu.make_async_copy(column(ens_any, i), column(ens, i), load_sem.at[i]).wait()
        start = pl.multiple_of(i * XROWS, XROWS)
        ens32[pl.ds(start, XROWS)] = ens[pl.ds(start, XROWS)].astype(F32)

    @pl.loop(0, OBS // GATHER)
    def _(g):
        for r in range(GATHER):
            o = g * GATHER + r
            picked[pl.ds(o, 1)] = ens32[pl.ds(cell_ref[0, o], 1)]

    def accumulate(total, lanes, deviation, centre):
        scale, value = rows[0:1, lanes], rows[1:2, lanes]
        anomaly = (scale * deviation).astype(BF16)
        innovation = jnp.broadcast_to(scale * (value - centre), (16, QUART)).astype(BF16)
        return total + mm_nt(jnp.concatenate([anomaly, innovation], axis=0), anomaly)

    def exchange(t, sent, got, send_sem, recv_sem, shift):
        copies = []
        for k, step in enumerate(STAT_STEPS):
            there = STAT_STEPS.index(-step)
            copies.append(
                pltpu.make_async_remote_copy(
                    src_ref=sent.at[t],
                    dst_ref=got.at[t, there],
                    send_sem=send_sem.at[t, k],
                    recv_sem=recv_sem.at[t, there],
                    device_id=at(*shift(step)),
                    device_id_type=MESH,
                )
            )
        return copies

    pending = []

    def settle():
        while pending:
            pending.pop().wait_send()

    def weighted(t, total, got, copies):
        for k in reversed(range(4)):
            copies[STAT_STEPS.index(-STAT_STEPS[k])].wait_recv()
            total = total + STAT_WEIGHTS[k] * got[t, k].astype(F32)
        pending.extend(copies)
        return total

    def nothing(i):
        pass

    def apply_some(first, last):
        apply_columns(first, last, matrices, stationary, ens, applied, nothing, nothing)

    for t in range(ITERS):
        total = jnp.zeros((K + 16, K), F32)
        if t == 0:
            row, col = iotas((K + 16, K))
            centre_rows = jnp.where(row == col, (K - 1.0) / K, jnp.where(row < K, -1.0 / K, 1.0 / K))
            centre_rows = centre_rows.astype(BF16)
            for q in range(OBS // QUART):
                lanes = slice(q * QUART, (q + 1) * QUART)
                moved = mm_nt(centre_rows, picked[lanes].astype(BF16))
                total = accumulate(total, lanes, moved[:K], moved[K : K + 1])
                deviations[:, lanes] = moved[:K].astype(BF16)
                rows[8:9, lanes] = moved[K : K + 1]
        else:
            for q in range(OBS // QUART):
                lanes = slice(q * QUART, (q + 1) * QUART)
                out = mm(transforms[...], deviations[:, lanes])
                fresh = rows[8:9, lanes]
                for a in range(3):
                    at_a = a * 3 * K
                    part = rows[5:6, lanes] * out[at_a : at_a + K]
                    part = part + rows[6:7, lanes] * out[at_a + K : at_a + 2 * K]
                    part = part + rows[7:8, lanes] * out[at_a + 2 * K : at_a + 3 * K]
                    fresh = fresh + rows[2 + a : 3 + a, lanes] * part
                fresh = fresh.astype(BF16).astype(F32)
                centre = jnp.sum(fresh, axis=0, keepdims=True) * (1.0 / K)
                total = accumulate(total, lanes, fresh - centre, centre)
        own = opened(total[:K], total[K : K + 1])
        stat_x[t] = closed(own)

        if t == 0:
            pl.semaphore_wait(barrier, len(partners))
        copies = exchange(t, stat_x, got_x, send_x, recv_x, lambda step: (step, 0))
        for copy in copies:
            copy.start()
        if t == 1:
            matrices[...] = full_matrices(transforms[...])
            apply_some(0, CX // 2)
            settle()
        own = weighted(t, own, got_x, copies)
        stat_y[t] = closed(own)
        copies = exchange(t, stat_y, got_y, send_y, recv_y, lambda step: (0, step))
        for copy in copies:
            copy.start()
        if t == 1:
            apply_some(CX // 2, CX)
        spread, weights = transform_parts(weighted(t, own, got_y, copies))
        own_ref[t] = closed(opened(spread, weights))
        landing = nearby if t == 0 else blend_ref
        copies = {}
        for k, (a, b) in enumerate(BLEND_STEPS):
            there = slot_of(-a, -b)
            copies[(-a, -b)] = pltpu.make_async_remote_copy(
                src_ref=own_ref.at[t],
                dst_ref=landing.at[there],
                send_sem=send_t.at[t, k],
                recv_sem=recv_t.at[t, there],
                device_id=at(a, b),
                device_id_type=MESH,
            )
        for copy in copies.values():
            copy.start()
        own = slot_of(0, 0)
        if t == 0:
            transforms[own * K : (own + 1) * K] = (weights + spread).astype(BF16)
        else:
            mine = pltpu.make_async_copy(own_ref.at[t], landing.at[own], own_sem)
            mine.start()
            settle()
        for step in reversed(BLEND_STEPS):
            copies[step].wait_recv()
        if t == 0:
            for step in BLEND_STEPS:
                slot = slot_of(*step)
                transforms[slot * K : (slot + 1) * K] = unpack_transform(nearby[slot])
        else:
            mine.wait()
        pending.extend(copies.values())
    settle()


def last_kernel(nearby, ens, out_any, applied, transforms, matrices, stationary, store_sem):
    for slot in range(9):
        transforms[slot * K : (slot + 1) * K] = unpack_transform(nearby[slot])
    matrices[...] = full_matrices(transforms[...])

    def nothing(i):
        pass

    def store(i):
        pltpu.make_async_copy(column(applied, i), column(out_any, i), store_sem.at[i]).start()

    apply_columns(0, CX, matrices, stationary, ens, applied, nothing, store)

    @pl.loop(0, CX)
    def _(i):
        pltpu.make_async_copy(column(applied, i), column(out_any, i), store_sem.at[i]).wait()


def shards(ensemble, obs_cell, obs_value, obs_weight, obs_count):
    flat = ensemble.reshape(ROWS, K)
    anywhere = pl.BlockSpec(memory_space=pl.ANY)
    fixed = pl.BlockSpec(memory_space=pltpu.HBM)
    dma = pltpu.SemaphoreType.DMA
    following, blend = pl.pallas_call(
        first_kernel,
        out_shape=(
            jax.ShapeDtypeStruct((ROWS, K), BF16),
            jax.ShapeDtypeStruct((9, PACKED, K), BF16),
        ),
        in_specs=[fixed] * 5,
        out_specs=(pl.BlockSpec(memory_space=pltpu.VMEM), anywhere),
        scratch_shapes=[
            pltpu.SMEM((BX, BY), jnp.int32),
            pltpu.SMEM((1, OBS), jnp.int32),
            pltpu.VMEM((2, 1, OBS), F32),
            pltpu.VMEM((1, OBS), jnp.int32),
            pltpu.VMEM((ROWS, K), BF16),
            pltpu.VMEM((ROWS, K), F32),
            pltpu.VMEM((OBS, K), F32),
            pltpu.VMEM((16, OBS), F32),
            pltpu.VMEM((K, OBS), BF16),
            pltpu.VMEM((9 * K, K), F32),
            pltpu.VMEM((2, 3 * K, 2 * K), BF16),
            pltpu.VMEM((ITERS, PACKED, K), BF16),
            pltpu.VMEM((ITERS, PACKED, K), BF16),
            pltpu.VMEM((ITERS, 4, PACKED, K), BF16),
            pltpu.VMEM((ITERS, 4, PACKED, K), BF16),
            pltpu.VMEM((9, PACKED, K), BF16),
            pltpu.VMEM((9 * K, K), BF16),
            pltpu.VMEM((ITERS, PACKED, K), BF16),
            dma((5,)),
            dma((CX,)),
            dma(()),
            dma((ITERS, 4)),
            dma((ITERS, 4)),
            dma((ITERS, 4)),
            dma((ITERS, 4)),
            dma((ITERS, 8)),
            dma((ITERS, 9)),
        ],
        compiler_params=pltpu.CompilerParams(
            collective_id=0, has_side_effects=True, vmem_limit_bytes=44 * 1024 * 1024
        ),
        name="analyse",
    )(
        *(
            pltpu.with_memory_space_constraint(array, pltpu.HBM)
            for array in (
                obs_count,
                obs_cell.reshape(1, OBS),
                obs_value.reshape(1, OBS),
                obs_weight.reshape(1, OBS),
                flat,
            )
        )
    )
    out = pl.pallas_call(
        last_kernel,
        out_shape=jax.ShapeDtypeStruct((ROWS, K), BF16),
        in_specs=[pl.BlockSpec(memory_space=pltpu.VMEM)] * 2,
        out_specs=fixed,
        scratch_shapes=[
            pltpu.VMEM((ROWS, K), BF16),
            pltpu.VMEM((9 * K, K), BF16),
            pltpu.VMEM((9 * K, K), F32),
            pltpu.VMEM((2, 3 * K, 2 * K), BF16),
            dma((CX,)),
        ],
        compiler_params=pltpu.CompilerParams(vmem_limit_bytes=44 * 1024 * 1024),
        name="blend",
    )(blend, following)
    return out.reshape(ensemble.shape)


def solution(mesh):
    placed = (
        P("gx", "gy", None, None),
        P("gx", "gy", None),
        P("gx", "gy", None),
        P("gx", "gy", None),
        P(),
    )
    return jax.shard_map(
        shards, mesh=mesh, in_specs=placed, out_specs=P("gx", "gy", None, None), check_vma=False
    )
```

```python
import jax
import jax.numpy as jnp
from jax import lax
from jax.experimental import pallas as pl
from jax.experimental.pallas import tpu as pltpu
from jax.sharding import PartitionSpec as P

K = 128
CX = 16
CY = 32
LEV = 48
ROWS = CX * CY * LEV
XROWS = CY * LEV
OBS = 2048
NEWTON = 6
ITERS = 2
QUART = 512
PART = 256
GROUP = 8
UNROLL = 4
GATHER = 64
PACKED = 80
BX = 8
BY = 16

MESH = pl.DeviceIdType.MESH
F32 = jnp.float32
BF16 = jnp.bfloat16
STAT_STEPS = (-1, 1, -2, 2)
STAT_WEIGHTS = (0.75, 0.75, 0.5, 0.5)
BLEND_STEPS = tuple((a, b) for a in (-1, 1, 0) for b in (-1, 1, 0) if (a, b) != (0, 0))


def slot_of(a, b):
    return (a + 1) * 3 + (b + 1)


def mm(a, b):
    return jnp.dot(a, b, preferred_element_type=F32)


def mm_nt(a, b):
    return lax.dot_general(a, b, (((1,), (1,)), ((), ())), preferred_element_type=F32)


def split(x):
    high = x.astype(BF16)
    low = (x - high.astype(F32)).astype(BF16)
    return high, low


def wide(x):
    high, low = split(x)
    return jnp.concatenate([high, low], axis=1)


def times(a, b):
    both = wide(b)
    out = mm(wide(a), jnp.concatenate([both, both], axis=0))
    return out[:, :K] + out[:, K:]


def iotas(shape):
    return lax.broadcasted_iota(jnp.int32, shape, 0), lax.broadcasted_iota(jnp.int32, shape, 1)


def centring():
    row, col = iotas((K, K))
    return jnp.where(row == col, (K - 1.0) / K, -1.0 / K).astype(BF16)


def fold(matrix):
    half = K // 2
    row, lane = iotas((half, K))
    return jnp.where(lane < row, pltpu.roll(matrix[half:], half, 1), matrix[:half])


def unfold(body, diagonal):
    half = K // 2
    row, lane = iotas((half, K))
    flipped = jnp.concatenate([body, jnp.zeros((half, K), F32)], axis=0).T
    top = jnp.where(lane < row, flipped[:half], body)
    lower = jnp.where(lane < row, body, flipped[:half])
    bottom = jnp.where(lane < half, flipped[half:], pltpu.roll(lower, half, 1))
    row, col = iotas((K, K))
    return jnp.where(row == col, diagonal, jnp.concatenate([top, bottom], axis=0))


def diagonal_of(matrix):
    row, col = iotas((K, K))
    return jnp.sum(jnp.where(row == col, matrix, 0.0), axis=0, keepdims=True)


def opened(symmetric, line):
    tail_row, _ = iotas((PACKED - K // 2, K))
    tail = jnp.where(tail_row == 0, diagonal_of(symmetric), jnp.where(tail_row == 2, line, 0.0))
    return jnp.concatenate([fold(symmetric), tail], axis=0)


def lines_of(packed):
    half = K // 2
    diagonal = packed[half : half + 1] + packed[half + 1 : half + 2]
    return diagonal, packed[half + 2 : half + 3] + packed[half + 3 : half + 4]


def closed(packed):
    tail_row, _ = iotas((PACKED - K // 2, K))
    tail = jnp.zeros((PACKED - K // 2, K), F32)
    for k, line in enumerate(lines_of(packed)):
        high, low = split(line)
        tail = jnp.where(tail_row == 2 * k, high.astype(F32), tail)
        tail = jnp.where(tail_row == 2 * k + 1, low.astype(F32), tail)
    return jnp.concatenate([packed[: K // 2], tail], axis=0).astype(BF16)


def unpack(packed):
    diagonal, line = lines_of(packed)
    return unfold(packed[: K // 2], diagonal), line


def unpack_transform(packed):
    spread, weights = unpack(packed.astype(F32))
    return (weights + spread).astype(BF16)


def transform_parts(packed):
    gram, projected = unpack(packed)
    row, col = iotas((K, K))
    identity = jnp.where(row == col, 1.0, 0.0).astype(F32)
    system = gram + (K - 1) * identity
    squares = jnp.sum(system * system, axis=0, keepdims=True)
    frobenius = jnp.sqrt(jnp.sum(squares, axis=1, keepdims=True))
    root = system / frobenius
    correction = 1.5 * identity - 0.5 * root
    root, inverse = times(correction, root), correction
    for step in range(1, NEWTON - 1):
        correction = 1.5 * identity - 0.5 * times(inverse, root)
        root, inverse = times(correction, root), times(correction, inverse)
    correction = 1.5 * identity - 0.5 * times(inverse, root)
    carried = times(jnp.broadcast_to(projected, (16, K)), inverse)
    carried, inverse = times(carried, correction), times(correction, inverse)
    weights = times(carried, inverse)[0:1] / frobenius
    return jnp.sqrt((K - 1) / frobenius) * inverse, weights


def hats(position):
    below = jnp.maximum(0.0, 0.5 - position)
    above = jnp.maximum(0.0, position - 0.5)
    return below, 1.0 - below - above, above


def hat_of(j, count):
    position = (j + 0.5) / count
    below, above = max(0.0, 0.5 - position), max(0.0, position - 0.5)
    return below, 1.0 - below - above, above


def blend_column(i, slot, matrices, stationary):
    weights = hats((i.astype(F32) + 0.5) / CX)
    for b in range(3):
        blend = weights[0] * matrices[b * K : (b + 1) * K]
        for a in (1, 2):
            at = (a * 3 + b) * K
            blend = blend + weights[a] * matrices[at : at + K]
        stationary[slot, b * K : (b + 1) * K] = wide(blend)


def apply_column(i, slot, ens, fresh, stationary):
    for half in range(2):
        matrix = stationary[slot, half * K : half * K + 2 * K]
        for group in range(CY // 2 // GROUP):
            first = half * (CY // 2) + group * GROUP
            here = pl.ds(pl.multiple_of(i * XROWS + first * LEV, 16), GROUP * LEV)
            block = ens[here]
            out = mm_nt(jnp.concatenate([block, block], axis=1), matrix)
            parts = []
            for j in range(GROUP):
                hat = hat_of(first + j, CY)
                piece = out[j * LEV : (j + 1) * LEV]
                parts.append(hat[half] * piece[:, :K] + hat[half + 1] * piece[:, K:])
            fresh[here] = jnp.concatenate(parts, axis=0).astype(BF16)


def apply_columns(first, last, matrices, stationary, ens, fresh, before, after):
    blend_column(jnp.int32(first), 0, matrices, stationary)

    @pl.loop(first // UNROLL, last // UNROLL)
    def _(step):
        for k in range(UNROLL):
            before(step * UNROLL + k)
        for k in range(UNROLL):
            i = step * UNROLL + k
            apply_column(i, k % 2, ens, fresh, stationary)
            after(i)
            blend_column(jnp.minimum(i + 1, CX - 1), 1 - k % 2, matrices, stationary)


def full_matrices(transforms):
    return mm(transforms, centring()) + 1.0 / K


def column(ref, i):
    return ref.at[pl.ds(pl.multiple_of(i * XROWS, XROWS), XROWS)]


def first_kernel(
    count_any, cell_any, value_any, weight_any, ens_any,
    applied, blend_ref,
    count_ref, cell_ref, given, cells_ref, ens, ens32, picked, rows, deviations, scaled, matrices, stationary,
    stat_x, stat_y, got_x, got_y, nearby, transforms, own_ref,
    small_sem, load_sem, own_sem, send_x, recv_x, send_y, recv_y, send_t, recv_t,
):
    gx, gy = lax.axis_index("gx"), lax.axis_index("gy")
    nx, ny = lax.axis_size("gx"), lax.axis_size("gy")

    def at(a, b):
        return (lax.rem(gx + a + nx, nx), lax.rem(gy + b + ny, ny))

    small = [
        pltpu.make_async_copy(count_any, count_ref, small_sem.at[0]),
        pltpu.make_async_copy(cell_any, cell_ref, small_sem.at[1]),
        pltpu.make_async_copy(cell_any, cells_ref, small_sem.at[2]),
        pltpu.make_async_copy(value_any, given.at[0], small_sem.at[3]),
        pltpu.make_async_copy(weight_any, given.at[1], small_sem.at[4]),
    ]
    for copy in small:
        copy.start()

    @pl.loop(0, CX)
    def _(i):
        pltpu.make_async_copy(column(ens_any, i), column(ens, i), load_sem.at[i]).start()

    partners = [(s, 0) for s in STAT_STEPS] + [(0, s) for s in STAT_STEPS]
    partners += [(a, b) for a in (-1, 1) for b in (-1, 1)]
    barrier = pltpu.get_barrier_semaphore()
    for a, b in partners:
        pl.semaphore_signal(barrier, inc=1, device_id=at(a, b), device_id_type=MESH)

    for copy in small:
        copy.wait()
    count = count_ref[gx, gy]
    cells = cells_ref[...].astype(F32)
    slot = lax.broadcasted_iota(jnp.int32, (1, OBS), 1)
    rows[0:1] = jnp.where(slot < count, given[1], 0.0)
    rows[1:2] = given[0]
    east = jnp.floor((cells + 0.5) * (1.0 / XROWS))
    north = jnp.floor((cells - XROWS * east + 0.5) * (1.0 / LEV))
    hat_x, hat_y = hats((east + 0.5) / CX), hats((north + 0.5) / CY)
    for slot in range(9):
        rows[3 + slot : 4 + slot] = hat_x[slot // 3] * hat_y[slot % 3]

    @pl.loop(0, CX)
    def _(i):
        pltpu.make_async_copy(column(ens_any, i), column(ens, i), load_sem.at[i]).wait()
        start = pl.multiple_of(i * XROWS, XROWS)
        ens32[pl.ds(start, XROWS)] = ens[pl.ds(start, XROWS)].astype(F32)

    @pl.loop(0, OBS // GATHER)
    def _(g):
        for r in range(GATHER):
            o = g * GATHER + r
            picked[pl.ds(o, 1)] = ens32[pl.ds(cell_ref[0, o], 1)]

    def accumulate(total, lanes, deviation, centre):
        scale, value = rows[0:1, lanes], rows[1:2, lanes]
        anomaly = (scale * deviation).astype(BF16)
        innovation = jnp.broadcast_to(scale * (value - centre), (16, QUART)).astype(BF16)
        return total + mm_nt(jnp.concatenate([anomaly, innovation], axis=0), anomaly)

    def exchange(t, sent, got, send_sem, recv_sem, shift):
        copies = []
        for k, step in enumerate(STAT_STEPS):
            there = STAT_STEPS.index(-step)
            copies.append(
                pltpu.make_async_remote_copy(
                    src_ref=sent.at[t],
                    dst_ref=got.at[t, there],
                    send_sem=send_sem.at[t, k],
                    recv_sem=recv_sem.at[t, there],
                    device_id=at(*shift(step)),
                    device_id_type=MESH,
                )
            )
        return copies

    pending = []

    def settle():
        while pending:
            pending.pop().wait_send()

    def weighted(t, total, got, copies):
        for k in reversed(range(4)):
            copies[STAT_STEPS.index(-STAT_STEPS[k])].wait_recv()
            total = total + STAT_WEIGHTS[k] * got[t, k].astype(F32)
        pending.extend(copies)
        return total

    def nothing(i):
        pass

    def apply_some(first, last):
        apply_columns(first, last, matrices, stationary, ens, applied, nothing, nothing)

    for t in range(ITERS):
        total = jnp.zeros((K + 16, K), F32)
        if t == 0:
            row, col = iotas((K + 16, K))
            centre_rows = jnp.where(row == col, (K - 1.0) / K, jnp.where(row < K, -1.0 / K, 1.0 / K))
            centre_rows = centre_rows.astype(BF16)
            for q in range(OBS // QUART):
                lanes = slice(q * QUART, (q + 1) * QUART)
                moved = mm_nt(centre_rows, picked[lanes].astype(BF16))
                total = accumulate(total, lanes, moved[:K], moved[K : K + 1])
                deviations[:, lanes] = moved[:K]
                rows[2:3, lanes] = moved[K : K + 1]
        else:
            for q in range(OBS // QUART):
                lanes = slice(q * QUART, (q + 1) * QUART)
                fresh = rows[2:3, lanes] + mm(transforms[...], scaled[:, lanes])
                fresh = fresh.astype(BF16).astype(F32)
                centre = jnp.sum(fresh, axis=0, keepdims=True) * (1.0 / K)
                total = accumulate(total, lanes, fresh - centre, centre)
        own = opened(total[:K], total[K : K + 1])
        stat_x[t] = closed(own)

        if t == 0:
            pl.semaphore_wait(barrier, len(partners))
        copies = exchange(t, stat_x, got_x, send_x, recv_x, lambda step: (step, 0))
        for copy in copies:
            copy.start()
        if t == 1:
            for slot in range(9):
                matrices[slot * K : (slot + 1) * K] = full_matrices(transforms[:, slot * K : (slot + 1) * K])
            apply_some(0, CX // 2)
            settle()
        own = weighted(t, own, got_x, copies)
        stat_y[t] = closed(own)
        copies = exchange(t, stat_y, got_y, send_y, recv_y, lambda step: (0, step))
        for copy in reversed(copies):
            copy.start()
        if t == 1:
            apply_some(CX // 2, CX)
        spread, weights = transform_parts(weighted(t, own, got_y, copies))
        own_ref[t] = closed(opened(spread, weights))
        landing = nearby if t == 0 else blend_ref
        copies = {}
        for k, (a, b) in enumerate(BLEND_STEPS):
            there = slot_of(-a, -b)
            copies[(-a, -b)] = pltpu.make_async_remote_copy(
                src_ref=own_ref.at[t],
                dst_ref=landing.at[there],
                send_sem=send_t.at[t, k],
                recv_sem=recv_t.at[t, there],
                device_id=at(a, b),
                device_id_type=MESH,
            )
        for copy in copies.values():
            copy.start()
        own = slot_of(0, 0)
        if t == 0:
            transforms[:, own * K : (own + 1) * K] = (weights + spread).astype(BF16)

            @pl.loop(0, OBS // PART)
            def _(q):
                lanes = pl.ds(pl.multiple_of(q * PART, PART), PART)
                for slot in range(9):
                    part = rows[3 + slot : 4 + slot, lanes] * deviations[:, lanes]
                    scaled[slot * K : (slot + 1) * K, lanes] = part.astype(BF16)

        else:
            mine = pltpu.make_async_copy(own_ref.at[t], landing.at[own], own_sem)
            mine.start()
            settle()
        for step in reversed(BLEND_STEPS):
            copies[step].wait_recv()
        if t == 0:
            for step in BLEND_STEPS:
                slot = slot_of(*step)
                transforms[:, slot * K : (slot + 1) * K] = unpack_transform(nearby[slot])
        else:
            mine.wait()
        pending.extend(copies.values())
    settle()


def last_kernel(nearby, ens, out_any, applied, transforms, matrices, stationary, store_sem):
    for slot in range(9):
        transforms[slot * K : (slot + 1) * K] = unpack_transform(nearby[slot])
    matrices[...] = full_matrices(transforms[...])

    def nothing(i):
        pass

    def store(i):
        pltpu.make_async_copy(column(applied, i), column(out_any, i), store_sem.at[i]).start()

    apply_columns(0, CX, matrices, stationary, ens, applied, nothing, store)

    @pl.loop(0, CX)
    def _(i):
        pltpu.make_async_copy(column(applied, i), column(out_any, i), store_sem.at[i]).wait()


def shards(ensemble, obs_cell, obs_value, obs_weight, obs_count):
    flat = ensemble.reshape(ROWS, K)
    anywhere = pl.BlockSpec(memory_space=pl.ANY)
    fixed = pl.BlockSpec(memory_space=pltpu.HBM)
    dma = pltpu.SemaphoreType.DMA
    following, blend = pl.pallas_call(
        first_kernel,
        out_shape=(
            jax.ShapeDtypeStruct((ROWS, K), BF16),
            jax.ShapeDtypeStruct((9, PACKED, K), BF16),
        ),
        in_specs=[fixed] * 5,
        out_specs=(pl.BlockSpec(memory_space=pltpu.VMEM), anywhere),
        scratch_shapes=[
            pltpu.SMEM((BX, BY), jnp.int32),
            pltpu.SMEM((1, OBS), jnp.int32),
            pltpu.VMEM((2, 1, OBS), F32),
            pltpu.VMEM((1, OBS), jnp.int32),
            pltpu.VMEM((ROWS, K), BF16),
            pltpu.VMEM((ROWS, K), F32),
            pltpu.VMEM((OBS, K), F32),
            pltpu.VMEM((16, OBS), F32),
            pltpu.VMEM((K, OBS), F32),
            pltpu.VMEM((9 * K, OBS), BF16),
            pltpu.VMEM((9 * K, K), F32),
            pltpu.VMEM((2, 3 * K, 2 * K), BF16),
            pltpu.VMEM((ITERS, PACKED, K), BF16),
            pltpu.VMEM((ITERS, PACKED, K), BF16),
            pltpu.VMEM((ITERS, 4, PACKED, K), BF16),
            pltpu.VMEM((ITERS, 4, PACKED, K), BF16),
            pltpu.VMEM((9, PACKED, K), BF16),
            pltpu.VMEM((K, 9 * K), BF16),
            pltpu.VMEM((ITERS, PACKED, K), BF16),
            dma((5,)),
            dma((CX,)),
            dma(()),
            dma((ITERS, 4)),
            dma((ITERS, 4)),
            dma((ITERS, 4)),
            dma((ITERS, 4)),
            dma((ITERS, 8)),
            dma((ITERS, 9)),
        ],
        compiler_params=pltpu.CompilerParams(
            collective_id=0, has_side_effects=True, vmem_limit_bytes=44 * 1024 * 1024
        ),
        name="analyse",
    )(
        *(
            pltpu.with_memory_space_constraint(array, pltpu.HBM)
            for array in (
                obs_count,
                obs_cell.reshape(1, OBS),
                obs_value.reshape(1, OBS),
                obs_weight.reshape(1, OBS),
                flat,
            )
        )
    )
    out = pl.pallas_call(
        last_kernel,
        out_shape=jax.ShapeDtypeStruct((ROWS, K), BF16),
        in_specs=[pl.BlockSpec(memory_space=pltpu.VMEM)] * 2,
        out_specs=fixed,
        scratch_shapes=[
            pltpu.VMEM((ROWS, K), BF16),
            pltpu.VMEM((9 * K, K), BF16),
            pltpu.VMEM((9 * K, K), F32),
            pltpu.VMEM((2, 3 * K, 2 * K), BF16),
            dma((CX,)),
        ],
        compiler_params=pltpu.CompilerParams(vmem_limit_bytes=44 * 1024 * 1024),
        name="blend",
    )(blend, following)
    return out.reshape(ensemble.shape)


def solution(mesh):
    placed = (
        P("gx", "gy", None, None),
        P("gx", "gy", None),
        P("gx", "gy", None),
        P("gx", "gy", None),
        P(),
    )
    return jax.shard_map(
        shards, mesh=mesh, in_specs=placed, out_specs=P("gx", "gy", None, None), check_vma=False
    )
```

```python
import jax
import jax.numpy as jnp
from jax import lax
from jax.experimental import pallas as pl
from jax.experimental.pallas import tpu as pltpu
from jax.sharding import PartitionSpec as P

K = 128
CX = 16
CY = 32
LEV = 48
ROWS = CX * CY * LEV
XROWS = CY * LEV
OBS = 2048
NEWTON = 6
ITERS = 2
QUART = 512
PART = 256
GROUP = 8
UNROLL = 4
SLOTS = 4
GATHER = 64
PACKED = 80
BX = 8
BY = 16

MESH = pl.DeviceIdType.MESH
F32 = jnp.float32
BF16 = jnp.bfloat16
STAT_STEPS = (-1, 1, -2, 2)
STAT_WEIGHTS = (0.75, 0.75, 0.5, 0.5)
BLEND_STEPS = tuple((a, b) for a in (-1, 1, 0) for b in (-1, 1, 0) if (a, b) != (0, 0))


def slot_of(a, b):
    return (a + 1) * 3 + (b + 1)


def mm(a, b):
    return jnp.dot(a, b, preferred_element_type=F32)


def mm_nt(a, b):
    return lax.dot_general(a, b, (((1,), (1,)), ((), ())), preferred_element_type=F32)


def split(x):
    high = x.astype(BF16)
    low = (x - high.astype(F32)).astype(BF16)
    return high, low


def wide(x):
    high, low = split(x)
    return jnp.concatenate([high, low], axis=1)


def times(a, b):
    both = wide(b)
    out = mm(wide(a), jnp.concatenate([both, both], axis=0))
    return out[:, :K] + out[:, K:]


def iotas(shape):
    return lax.broadcasted_iota(jnp.int32, shape, 0), lax.broadcasted_iota(jnp.int32, shape, 1)


def centring():
    row, col = iotas((K, K))
    return jnp.where(row == col, (K - 1.0) / K, -1.0 / K).astype(BF16)


def fold(matrix):
    half = K // 2
    row, lane = iotas((half, K))
    return jnp.where(lane < row, pltpu.roll(matrix[half:], half, 1), matrix[:half])


def unfold(body, diagonal):
    half = K // 2
    row, lane = iotas((half, K))
    flipped = jnp.concatenate([body, jnp.zeros((half, K), F32)], axis=0).T
    top = jnp.where(lane < row, flipped[:half], body)
    lower = jnp.where(lane < row, body, flipped[:half])
    bottom = jnp.where(lane < half, flipped[half:], pltpu.roll(lower, half, 1))
    row, col = iotas((K, K))
    return jnp.where(row == col, diagonal, jnp.concatenate([top, bottom], axis=0))


def diagonal_of(matrix):
    row, col = iotas((K, K))
    return jnp.sum(jnp.where(row == col, matrix, 0.0), axis=0, keepdims=True)


def opened(symmetric, line):
    tail_row, _ = iotas((PACKED - K // 2, K))
    tail = jnp.where(tail_row == 0, diagonal_of(symmetric), jnp.where(tail_row == 2, line, 0.0))
    return jnp.concatenate([fold(symmetric), tail], axis=0)


def lines_of(packed):
    half = K // 2
    diagonal = packed[half : half + 1] + packed[half + 1 : half + 2]
    return diagonal, packed[half + 2 : half + 3] + packed[half + 3 : half + 4]


def closed(packed):
    tail_row, _ = iotas((PACKED - K // 2, K))
    tail = jnp.zeros((PACKED - K // 2, K), F32)
    for k, line in enumerate(lines_of(packed)):
        high, low = split(line)
        tail = jnp.where(tail_row == 2 * k, high.astype(F32), tail)
        tail = jnp.where(tail_row == 2 * k + 1, low.astype(F32), tail)
    return jnp.concatenate([packed[: K // 2], tail], axis=0).astype(BF16)


def unpack(packed):
    diagonal, line = lines_of(packed)
    return unfold(packed[: K // 2], diagonal), line


def unpack_transform(packed):
    spread, weights = unpack(packed.astype(F32))
    return (weights + spread).astype(BF16)


def transform_parts(packed):
    gram, projected = unpack(packed)
    row, col = iotas((K, K))
    identity = jnp.where(row == col, 1.0, 0.0).astype(F32)
    system = gram + (K - 1) * identity
    squares = jnp.sum(system * system, axis=0, keepdims=True)
    frobenius = jnp.sqrt(jnp.sum(squares, axis=1, keepdims=True))
    root = system / frobenius
    correction = 1.5 * identity - 0.5 * root
    root, inverse = times(correction, root), correction
    for step in range(1, NEWTON - 1):
        correction = 1.5 * identity - 0.5 * times(inverse, root)
        root, inverse = times(correction, root), times(correction, inverse)
    correction = 1.5 * identity - 0.5 * times(inverse, root)
    carried = times(jnp.broadcast_to(projected, (16, K)), inverse)
    carried, inverse = times(carried, correction), times(correction, inverse)
    weights = times(carried, inverse)[0:1] / frobenius
    return jnp.sqrt((K - 1) / frobenius) * inverse, weights


def hats(position):
    below = jnp.maximum(0.0, 0.5 - position)
    above = jnp.maximum(0.0, position - 0.5)
    return below, 1.0 - below - above, above


def hat_of(j, count):
    position = (j + 0.5) / count
    below, above = max(0.0, 0.5 - position), max(0.0, position - 0.5)
    return below, 1.0 - below - above, above


def blend_column(i, slot, matrices, stationary):
    static = isinstance(i, int)
    weights = hat_of(i, CX) if static else hats((i.astype(F32) + 0.5) / CX)
    for b in range(3):
        blend = None
        for a in range(3):
            if static and weights[a] == 0.0:
                continue
            at = (a * 3 + b) * K
            term = weights[a] * matrices[at : at + K]
            blend = term if blend is None else blend + term
        stationary[slot, b * K : (b + 1) * K] = wide(blend)


def row_of(i, offset=0):
    row = i * XROWS + offset
    return row if isinstance(i, int) else pl.multiple_of(row, 16)


def apply_column(i, slot, ens, fresh, stationary):
    for half in range(2):
        matrix = stationary[slot, half * K : half * K + 2 * K]
        for group in range(CY // 2 // GROUP):
            first = half * (CY // 2) + group * GROUP
            here = pl.ds(row_of(i, first * LEV), GROUP * LEV)
            block = ens[here]
            out = mm_nt(jnp.concatenate([block, block], axis=1), matrix)
            parts = []
            for j in range(GROUP):
                hat = hat_of(first + j, CY)
                piece = out[j * LEV : (j + 1) * LEV]
                parts.append(hat[half] * piece[:, :K] + hat[half + 1] * piece[:, K:])
            fresh[here] = jnp.concatenate(parts, axis=0).astype(BF16)


def apply_columns(first, last, matrices, stationary, ens, fresh):
    blend_column(jnp.int32(first), 0, matrices, stationary)

    @pl.loop(first // UNROLL, last // UNROLL)
    def _(step):
        for k in range(UNROLL):
            i = step * UNROLL + k
            apply_column(i, k % 2, ens, fresh, stationary)
            blend_column(jnp.minimum(i + 1, CX - 1), 1 - k % 2, matrices, stationary)


def full_matrices(transforms):
    return mm(transforms, centring()) + 1.0 / K


def column(ref, i):
    return ref.at[pl.ds(row_of(i), XROWS)]


def first_kernel(
    count_any, cell_any, value_any, weight_any, ens_any,
    applied, blend_ref,
    count_ref, cell_ref, given, cells_ref, ens, ens32, picked, rows, deviations, scaled, matrices, stationary,
    stat_x, stat_y, got_x, got_y, nearby, transforms, own_ref,
    small_sem, load_sem, own_sem, send_x, recv_x, send_y, recv_y, send_t, recv_t,
):
    gx, gy = lax.axis_index("gx"), lax.axis_index("gy")
    nx, ny = lax.axis_size("gx"), lax.axis_size("gy")

    def at(a, b):
        return (lax.rem(gx + a + nx, nx), lax.rem(gy + b + ny, ny))

    small = [
        pltpu.make_async_copy(count_any, count_ref, small_sem.at[0]),
        pltpu.make_async_copy(cell_any, cell_ref, small_sem.at[1]),
        pltpu.make_async_copy(cell_any, cells_ref, small_sem.at[2]),
        pltpu.make_async_copy(value_any, given.at[0], small_sem.at[3]),
        pltpu.make_async_copy(weight_any, given.at[1], small_sem.at[4]),
    ]
    for copy in small:
        copy.start()

    @pl.loop(0, CX)
    def _(i):
        pltpu.make_async_copy(column(ens_any, i), column(ens, i), load_sem.at[i]).start()

    partners = [(s, 0) for s in STAT_STEPS] + [(0, s) for s in STAT_STEPS]
    partners += [(a, b) for a in (-1, 1) for b in (-1, 1)]
    barrier = pltpu.get_barrier_semaphore()
    for a, b in partners:
        pl.semaphore_signal(barrier, inc=1, device_id=at(a, b), device_id_type=MESH)

    for copy in small:
        copy.wait()
    count = count_ref[gx, gy]
    cells = cells_ref[...].astype(F32)
    slot = lax.broadcasted_iota(jnp.int32, (1, OBS), 1)
    rows[0:1] = jnp.where(slot < count, given[1], 0.0)
    rows[1:2] = given[0]
    east = jnp.floor((cells + 0.5) * (1.0 / XROWS))
    north = jnp.floor((cells - XROWS * east + 0.5) * (1.0 / LEV))
    hat_x, hat_y = hats((east + 0.5) / CX), hats((north + 0.5) / CY)
    for slot in range(9):
        rows[3 + slot : 4 + slot] = hat_x[slot // 3] * hat_y[slot % 3]

    @pl.loop(0, CX)
    def _(i):
        pltpu.make_async_copy(column(ens_any, i), column(ens, i), load_sem.at[i]).wait()
        start = pl.multiple_of(i * XROWS, XROWS)
        ens32[pl.ds(start, XROWS)] = ens[pl.ds(start, XROWS)].astype(F32)

    @pl.loop(0, OBS // GATHER)
    def _(g):
        for r in range(GATHER):
            o = g * GATHER + r
            picked[pl.ds(o, 1)] = ens32[pl.ds(cell_ref[0, o], 1)]

    def accumulate(total, lanes, deviation, centre):
        scale, value = rows[0:1, lanes], rows[1:2, lanes]
        anomaly = (scale * deviation).astype(BF16)
        innovation = jnp.broadcast_to(scale * (value - centre), (16, QUART)).astype(BF16)
        return total + mm_nt(jnp.concatenate([anomaly, innovation], axis=0), anomaly)

    def exchange(t, sent, got, send_sem, recv_sem, shift):
        copies = []
        for k, step in enumerate(STAT_STEPS):
            there = STAT_STEPS.index(-step)
            copies.append(
                pltpu.make_async_remote_copy(
                    src_ref=sent.at[t],
                    dst_ref=got.at[t, there],
                    send_sem=send_sem.at[t, k],
                    recv_sem=recv_sem.at[t, there],
                    device_id=at(*shift(step)),
                    device_id_type=MESH,
                )
            )
        return copies

    pending = []

    def settle():
        while pending:
            pending.pop().wait_send()

    def weighted(t, total, got, copies):
        for k in reversed(range(4)):
            copies[STAT_STEPS.index(-STAT_STEPS[k])].wait_recv()
            total = total + STAT_WEIGHTS[k] * got[t, k].astype(F32)
        pending.extend(copies)
        return total

    def apply_some(first, last):
        apply_columns(first, last, matrices, stationary, ens, applied)

    for t in range(ITERS):
        total = jnp.zeros((K + 16, K), F32)
        if t == 0:
            row, col = iotas((K + 16, K))
            centre_rows = jnp.where(row == col, (K - 1.0) / K, jnp.where(row < K, -1.0 / K, 1.0 / K))
            centre_rows = centre_rows.astype(BF16)
            for q in range(OBS // QUART):
                lanes = slice(q * QUART, (q + 1) * QUART)
                moved = mm_nt(centre_rows, picked[lanes].astype(BF16))
                total = accumulate(total, lanes, moved[:K], moved[K : K + 1])
                deviations[:, lanes] = moved[:K]
                rows[2:3, lanes] = moved[K : K + 1]
        else:
            for q in range(OBS // QUART):
                lanes = slice(q * QUART, (q + 1) * QUART)
                fresh = rows[2:3, lanes] + mm(transforms[...], scaled[:, lanes])
                fresh = fresh.astype(BF16).astype(F32)
                centre = jnp.sum(fresh, axis=0, keepdims=True) * (1.0 / K)
                total = accumulate(total, lanes, fresh - centre, centre)
        own = opened(total[:K], total[K : K + 1])
        stat_x[t] = closed(own)

        if t == 0:
            pl.semaphore_wait(barrier, len(partners))
        copies = exchange(t, stat_x, got_x, send_x, recv_x, lambda step: (step, 0))
        for copy in copies:
            copy.start()
        if t == 1:
            for slot in range(9):
                matrices[slot * K : (slot + 1) * K] = full_matrices(transforms[:, slot * K : (slot + 1) * K])
            apply_some(0, CX // 2)
            settle()
        own = weighted(t, own, got_x, copies)
        stat_y[t] = closed(own)
        copies = exchange(t, stat_y, got_y, send_y, recv_y, lambda step: (0, step))
        for copy in reversed(copies):
            copy.start()
        if t == 1:
            apply_some(CX // 2, CX)
        spread, weights = transform_parts(weighted(t, own, got_y, copies))
        own_ref[t] = closed(opened(spread, weights))
        landing = nearby if t == 0 else blend_ref
        copies = {}
        for k, (a, b) in enumerate(BLEND_STEPS):
            there = slot_of(-a, -b)
            copies[(-a, -b)] = pltpu.make_async_remote_copy(
                src_ref=own_ref.at[t],
                dst_ref=landing.at[there],
                send_sem=send_t.at[t, k],
                recv_sem=recv_t.at[t, there],
                device_id=at(a, b),
                device_id_type=MESH,
            )
        for copy in copies.values():
            copy.start()
        own = slot_of(0, 0)
        if t == 0:
            transforms[:, own * K : (own + 1) * K] = (weights + spread).astype(BF16)

            @pl.loop(0, OBS // PART)
            def _(q):
                lanes = pl.ds(pl.multiple_of(q * PART, PART), PART)
                for slot in range(9):
                    part = rows[3 + slot : 4 + slot, lanes] * deviations[:, lanes]
                    scaled[slot * K : (slot + 1) * K, lanes] = part.astype(BF16)

        else:
            mine = pltpu.make_async_copy(own_ref.at[t], landing.at[own], own_sem)
            mine.start()
            settle()
        for step in reversed(BLEND_STEPS):
            copies[step].wait_recv()
        if t == 0:
            for step in BLEND_STEPS:
                slot = slot_of(*step)
                transforms[:, slot * K : (slot + 1) * K] = unpack_transform(nearby[slot])
        else:
            mine.wait()
        pending.extend(copies.values())
    settle()


def last_kernel(nearby, ens, out_any, applied, matrices, stationary, store_sem):
    def ready(slots):
        for slot in slots:
            matrices[slot * K : (slot + 1) * K] = full_matrices(unpack_transform(nearby[slot]))

    def store(i):
        return pltpu.make_async_copy(column(applied, i), column(out_any, i), store_sem.at[i])

    ready(range(6))
    blend_column(0, 0, matrices, stationary)
    for i in range(CX):
        apply_column(i, i % SLOTS, ens, applied, stationary)
        if i + 1 < CX:
            blend_column(i + 1, (i + 1) % SLOTS, matrices, stationary)
        store(i).start()
        if i == 1:
            ready(range(6, 9))

    for i in range(CX):
        store(i).wait()


def shards(ensemble, obs_cell, obs_value, obs_weight, obs_count):
    flat = ensemble.reshape(ROWS, K)
    anywhere = pl.BlockSpec(memory_space=pl.ANY)
    fixed = pl.BlockSpec(memory_space=pltpu.HBM)
    dma = pltpu.SemaphoreType.DMA
    following, blend = pl.pallas_call(
        first_kernel,
        out_shape=(
            jax.ShapeDtypeStruct((ROWS, K), BF16),
            jax.ShapeDtypeStruct((9, PACKED, K), BF16),
        ),
        in_specs=[fixed] * 5,
        out_specs=(pl.BlockSpec(memory_space=pltpu.VMEM), anywhere),
        scratch_shapes=[
            pltpu.SMEM((BX, BY), jnp.int32),
            pltpu.SMEM((1, OBS), jnp.int32),
            pltpu.VMEM((2, 1, OBS), F32),
            pltpu.VMEM((1, OBS), jnp.int32),
            pltpu.VMEM((ROWS, K), BF16),
            pltpu.VMEM((ROWS, K), F32),
            pltpu.VMEM((OBS, K), F32),
            pltpu.VMEM((16, OBS), F32),
            pltpu.VMEM((K, OBS), F32),
            pltpu.VMEM((9 * K, OBS), BF16),
            pltpu.VMEM((9 * K, K), F32),
            pltpu.VMEM((2, 3 * K, 2 * K), BF16),
            pltpu.VMEM((ITERS, PACKED, K), BF16),
            pltpu.VMEM((ITERS, PACKED, K), BF16),
            pltpu.VMEM((ITERS, 4, PACKED, K), BF16),
            pltpu.VMEM((ITERS, 4, PACKED, K), BF16),
            pltpu.VMEM((9, PACKED, K), BF16),
            pltpu.VMEM((K, 9 * K), BF16),
            pltpu.VMEM((ITERS, PACKED, K), BF16),
            dma((5,)),
            dma((CX,)),
            dma(()),
            dma((ITERS, 4)),
            dma((ITERS, 4)),
            dma((ITERS, 4)),
            dma((ITERS, 4)),
            dma((ITERS, 8)),
            dma((ITERS, 9)),
        ],
        compiler_params=pltpu.CompilerParams(
            collective_id=0, has_side_effects=True, vmem_limit_bytes=44 * 1024 * 1024
        ),
        name="analyse",
    )(
        *(
            pltpu.with_memory_space_constraint(array, pltpu.HBM)
            for array in (
                obs_count,
                obs_cell.reshape(1, OBS),
                obs_value.reshape(1, OBS),
                obs_weight.reshape(1, OBS),
                flat,
            )
        )
    )
    out = pl.pallas_call(
        last_kernel,
        out_shape=jax.ShapeDtypeStruct((ROWS, K), BF16),
        in_specs=[pl.BlockSpec(memory_space=pltpu.VMEM)] * 2,
        out_specs=fixed,
        scratch_shapes=[
            pltpu.VMEM((ROWS, K), BF16),
            pltpu.VMEM((9 * K, K), F32),
            pltpu.VMEM((SLOTS, 3 * K, 2 * K), BF16),
            dma((CX,)),
        ],
        compiler_params=pltpu.CompilerParams(vmem_limit_bytes=44 * 1024 * 1024),
        name="blend",
    )(blend, following)
    return out.reshape(ensemble.shape)


def solution(mesh):
    placed = (
        P("gx", "gy", None, None),
        P("gx", "gy", None),
        P("gx", "gy", None),
        P("gx", "gy", None),
        P(),
    )
    return jax.shard_map(
        shards, mesh=mesh, in_specs=placed, out_specs=P("gx", "gy", None, None), check_vma=False
    )
```

```python
import jax
import jax.numpy as jnp
from jax import lax
from jax.experimental import pallas as pl
from jax.experimental.pallas import tpu as pltpu
from jax.sharding import PartitionSpec as P

K = 128
CX = 16
CY = 32
LEV = 48
ROWS = CX * CY * LEV
XROWS = CY * LEV
OBS = 2048
NEWTON = 6
ITERS = 2
QUART = 512
PART = 256
GROUP = 8
UNROLL = 4
SLOTS = 4
GATHER = 64
PACKED = 80
BX = 8
BY = 16

MESH = pl.DeviceIdType.MESH
F32 = jnp.float32
BF16 = jnp.bfloat16
STAT_STEPS = (-1, 1, -2, 2)
STAT_WEIGHTS = (0.75, 0.75, 0.5, 0.5)
BLEND_STEPS = tuple((a, b) for a in (-1, 1, 0) for b in (-1, 1, 0) if (a, b) != (0, 0))


def slot_of(a, b):
    return (a + 1) * 3 + (b + 1)


def mm(a, b):
    return jnp.dot(a, b, preferred_element_type=F32)


def mm_nt(a, b):
    return lax.dot_general(a, b, (((1,), (1,)), ((), ())), preferred_element_type=F32)


def split(x):
    high = x.astype(BF16)
    low = (x - high.astype(F32)).astype(BF16)
    return high, low


def wide(x):
    high, low = split(x)
    return jnp.concatenate([high, low], axis=1)


def times(a, b):
    both = wide(b)
    out = mm(wide(a), jnp.concatenate([both, both], axis=0))
    return out[:, :K] + out[:, K:]


def iotas(shape):
    return lax.broadcasted_iota(jnp.int32, shape, 0), lax.broadcasted_iota(jnp.int32, shape, 1)


def centring():
    row, col = iotas((K, K))
    return jnp.where(row == col, (K - 1.0) / K, -1.0 / K).astype(BF16)


def fold(matrix):
    half = K // 2
    row, lane = iotas((half, K))
    return jnp.where(lane < row, pltpu.roll(matrix[half:], half, 1), matrix[:half])


def unfold(body, diagonal):
    half = K // 2
    row, lane = iotas((half, K))
    flipped = jnp.concatenate([body, jnp.zeros((half, K), F32)], axis=0).T
    top = jnp.where(lane < row, flipped[:half], body)
    lower = jnp.where(lane < row, body, flipped[:half])
    bottom = jnp.where(lane < half, flipped[half:], pltpu.roll(lower, half, 1))
    row, col = iotas((K, K))
    return jnp.where(row == col, diagonal, jnp.concatenate([top, bottom], axis=0))


def diagonal_of(matrix):
    row, col = iotas((K, K))
    return jnp.sum(jnp.where(row == col, matrix, 0.0), axis=0, keepdims=True)


def opened(symmetric, line):
    tail_row, _ = iotas((PACKED - K // 2, K))
    tail = jnp.where(tail_row == 0, diagonal_of(symmetric), jnp.where(tail_row == 2, line, 0.0))
    return jnp.concatenate([fold(symmetric), tail], axis=0)


def lines_of(packed):
    half = K // 2
    diagonal = packed[half : half + 1] + packed[half + 1 : half + 2]
    return diagonal, packed[half + 2 : half + 3] + packed[half + 3 : half + 4]


def closed(packed):
    tail_row, _ = iotas((PACKED - K // 2, K))
    tail = jnp.zeros((PACKED - K // 2, K), F32)
    for k, line in enumerate(lines_of(packed)):
        high, low = split(line)
        tail = jnp.where(tail_row == 2 * k, high.astype(F32), tail)
        tail = jnp.where(tail_row == 2 * k + 1, low.astype(F32), tail)
    return jnp.concatenate([packed[: K // 2], tail], axis=0).astype(BF16)


def unpack(packed):
    diagonal, line = lines_of(packed)
    return unfold(packed[: K // 2], diagonal), line


def unpack_transform(packed):
    spread, weights = unpack(packed.astype(F32))
    return (weights + spread).astype(BF16)


def transform_parts(packed):
    gram, projected = unpack(packed)
    row, col = iotas((K, K))
    identity = jnp.where(row == col, 1.0, 0.0).astype(F32)
    system = gram + (K - 1) * identity
    squares = jnp.sum(system * system, axis=0, keepdims=True)
    frobenius = jnp.sqrt(jnp.sum(squares, axis=1, keepdims=True))
    root = system / frobenius
    correction = 1.5 * identity - 0.5 * root
    root, inverse = times(correction, root), correction
    for step in range(1, NEWTON - 1):
        correction = 1.5 * identity - 0.5 * times(inverse, root)
        root, inverse = times(correction, root), times(correction, inverse)
    correction = 1.5 * identity - 0.5 * times(inverse, root)
    carried = times(jnp.broadcast_to(projected, (16, K)), inverse)
    carried, inverse = times(carried, correction), times(correction, inverse)
    weights = times(carried, inverse)[0:1] / frobenius
    return jnp.sqrt((K - 1) / frobenius) * inverse, weights


def hats(position):
    below = jnp.maximum(0.0, 0.5 - position)
    above = jnp.maximum(0.0, position - 0.5)
    return below, 1.0 - below - above, above


def hat_of(j, count):
    position = (j + 0.5) / count
    below, above = max(0.0, 0.5 - position), max(0.0, position - 0.5)
    return below, 1.0 - below - above, above


def blend_column(i, slot, matrix_of, stationary):
    static = isinstance(i, int)
    weights = hat_of(i, CX) if static else hats((i.astype(F32) + 0.5) / CX)
    for b in range(3):
        blend = None
        for a in range(3):
            if static and weights[a] == 0.0:
                continue
            term = weights[a] * matrix_of(a * 3 + b)
            blend = term if blend is None else blend + term
        stationary[slot, b * K : (b + 1) * K] = wide(blend)


def row_of(i, offset=0):
    row = i * XROWS + offset
    return row if isinstance(i, int) else pl.multiple_of(row, 16)


def apply_column(i, slot, ens, fresh, stationary):
    for half in range(2):
        matrix = stationary[slot, half * K : half * K + 2 * K]
        for group in range(CY // 2 // GROUP):
            first = half * (CY // 2) + group * GROUP
            here = pl.ds(row_of(i, first * LEV), GROUP * LEV)
            block = ens[here]
            out = mm_nt(jnp.concatenate([block, block], axis=1), matrix)
            parts = []
            for j in range(GROUP):
                hat = hat_of(first + j, CY)
                piece = out[j * LEV : (j + 1) * LEV]
                parts.append(hat[half] * piece[:, :K] + hat[half + 1] * piece[:, K:])
            fresh[here] = jnp.concatenate(parts, axis=0).astype(BF16)


def apply_columns(first, last, matrix_of, stationary, ens, fresh):
    blend_column(jnp.int32(first), 0, matrix_of, stationary)

    @pl.loop(first // UNROLL, last // UNROLL)
    def _(step):
        for k in range(UNROLL):
            i = step * UNROLL + k
            apply_column(i, k % 2, ens, fresh, stationary)
            blend_column(jnp.minimum(i + 1, CX - 1), 1 - k % 2, matrix_of, stationary)


def full_matrices(transforms):
    return mm(transforms, centring()) + 1.0 / K


def column(ref, i):
    return ref.at[pl.ds(row_of(i), XROWS)]


def first_kernel(
    count_any, cell_any, value_any, weight_any, ens_any,
    applied, blend_ref, middle_ref,
    count_ref, cell_ref, given, cells_ref, ens, ens32, picked, rows, deviations, scaled, matrices, stationary,
    stat_x, stat_y, got_x, got_y, nearby, transforms, own_ref,
    small_sem, load_sem, own_sem, send_x, recv_x, send_y, recv_y, send_t, recv_t,
):
    gx, gy = lax.axis_index("gx"), lax.axis_index("gy")
    nx, ny = lax.axis_size("gx"), lax.axis_size("gy")

    def at(a, b):
        return (lax.rem(gx + a + nx, nx), lax.rem(gy + b + ny, ny))

    small = [
        pltpu.make_async_copy(count_any, count_ref, small_sem.at[0]),
        pltpu.make_async_copy(cell_any, cell_ref, small_sem.at[1]),
        pltpu.make_async_copy(cell_any, cells_ref, small_sem.at[2]),
        pltpu.make_async_copy(value_any, given.at[0], small_sem.at[3]),
        pltpu.make_async_copy(weight_any, given.at[1], small_sem.at[4]),
    ]
    for copy in small:
        copy.start()

    @pl.loop(0, CX)
    def _(i):
        pltpu.make_async_copy(column(ens_any, i), column(ens, i), load_sem.at[i]).start()

    partners = [(s, 0) for s in STAT_STEPS] + [(0, s) for s in STAT_STEPS]
    partners += [(a, b) for a in (-1, 1) for b in (-1, 1)]
    barrier = pltpu.get_barrier_semaphore()
    for a, b in partners:
        pl.semaphore_signal(barrier, inc=1, device_id=at(a, b), device_id_type=MESH)

    for copy in small:
        copy.wait()
    count = count_ref[gx, gy]
    cells = cells_ref[...].astype(F32)
    slot = lax.broadcasted_iota(jnp.int32, (1, OBS), 1)
    rows[0:1] = jnp.where(slot < count, given[1], 0.0)
    rows[1:2] = given[0]
    east = jnp.floor((cells + 0.5) * (1.0 / XROWS))
    north = jnp.floor((cells - XROWS * east + 0.5) * (1.0 / LEV))
    hat_x, hat_y = hats((east + 0.5) / CX), hats((north + 0.5) / CY)
    for slot in range(9):
        rows[3 + slot : 4 + slot] = hat_x[slot // 3] * hat_y[slot % 3]

    @pl.loop(0, CX)
    def _(i):
        pltpu.make_async_copy(column(ens_any, i), column(ens, i), load_sem.at[i]).wait()
        start = pl.multiple_of(i * XROWS, XROWS)
        ens32[pl.ds(start, XROWS)] = ens[pl.ds(start, XROWS)].astype(F32)

    @pl.loop(0, OBS // GATHER)
    def _(g):
        for r in range(GATHER):
            o = g * GATHER + r
            picked[pl.ds(o, 1)] = ens32[pl.ds(cell_ref[0, o], 1)]

    def accumulate(total, lanes, deviation, centre):
        scale, value = rows[0:1, lanes], rows[1:2, lanes]
        anomaly = (scale * deviation).astype(BF16)
        innovation = jnp.broadcast_to(scale * (value - centre), (16, QUART)).astype(BF16)
        return total + mm_nt(jnp.concatenate([anomaly, innovation], axis=0), anomaly)

    def exchange(t, sent, got, send_sem, recv_sem, shift):
        copies = []
        for k, step in enumerate(STAT_STEPS):
            there = STAT_STEPS.index(-step)
            copies.append(
                pltpu.make_async_remote_copy(
                    src_ref=sent.at[t],
                    dst_ref=got.at[t, there],
                    send_sem=send_sem.at[t, k],
                    recv_sem=recv_sem.at[t, there],
                    device_id=at(*shift(step)),
                    device_id_type=MESH,
                )
            )
        return copies

    pending = []

    def settle():
        while pending:
            pending.pop().wait_send()

    def weighted(t, total, got, copies):
        for k in reversed(range(4)):
            copies[STAT_STEPS.index(-STAT_STEPS[k])].wait_recv()
            total = total + STAT_WEIGHTS[k] * got[t, k].astype(F32)
        pending.extend(copies)
        return total

    def apply_some(first, last):
        apply_columns(first, last, lambda slot: matrices[slot * K : (slot + 1) * K], stationary, ens, applied)

    for t in range(ITERS):
        total = jnp.zeros((K + 16, K), F32)
        if t == 0:
            row, col = iotas((K + 16, K))
            centre_rows = jnp.where(row == col, (K - 1.0) / K, jnp.where(row < K, -1.0 / K, 1.0 / K))
            centre_rows = centre_rows.astype(BF16)
            for q in range(OBS // QUART):
                lanes = slice(q * QUART, (q + 1) * QUART)
                moved = mm_nt(centre_rows, picked[lanes].astype(BF16))
                total = accumulate(total, lanes, moved[:K], moved[K : K + 1])
                deviations[:, lanes] = moved[:K]
                rows[2:3, lanes] = moved[K : K + 1]
        else:
            for q in range(OBS // QUART):
                lanes = slice(q * QUART, (q + 1) * QUART)
                fresh = rows[2:3, lanes] + mm(transforms[...], scaled[:, lanes])
                fresh = fresh.astype(BF16).astype(F32)
                centre = jnp.sum(fresh, axis=0, keepdims=True) * (1.0 / K)
                total = accumulate(total, lanes, fresh - centre, centre)
        own = opened(total[:K], total[K : K + 1])
        stat_x[t] = closed(own)

        if t == 0:
            pl.semaphore_wait(barrier, len(partners))
        copies = exchange(t, stat_x, got_x, send_x, recv_x, lambda step: (step, 0))
        for copy in copies:
            copy.start()
        if t == 1:
            for slot in range(9):
                matrices[slot * K : (slot + 1) * K] = full_matrices(transforms[:, slot * K : (slot + 1) * K])
            apply_some(0, CX // 2)
            settle()
        own = weighted(t, own, got_x, copies)
        stat_y[t] = closed(own)
        copies = exchange(t, stat_y, got_y, send_y, recv_y, lambda step: (0, step))
        for copy in reversed(copies):
            copy.start()
        if t == 1:
            apply_some(CX // 2, CX)
        spread, weights = transform_parts(weighted(t, own, got_y, copies))
        own_ref[t] = closed(opened(spread, weights))
        landing = nearby if t == 0 else blend_ref
        copies = {}
        for k, (a, b) in enumerate(BLEND_STEPS):
            there = slot_of(-a, -b)
            copies[(-a, -b)] = pltpu.make_async_remote_copy(
                src_ref=own_ref.at[t],
                dst_ref=landing.at[there],
                send_sem=send_t.at[t, k],
                recv_sem=recv_t.at[t, there],
                device_id=at(a, b),
                device_id_type=MESH,
            )
        for copy in copies.values():
            copy.start()
        own = slot_of(0, 0)
        if t == 0:
            transforms[:, own * K : (own + 1) * K] = (weights + spread).astype(BF16)

            @pl.loop(0, OBS // PART)
            def _(q):
                lanes = pl.ds(pl.multiple_of(q * PART, PART), PART)
                for slot in range(9):
                    part = rows[3 + slot : 4 + slot, lanes] * deviations[:, lanes]
                    scaled[slot * K : (slot + 1) * K, lanes] = part.astype(BF16)

        else:
            mine = pltpu.make_async_copy(own_ref.at[t], landing.at[own], own_sem)
            mine.start()
            settle()
        near, far = BLEND_STEPS[6:], BLEND_STEPS[:6]
        for step in near:
            copies[step].wait_recv()
        if t == 1:
            mine.wait()
            middle_ref[K : 2 * K] = full_matrices((weights + spread).astype(BF16))
        for step in near:
            slot = slot_of(*step)
            if t == 0:
                transforms[:, slot * K : (slot + 1) * K] = unpack_transform(nearby[slot])
            else:
                here = (step[1] + 1) * K
                middle_ref[here : here + K] = full_matrices(unpack_transform(blend_ref[slot]))
        for step in far:
            copies[step].wait_recv()
        if t == 0:
            for step in far:
                slot = slot_of(*step)
                transforms[:, slot * K : (slot + 1) * K] = unpack_transform(nearby[slot])
        pending.extend(copies.values())
    settle()


def last_kernel(nearby, middle, ens, out_any, applied, matrices, stationary, store_sem):
    def ready(slots):
        for slot in slots:
            matrices[slot * K : (slot + 1) * K] = full_matrices(unpack_transform(nearby[slot]))

    def store(i):
        return pltpu.make_async_copy(column(applied, i), column(out_any, i), store_sem.at[i])

    def matrix_of(slot):
        if 3 <= slot < 6:
            return middle[(slot - 3) * K : (slot - 2) * K]
        return matrices[slot * K : (slot + 1) * K]

    ready(range(3))
    blend_column(0, 0, matrix_of, stationary)
    for i in range(CX):
        apply_column(i, i % SLOTS, ens, applied, stationary)
        if i + 1 < CX:
            blend_column(i + 1, (i + 1) % SLOTS, matrix_of, stationary)
        store(i).start()
        if i == 1:
            ready(range(6, 9))

    for i in range(CX):
        store(i).wait()


def shards(ensemble, obs_cell, obs_value, obs_weight, obs_count):
    flat = ensemble.reshape(ROWS, K)
    anywhere = pl.BlockSpec(memory_space=pl.ANY)
    fixed = pl.BlockSpec(memory_space=pltpu.HBM)
    dma = pltpu.SemaphoreType.DMA
    following, blend, middle = pl.pallas_call(
        first_kernel,
        out_shape=(
            jax.ShapeDtypeStruct((ROWS, K), BF16),
            jax.ShapeDtypeStruct((9, PACKED, K), BF16),
            jax.ShapeDtypeStruct((3 * K, K), F32),
        ),
        in_specs=[fixed] * 5,
        out_specs=(pl.BlockSpec(memory_space=pltpu.VMEM),) * 3,
        scratch_shapes=[
            pltpu.SMEM((BX, BY), jnp.int32),
            pltpu.SMEM((1, OBS), jnp.int32),
            pltpu.VMEM((2, 1, OBS), F32),
            pltpu.VMEM((1, OBS), jnp.int32),
            pltpu.VMEM((ROWS, K), BF16),
            pltpu.VMEM((ROWS, K), F32),
            pltpu.VMEM((OBS, K), F32),
            pltpu.VMEM((16, OBS), F32),
            pltpu.VMEM((K, OBS), F32),
            pltpu.VMEM((9 * K, OBS), BF16),
            pltpu.VMEM((9 * K, K), F32),
            pltpu.VMEM((2, 3 * K, 2 * K), BF16),
            pltpu.VMEM((ITERS, PACKED, K), BF16),
            pltpu.VMEM((ITERS, PACKED, K), BF16),
            pltpu.VMEM((ITERS, 4, PACKED, K), BF16),
            pltpu.VMEM((ITERS, 4, PACKED, K), BF16),
            pltpu.VMEM((9, PACKED, K), BF16),
            pltpu.VMEM((K, 9 * K), BF16),
            pltpu.VMEM((ITERS, PACKED, K), BF16),
            dma((5,)),
            dma((CX,)),
            dma(()),
            dma((ITERS, 4)),
            dma((ITERS, 4)),
            dma((ITERS, 4)),
            dma((ITERS, 4)),
            dma((ITERS, 8)),
            dma((ITERS, 9)),
        ],
        compiler_params=pltpu.CompilerParams(
            collective_id=0, has_side_effects=True, vmem_limit_bytes=44 * 1024 * 1024
        ),
        name="analyse",
    )(
        *(
            pltpu.with_memory_space_constraint(array, pltpu.HBM)
            for array in (
                obs_count,
                obs_cell.reshape(1, OBS),
                obs_value.reshape(1, OBS),
                obs_weight.reshape(1, OBS),
                flat,
            )
        )
    )
    out = pl.pallas_call(
        last_kernel,
        out_shape=jax.ShapeDtypeStruct((ROWS, K), BF16),
        in_specs=[pl.BlockSpec(memory_space=pltpu.VMEM)] * 3,
        out_specs=fixed,
        scratch_shapes=[
            pltpu.VMEM((ROWS, K), BF16),
            pltpu.VMEM((9 * K, K), F32),
            pltpu.VMEM((SLOTS, 3 * K, 2 * K), BF16),
            dma((CX,)),
        ],
        compiler_params=pltpu.CompilerParams(vmem_limit_bytes=44 * 1024 * 1024),
        name="blend",
    )(blend, middle, following)
    return out.reshape(ensemble.shape)


def solution(mesh):
    placed = (
        P("gx", "gy", None, None),
        P("gx", "gy", None),
        P("gx", "gy", None),
        P("gx", "gy", None),
        P(),
    )
    return jax.shard_map(
        shards, mesh=mesh, in_specs=placed, out_specs=P("gx", "gy", None, None), check_vma=False
    )
```

```python
import jax
import jax.numpy as jnp
from jax import lax
from jax.experimental import pallas as pl
from jax.experimental.pallas import tpu as pltpu
from jax.sharding import PartitionSpec as P

K = 128
CX = 16
CY = 32
LEV = 48
ROWS = CX * CY * LEV
XROWS = CY * LEV
OBS = 2048
NEWTON = 6
ITERS = 2
QUART = 1024
PART = 256
GROUP = 8
UNROLL = 4
SLOTS = 4
GATHER = 128
PACKED = 80
BX = 8
BY = 16

MESH = pl.DeviceIdType.MESH
F32 = jnp.float32
BF16 = jnp.bfloat16
STAT_STEPS = (-1, 1, -2, 2)
STAT_WEIGHTS = (0.75, 0.75, 0.5, 0.5)
BLEND_STEPS = tuple((a, b) for a in (-1, 1, 0) for b in (-1, 1, 0) if (a, b) != (0, 0))


def slot_of(a, b):
    return (a + 1) * 3 + (b + 1)


def place_of(slot):
    return (3, 4, 5, 0, 1, 2, 6, 7, 8)[slot]


def lanes_of(slot):
    return slice(place_of(slot) * K, place_of(slot) * K + K)


def mm(a, b):
    return jnp.dot(a, b, preferred_element_type=F32)


def mm_nt(a, b):
    return lax.dot_general(a, b, (((1,), (1,)), ((), ())), preferred_element_type=F32)


def split(x):
    high = x.astype(BF16)
    low = (x - high.astype(F32)).astype(BF16)
    return high, low


def wide(x):
    high, low = split(x)
    return jnp.concatenate([high, low], axis=1)


def times(a, b):
    both = wide(b)
    out = mm(wide(a), jnp.concatenate([both, both], axis=0))
    return out[:, :K] + out[:, K:]


def times_late(a, b):
    a_high, a_low = split(a)
    b_high, b_low = split(b)
    left = jnp.concatenate([a_high, a_low, a_high], axis=1)
    return mm(left, jnp.concatenate([b_high, b_high, b_low], axis=0))


def iotas(shape):
    return lax.broadcasted_iota(jnp.int32, shape, 0), lax.broadcasted_iota(jnp.int32, shape, 1)


def centring():
    row, col = iotas((K, K))
    return jnp.where(row == col, (K - 1.0) / K, -1.0 / K).astype(BF16)


def fold(matrix):
    half = K // 2
    row, lane = iotas((half, K))
    return jnp.where(lane < row, pltpu.roll(matrix[half:], half, 1), matrix[:half])


def unfold(body, diagonal):
    half = K // 2
    row, lane = iotas((half, K))
    flipped = jnp.concatenate([body, jnp.zeros((half, K), F32)], axis=0).T
    top = jnp.where(lane < row, flipped[:half], body)
    lower = jnp.where(lane < row, body, flipped[:half])
    bottom = jnp.where(lane < half, flipped[half:], pltpu.roll(lower, half, 1))
    row, col = iotas((K, K))
    return jnp.where(row == col, diagonal, jnp.concatenate([top, bottom], axis=0))


def diagonal_of(matrix):
    row, col = iotas((K, K))
    return jnp.sum(jnp.where(row == col, matrix, 0.0), axis=0, keepdims=True)


def opened(symmetric, line):
    tail_row, _ = iotas((PACKED - K // 2, K))
    tail = jnp.where(tail_row == 0, diagonal_of(symmetric), jnp.where(tail_row == 2, line, 0.0))
    return jnp.concatenate([fold(symmetric), tail], axis=0)


def lines_of(packed):
    half = K // 2
    diagonal = packed[half : half + 1] + packed[half + 1 : half + 2]
    return diagonal, packed[half + 2 : half + 3] + packed[half + 3 : half + 4]


def closed(packed):
    tail_row, _ = iotas((PACKED - K // 2, K))
    tail = jnp.zeros((PACKED - K // 2, K), F32)
    for k, line in enumerate(lines_of(packed)):
        high, low = split(line)
        tail = jnp.where(tail_row == 2 * k, high.astype(F32), tail)
        tail = jnp.where(tail_row == 2 * k + 1, low.astype(F32), tail)
    return jnp.concatenate([packed[: K // 2], tail], axis=0).astype(BF16)


def unpack(packed):
    diagonal, line = lines_of(packed)
    return unfold(packed[: K // 2], diagonal), line


def unpack_transform(packed):
    spread, weights = unpack(packed.astype(F32))
    return (weights + spread).astype(BF16)


def transform_parts(packed):
    gram, projected = unpack(packed)
    row, col = iotas((K, K))
    identity = jnp.where(row == col, 1.0, 0.0).astype(F32)
    system = gram + (K - 1) * identity
    squares = jnp.sum(system * system, axis=0, keepdims=True)
    frobenius = jnp.sqrt(jnp.sum(squares, axis=1, keepdims=True))
    root = system / frobenius
    correction = 1.5 * identity - 0.5 * root
    root, inverse = times(correction, root), correction
    for step in range(1, NEWTON - 1):
        correction = 1.5 * identity - 0.5 * times_late(inverse, root)
        root, inverse = times(correction, root), times(correction, inverse)
    correction = 1.5 * identity - 0.5 * times_late(inverse, root)
    carried = times(jnp.broadcast_to(projected, (16, K)), inverse)
    carried, inverse = times_late(carried, correction), times(correction, inverse)
    weights = times_late(carried, inverse)[0:1] / frobenius
    return jnp.sqrt((K - 1) / frobenius) * inverse, weights


def hats(position):
    below = jnp.maximum(0.0, 0.5 - position)
    above = jnp.maximum(0.0, position - 0.5)
    return below, 1.0 - below - above, above


def hat_of(j, count):
    position = (j + 0.5) / count
    below, above = max(0.0, 0.5 - position), max(0.0, position - 0.5)
    return below, 1.0 - below - above, above


def blend_column(i, slot, matrix_of, stationary):
    static = isinstance(i, int)
    weights = hat_of(i, CX) if static else hats((i.astype(F32) + 0.5) / CX)
    for b in range(3):
        blend = None
        for a in range(3):
            if static and weights[a] == 0.0:
                continue
            term = weights[a] * matrix_of(a * 3 + b)
            blend = term if blend is None else blend + term
        stationary[slot, b * K : (b + 1) * K] = wide(blend)


def row_of(i, offset=0):
    row = i * XROWS + offset
    return row if isinstance(i, int) else pl.multiple_of(row, 16)


def apply_column(i, slot, ens, fresh, stationary):
    for half in range(2):
        matrix = stationary[slot, half * K : half * K + 2 * K]
        for group in range(CY // 2 // GROUP):
            first = half * (CY // 2) + group * GROUP
            here = pl.ds(row_of(i, first * LEV), GROUP * LEV)
            block = ens[here]
            out = mm_nt(jnp.concatenate([block, block], axis=1), matrix)
            parts = []
            for j in range(GROUP):
                hat = hat_of(first + j, CY)
                piece = out[j * LEV : (j + 1) * LEV]
                parts.append(hat[half] * piece[:, :K] + hat[half + 1] * piece[:, K:])
            fresh[here] = jnp.concatenate(parts, axis=0).astype(BF16)


def apply_columns(first, last, matrix_of, stationary, ens, fresh):
    blend_column(jnp.int32(first), 0, matrix_of, stationary)

    @pl.loop(first // UNROLL, last // UNROLL)
    def _(step):
        for k in range(UNROLL):
            i = step * UNROLL + k
            apply_column(i, k % 2, ens, fresh, stationary)
            blend_column(jnp.minimum(i + 1, CX - 1), 1 - k % 2, matrix_of, stationary)


def full_matrices(transforms):
    return mm(transforms, centring()) + 1.0 / K


def column(ref, i):
    return ref.at[pl.ds(row_of(i), XROWS)]


def first_kernel(
    count_any, cell_any, value_any, weight_any, ens_any,
    applied, blend_ref, middle_ref,
    count_ref, cell_ref, given, cells_ref, ens, ens32, picked, rows, deviations, scaled, matrices, stationary,
    stat_x, stat_y, got_x, got_y, nearby, transforms, own_ref,
    small_sem, load_sem, send_x, recv_x, send_y, recv_y, send_t, recv_t,
):
    gx, gy = lax.axis_index("gx"), lax.axis_index("gy")
    nx, ny = lax.axis_size("gx"), lax.axis_size("gy")

    def at(a, b):
        return (lax.rem(gx + a + nx, nx), lax.rem(gy + b + ny, ny))

    small = [
        pltpu.make_async_copy(count_any, count_ref, small_sem.at[0]),
        pltpu.make_async_copy(cell_any, cell_ref, small_sem.at[1]),
        pltpu.make_async_copy(cell_any, cells_ref, small_sem.at[2]),
        pltpu.make_async_copy(value_any, given.at[0], small_sem.at[3]),
        pltpu.make_async_copy(weight_any, given.at[1], small_sem.at[4]),
    ]
    for copy in small:
        copy.start()

    @pl.loop(0, CX)
    def _(i):
        pltpu.make_async_copy(column(ens_any, i), column(ens, i), load_sem.at[i]).start()

    partners = [(s, 0) for s in STAT_STEPS] + [(0, s) for s in STAT_STEPS]
    partners += [(a, b) for a in (-1, 1) for b in (-1, 1)]
    barrier = pltpu.get_barrier_semaphore()
    for a, b in partners:
        pl.semaphore_signal(barrier, inc=1, device_id=at(a, b), device_id_type=MESH)

    for copy in small:
        copy.wait()
    count = count_ref[gx, gy]
    cells = cells_ref[...].astype(F32)
    slot = lax.broadcasted_iota(jnp.int32, (1, OBS), 1)
    rows[0:1] = jnp.where(slot < count, given[1], 0.0)
    rows[1:2] = given[0]
    east = jnp.floor((cells + 0.5) * (1.0 / XROWS))
    north = jnp.floor((cells - XROWS * east + 0.5) * (1.0 / LEV))
    hat_x, hat_y = hats((east + 0.5) / CX), hats((north + 0.5) / CY)
    for slot in range(9):
        rows[3 + slot : 4 + slot] = hat_x[slot // 3] * hat_y[slot % 3]

    @pl.loop(0, CX)
    def _(i):
        pltpu.make_async_copy(column(ens_any, i), column(ens, i), load_sem.at[i]).wait()
        start = pl.multiple_of(i * XROWS, XROWS)
        ens32[pl.ds(start, XROWS)] = ens[pl.ds(start, XROWS)].astype(F32)

    @pl.loop(0, OBS // GATHER)
    def _(g):
        for r in range(GATHER):
            o = g * GATHER + r
            picked[pl.ds(o, 1)] = ens32[pl.ds(cell_ref[0, o], 1)]

    def accumulate(total, lanes, deviation, centre):
        scale, value = rows[0:1, lanes], rows[1:2, lanes]
        anomaly = (scale * deviation).astype(BF16)
        innovation = jnp.broadcast_to(scale * (value - centre), (16, QUART)).astype(BF16)
        return total + mm_nt(jnp.concatenate([anomaly, innovation], axis=0), anomaly)

    def exchange(t, sent, got, send_sem, recv_sem, shift):
        copies = []
        for k, step in enumerate(STAT_STEPS):
            there = STAT_STEPS.index(-step)
            copies.append(
                pltpu.make_async_remote_copy(
                    src_ref=sent.at[t],
                    dst_ref=got.at[t, there],
                    send_sem=send_sem.at[t, k],
                    recv_sem=recv_sem.at[t, there],
                    device_id=at(*shift(step)),
                    device_id_type=MESH,
                )
            )
        return copies

    pending = []

    def settle():
        while pending:
            pending.pop().wait_send()

    def weighted(t, total, got, copies):
        for k in reversed(range(4)):
            copies[STAT_STEPS.index(-STAT_STEPS[k])].wait_recv()
            total = total + STAT_WEIGHTS[k] * got[t, k].astype(F32)
        pending.extend(copies)
        return total

    def apply_some(first, last):
        apply_columns(first, last, lambda slot: matrices[slot * K : (slot + 1) * K], stationary, ens, applied)

    for t in range(ITERS):
        total = jnp.zeros((K + 16, K), F32)
        if t == 0:
            row, col = iotas((K + 16, K))
            centre_rows = jnp.where(row == col, (K - 1.0) / K, jnp.where(row < K, -1.0 / K, 1.0 / K))
            centre_rows = centre_rows.astype(BF16)
            for q in range(OBS // QUART):
                lanes = slice(q * QUART, (q + 1) * QUART)
                moved = mm_nt(centre_rows, picked[lanes].astype(BF16))
                total = accumulate(total, lanes, moved[:K], moved[K : K + 1])
                deviations[:, lanes] = moved[:K]
                rows[2:3, lanes] = moved[K : K + 1]
        else:
            for q in range(OBS // QUART):
                lanes = slice(q * QUART, (q + 1) * QUART)
                fresh = deviations[:, lanes] + mm(transforms[:, 3 * K :], scaled[3 * K :, lanes])
                fresh = fresh.astype(BF16).astype(F32)
                centre = jnp.sum(fresh, axis=0, keepdims=True) * (1.0 / K)
                total = accumulate(total, lanes, fresh - centre, centre)
        own = opened(total[:K], total[K : K + 1])
        stat_x[t] = closed(own)

        if t == 0:
            pl.semaphore_wait(barrier, len(partners))
        copies = exchange(t, stat_x, got_x, send_x, recv_x, lambda step: (step, 0))
        for copy in copies:
            copy.start()
        if t == 1:
            for slot in range(9):
                matrices[slot * K : (slot + 1) * K] = full_matrices(transforms[:, lanes_of(slot)])
            apply_some(0, CX // 2)
            settle()
        own = weighted(t, own, got_x, copies)
        stat_y[t] = closed(own)
        copies = exchange(t, stat_y, got_y, send_y, recv_y, lambda step: (0, step))
        for copy in reversed(copies):
            copy.start()
        if t == 1:
            apply_some(CX // 2, CX)
        spread, weights = transform_parts(weighted(t, own, got_y, copies))
        own_ref[t] = closed(opened(spread, weights))
        landing = nearby if t == 0 else blend_ref
        copies = {}
        for k, (a, b) in enumerate(BLEND_STEPS):
            there = slot_of(-a, -b)
            copies[(-a, -b)] = pltpu.make_async_remote_copy(
                src_ref=own_ref.at[t],
                dst_ref=landing.at[there],
                send_sem=send_t.at[t, k],
                recv_sem=recv_t.at[t, there],
                device_id=at(a, b),
                device_id_type=MESH,
            )
        for copy in copies.values():
            copy.start()
        own = slot_of(0, 0)
        if t == 0:
            transforms[:, lanes_of(own)] = (weights + spread).astype(BF16)

            @pl.loop(0, OBS // PART)
            def _(q):
                lanes = pl.ds(pl.multiple_of(q * PART, PART), PART)
                for slot in range(9):
                    part = rows[3 + slot : 4 + slot, lanes] * deviations[:, lanes]
                    scaled[lanes_of(slot), lanes] = part.astype(BF16)

        else:
            settle()
            middle_ref[K : 2 * K] = full_matrices((weights + spread).astype(BF16))
        near, far = BLEND_STEPS[6:], BLEND_STEPS[:6]
        for step in near:
            copies[step].wait_recv()
        for step in near:
            slot = slot_of(*step)
            if t == 0:
                transforms[:, lanes_of(slot)] = unpack_transform(nearby[slot])
            else:
                here = (step[1] + 1) * K
                middle_ref[here : here + K] = full_matrices(unpack_transform(blend_ref[slot]))
        if t == 0:
            for q in range(OBS // QUART):
                lanes = slice(q * QUART, (q + 1) * QUART)
                part = mm(transforms[:, : 3 * K], scaled[: 3 * K, lanes])
                deviations[:, lanes] = rows[2:3, lanes] + part
        for step in far:
            copies[step].wait_recv()
        if t == 0:
            for step in far:
                slot = slot_of(*step)
                transforms[:, lanes_of(slot)] = unpack_transform(nearby[slot])
        pending.extend(copies.values())
    settle()


def last_kernel(nearby, middle, ens, out_any, applied, matrices, stationary, store_sem):
    def ready(slots):
        for slot in slots:
            matrices[slot * K : (slot + 1) * K] = full_matrices(unpack_transform(nearby[slot]))

    def store(i):
        return pltpu.make_async_copy(column(applied, i), column(out_any, i), store_sem.at[i])

    def matrix_of(slot):
        if 3 <= slot < 6:
            return middle[(slot - 3) * K : (slot - 2) * K]
        return matrices[slot * K : (slot + 1) * K]

    ready(range(3))
    blend_column(0, 0, matrix_of, stationary)
    for i in range(CX):
        apply_column(i, i % SLOTS, ens, applied, stationary)
        if i + 1 < CX:
            blend_column(i + 1, (i + 1) % SLOTS, matrix_of, stationary)
        store(i).start()
        if i == 1:
            ready(range(6, 9))

    for i in range(CX):
        store(i).wait()


def shards(ensemble, obs_cell, obs_value, obs_weight, obs_count):
    flat = ensemble.reshape(ROWS, K)
    anywhere = pl.BlockSpec(memory_space=pl.ANY)
    fixed = pl.BlockSpec(memory_space=pltpu.HBM)
    dma = pltpu.SemaphoreType.DMA
    following, blend, middle = pl.pallas_call(
        first_kernel,
        out_shape=(
            jax.ShapeDtypeStruct((ROWS, K), BF16),
            jax.ShapeDtypeStruct((9, PACKED, K), BF16),
            jax.ShapeDtypeStruct((3 * K, K), F32),
        ),
        in_specs=[fixed] * 5,
        out_specs=(pl.BlockSpec(memory_space=pltpu.VMEM),) * 3,
        scratch_shapes=[
            pltpu.SMEM((BX, BY), jnp.int32),
            pltpu.SMEM((1, OBS), jnp.int32),
            pltpu.VMEM((2, 1, OBS), F32),
            pltpu.VMEM((1, OBS), jnp.int32),
            pltpu.VMEM((ROWS, K), BF16),
            pltpu.VMEM((ROWS, K), F32),
            pltpu.VMEM((OBS, K), F32),
            pltpu.VMEM((16, OBS), F32),
            pltpu.VMEM((K, OBS), F32),
            pltpu.VMEM((9 * K, OBS), BF16),
            pltpu.VMEM((9 * K, K), F32),
            pltpu.VMEM((2, 3 * K, 2 * K), BF16),
            pltpu.VMEM((ITERS, PACKED, K), BF16),
            pltpu.VMEM((ITERS, PACKED, K), BF16),
            pltpu.VMEM((ITERS, 4, PACKED, K), BF16),
            pltpu.VMEM((ITERS, 4, PACKED, K), BF16),
            pltpu.VMEM((9, PACKED, K), BF16),
            pltpu.VMEM((K, 9 * K), BF16),
            pltpu.VMEM((ITERS, PACKED, K), BF16),
            dma((5,)),
            dma((CX,)),
            dma((ITERS, 4)),
            dma((ITERS, 4)),
            dma((ITERS, 4)),
            dma((ITERS, 4)),
            dma((ITERS, 8)),
            dma((ITERS, 9)),
        ],
        compiler_params=pltpu.CompilerParams(
            collective_id=0, has_side_effects=True, vmem_limit_bytes=44 * 1024 * 1024
        ),
        name="analyse",
    )(
        *(
            pltpu.with_memory_space_constraint(array, pltpu.HBM)
            for array in (
                obs_count,
                obs_cell.reshape(1, OBS),
                obs_value.reshape(1, OBS),
                obs_weight.reshape(1, OBS),
                flat,
            )
        )
    )
    out = pl.pallas_call(
        last_kernel,
        out_shape=jax.ShapeDtypeStruct((ROWS, K), BF16),
        in_specs=[pl.BlockSpec(memory_space=pltpu.VMEM)] * 3,
        out_specs=fixed,
        scratch_shapes=[
            pltpu.VMEM((ROWS, K), BF16),
            pltpu.VMEM((9 * K, K), F32),
            pltpu.VMEM((SLOTS, 3 * K, 2 * K), BF16),
            dma((CX,)),
        ],
        compiler_params=pltpu.CompilerParams(vmem_limit_bytes=44 * 1024 * 1024),
        name="blend",
    )(blend, middle, following)
    return out.reshape(ensemble.shape)


def solution(mesh):
    placed = (
        P("gx", "gy", None, None),
        P("gx", "gy", None),
        P("gx", "gy", None),
        P("gx", "gy", None),
        P(),
    )
    return jax.shard_map(
        shards, mesh=mesh, in_specs=placed, out_specs=P("gx", "gy", None, None), check_vma=False
    )
```

```python
import jax
import jax.numpy as jnp
from jax import lax
from jax.experimental import pallas as pl
from jax.experimental.pallas import tpu as pltpu
from jax.sharding import PartitionSpec as P

K = 128
CX = 16
CY = 32
LEV = 48
ROWS = CX * CY * LEV
XROWS = CY * LEV
OBS = 2048
NEWTON = 6
ITERS = 2
QUART = 1024
PART = 256
GROUP = 8
UNROLL = 4
SLOTS = 4
GATHER = 128
PACKED = 80
BX = 8
BY = 16

MESH = pl.DeviceIdType.MESH
F32 = jnp.float32
BF16 = jnp.bfloat16
STAT_STEPS = (-1, 1, -2, 2)
STAT_WEIGHTS = (0.75, 0.75, 0.5, 0.5)
BLEND_STEPS = tuple((a, b) for a in (-1, 1, 0) for b in (-1, 1, 0) if (a, b) != (0, 0))


def slot_of(a, b):
    return (a + 1) * 3 + (b + 1)


def place_of(slot):
    return (3, 4, 5, 0, 1, 2, 6, 7, 8)[slot]


def lanes_of(slot):
    return slice(place_of(slot) * K, place_of(slot) * K + K)


def mm(a, b):
    return jnp.dot(a, b, preferred_element_type=F32)


def mm_nt(a, b):
    return lax.dot_general(a, b, (((1,), (1,)), ((), ())), preferred_element_type=F32)


def split(x):
    high = x.astype(BF16)
    low = (x - high.astype(F32)).astype(BF16)
    return high, low


def wide(x):
    high, low = split(x)
    return jnp.concatenate([high, low], axis=1)


def times(a, b):
    both = wide(b)
    out = mm(wide(a), jnp.concatenate([both, both], axis=0))
    return out[:, :K] + out[:, K:]


def times_late(a, b):
    a_high, a_low = split(a)
    b_high, b_low = split(b)
    left = jnp.concatenate([a_high, a_low, a_high], axis=1)
    return mm(left, jnp.concatenate([b_high, b_high, b_low], axis=0))


def iotas(shape):
    return lax.broadcasted_iota(jnp.int32, shape, 0), lax.broadcasted_iota(jnp.int32, shape, 1)


def centring():
    row, col = iotas((K, K))
    return jnp.where(row == col, (K - 1.0) / K, -1.0 / K).astype(BF16)


def fold(matrix):
    half = K // 2
    row, lane = iotas((half, K))
    return jnp.where(lane < row, pltpu.roll(matrix[half:], half, 1), matrix[:half])


def unfold(body, diagonal):
    half = K // 2
    row, lane = iotas((half, K))
    flipped = jnp.concatenate([body, jnp.zeros((half, K), F32)], axis=0).T
    top = jnp.where(lane < row, flipped[:half], body)
    lower = jnp.where(lane < row, body, flipped[:half])
    bottom = jnp.where(lane < half, flipped[half:], pltpu.roll(lower, half, 1))
    row, col = iotas((K, K))
    return jnp.where(row == col, diagonal, jnp.concatenate([top, bottom], axis=0))


def diagonal_of(matrix):
    row, col = iotas((K, K))
    return jnp.sum(jnp.where(row == col, matrix, 0.0), axis=0, keepdims=True)


def opened(symmetric, line):
    tail_row, _ = iotas((PACKED - K // 2, K))
    tail = jnp.where(tail_row == 0, diagonal_of(symmetric), jnp.where(tail_row == 2, line, 0.0))
    return jnp.concatenate([fold(symmetric), tail], axis=0)


def lines_of(packed):
    half = K // 2
    diagonal = packed[half : half + 1] + packed[half + 1 : half + 2]
    return diagonal, packed[half + 2 : half + 3] + packed[half + 3 : half + 4]


def closed(packed):
    tail_row, _ = iotas((PACKED - K // 2, K))
    tail = jnp.zeros((PACKED - K // 2, K), F32)
    for k, line in enumerate(lines_of(packed)):
        high, low = split(line)
        tail = jnp.where(tail_row == 2 * k, high.astype(F32), tail)
        tail = jnp.where(tail_row == 2 * k + 1, low.astype(F32), tail)
    return jnp.concatenate([packed[: K // 2], tail], axis=0).astype(BF16)


def unpack(packed):
    diagonal, line = lines_of(packed)
    return unfold(packed[: K // 2], diagonal), line


def unpack_transform(packed):
    spread, weights = unpack(packed.astype(F32))
    return (weights + spread).astype(BF16)


def transform_parts(packed):
    gram, projected = unpack(packed)
    row, col = iotas((K, K))
    identity = jnp.where(row == col, 1.0, 0.0).astype(F32)
    system = gram + (K - 1) * identity
    squares = jnp.sum(system * system, axis=0, keepdims=True)
    frobenius = jnp.sqrt(jnp.sum(squares, axis=1, keepdims=True))
    root = system / frobenius
    correction = 1.5 * identity - 0.5 * root
    root, inverse = times(correction, root), correction
    for step in range(1, NEWTON - 1):
        correction = 1.5 * identity - 0.5 * times_late(inverse, root)
        root, inverse = times(correction, root), times(correction, inverse)
    correction = 1.5 * identity - 0.5 * times_late(inverse, root)
    carried = times(jnp.broadcast_to(projected, (16, K)), inverse)
    carried, inverse = times_late(carried, correction), times(correction, inverse)
    weights = times_late(carried, inverse)[0:1] / frobenius
    return jnp.sqrt((K - 1) / frobenius) * inverse, weights


def hats(position):
    below = jnp.maximum(0.0, 0.5 - position)
    above = jnp.maximum(0.0, position - 0.5)
    return below, 1.0 - below - above, above


def hat_of(j, count):
    position = (j + 0.5) / count
    below, above = max(0.0, 0.5 - position), max(0.0, position - 0.5)
    return below, 1.0 - below - above, above


def blend_column(i, slot, matrix_of, stationary):
    static = isinstance(i, int)
    weights = hat_of(i, CX) if static else hats((i.astype(F32) + 0.5) / CX)
    for b in range(3):
        blend = None
        for a in range(3):
            if static and weights[a] == 0.0:
                continue
            term = weights[a] * matrix_of(a * 3 + b)
            blend = term if blend is None else blend + term
        stationary[slot, b * K : (b + 1) * K] = wide(blend)


def row_of(i, offset=0):
    row = i * XROWS + offset
    return row if isinstance(i, int) else pl.multiple_of(row, 16)


def apply_column(i, slot, ens, fresh, stationary):
    for half in range(2):
        matrix = stationary[slot, half * K : half * K + 2 * K]
        for group in range(CY // 2 // GROUP):
            first = half * (CY // 2) + group * GROUP
            here = pl.ds(row_of(i, first * LEV), GROUP * LEV)
            block = ens[here]
            out = mm_nt(jnp.concatenate([block, block], axis=1), matrix)
            parts = []
            for j in range(GROUP):
                hat = hat_of(first + j, CY)
                piece = out[j * LEV : (j + 1) * LEV]
                parts.append(hat[half] * piece[:, :K] + hat[half + 1] * piece[:, K:])
            fresh[here] = jnp.concatenate(parts, axis=0).astype(BF16)


def apply_columns(first, last, matrix_of, stationary, ens, fresh):
    blend_column(jnp.int32(first), 0, matrix_of, stationary)

    @pl.loop(first // UNROLL, last // UNROLL)
    def _(step):
        for k in range(UNROLL):
            i = step * UNROLL + k
            apply_column(i, k % 2, ens, fresh, stationary)
            blend_column(jnp.minimum(i + 1, CX - 1), 1 - k % 2, matrix_of, stationary)


def full_matrices(transforms):
    return mm(transforms, centring()) + 1.0 / K


def column(ref, i):
    return ref.at[pl.ds(row_of(i), XROWS)]


def first_kernel(
    count_any, cell_any, value_any, weight_any, ens_any,
    applied, blend_ref, middle_ref,
    count_ref, cell_ref, given, cells_ref, ens, ens32, picked, rows, deviations, scaled, matrices, stationary,
    stat_x, stat_y, got_x, got_y, nearby, transforms, own_ref,
    small_sem, load_sem, send_x, recv_x, send_y, recv_y, send_t, recv_t,
):
    gx, gy = lax.axis_index("gx"), lax.axis_index("gy")
    nx, ny = lax.axis_size("gx"), lax.axis_size("gy")

    def at(a, b):
        return (lax.rem(gx + a + nx, nx), lax.rem(gy + b + ny, ny))

    small = [
        pltpu.make_async_copy(count_any, count_ref, small_sem.at[0]),
        pltpu.make_async_copy(cell_any, cell_ref, small_sem.at[1]),
        pltpu.make_async_copy(cell_any, cells_ref, small_sem.at[2]),
        pltpu.make_async_copy(value_any, given.at[0], small_sem.at[3]),
        pltpu.make_async_copy(weight_any, given.at[1], small_sem.at[4]),
    ]
    for copy in small:
        copy.start()

    @pl.loop(0, CX)
    def _(i):
        pltpu.make_async_copy(column(ens_any, i), column(ens, i), load_sem.at[i]).start()

    partners = [(s, 0) for s in STAT_STEPS] + [(0, s) for s in STAT_STEPS]
    partners += [(a, b) for a in (-1, 1) for b in (-1, 1)]
    barrier = pltpu.get_barrier_semaphore()
    for a, b in partners:
        pl.semaphore_signal(barrier, inc=1, device_id=at(a, b), device_id_type=MESH)

    for copy in small:
        copy.wait()
    count = count_ref[gx, gy]
    slot = lax.broadcasted_iota(jnp.int32, (1, OBS), 1)
    rows[0:1] = jnp.where(slot < count, given[1], 0.0)
    rows[1:2] = given[0]

    @pl.loop(0, CX)
    def _(i):
        pltpu.make_async_copy(column(ens_any, i), column(ens, i), load_sem.at[i]).wait()
        start = pl.multiple_of(i * XROWS, XROWS)
        ens32[pl.ds(start, XROWS)] = ens[pl.ds(start, XROWS)].astype(F32)

    @pl.loop(0, OBS // GATHER)
    def _(g):
        for r in range(GATHER):
            o = g * GATHER + r
            picked[pl.ds(o, 1)] = ens32[pl.ds(cell_ref[0, o], 1)]

    def accumulate(total, lanes, deviation, centre):
        scale, value = rows[0:1, lanes], rows[1:2, lanes]
        anomaly = (scale * deviation).astype(BF16)
        innovation = jnp.broadcast_to(scale * (value - centre), (16, QUART)).astype(BF16)
        return total + mm_nt(jnp.concatenate([anomaly, innovation], axis=0), anomaly)

    def exchange(t, sent, got, send_sem, recv_sem, shift):
        copies = []
        for k, step in enumerate(STAT_STEPS):
            there = STAT_STEPS.index(-step)
            copies.append(
                pltpu.make_async_remote_copy(
                    src_ref=sent.at[t],
                    dst_ref=got.at[t, there],
                    send_sem=send_sem.at[t, k],
                    recv_sem=recv_sem.at[t, there],
                    device_id=at(*shift(step)),
                    device_id_type=MESH,
                )
            )
        return copies

    pending = []

    def settle():
        while pending:
            pending.pop().wait_send()

    def weighted(t, total, got, copies):
        for k in reversed(range(4)):
            copies[STAT_STEPS.index(-STAT_STEPS[k])].wait_recv()
            total = total + STAT_WEIGHTS[k] * got[t, k].astype(F32)
        pending.extend(copies)
        return total

    def apply_some(first, last):
        apply_columns(first, last, lambda slot: matrices[slot * K : (slot + 1) * K], stationary, ens, applied)

    for t in range(ITERS):
        total = jnp.zeros((K + 16, K), F32)
        if t == 0:
            row, col = iotas((K + 16, K))
            centre_rows = jnp.where(row == col, (K - 1.0) / K, jnp.where(row < K, -1.0 / K, 1.0 / K))
            centre_rows = centre_rows.astype(BF16)
            for q in range(OBS // QUART):
                lanes = slice(q * QUART, (q + 1) * QUART)
                moved = mm_nt(centre_rows, picked[lanes].astype(BF16))
                total = accumulate(total, lanes, moved[:K], moved[K : K + 1])
                deviations[:, lanes] = moved[:K]
                rows[2:3, lanes] = moved[K : K + 1]
        else:
            for q in range(OBS // QUART):
                lanes = slice(q * QUART, (q + 1) * QUART)
                fresh = deviations[:, lanes] + mm(transforms[:, 3 * K :], scaled[3 * K :, lanes])
                fresh = fresh.astype(BF16).astype(F32)
                centre = jnp.sum(fresh, axis=0, keepdims=True) * (1.0 / K)
                total = accumulate(total, lanes, fresh - centre, centre)
        own = opened(total[:K], total[K : K + 1])
        stat_x[t] = closed(own)

        if t == 0:
            pl.semaphore_wait(barrier, len(partners))
        copies = exchange(t, stat_x, got_x, send_x, recv_x, lambda step: (step, 0))
        for copy in copies:
            copy.start()
        if t == 0:
            cells = cells_ref[...].astype(F32)
            column_x = jnp.floor((cells + 0.5) * (1.0 / XROWS))
            column_y = jnp.floor((cells - XROWS * column_x + 0.5) * (1.0 / LEV))
            hat_x, hat_y = hats((column_x + 0.5) / CX), hats((column_y + 0.5) / CY)
            for slot in range(9):
                rows[3 + slot : 4 + slot] = hat_x[slot // 3] * hat_y[slot % 3]
        if t == 1:
            for slot in range(9):
                matrices[slot * K : (slot + 1) * K] = full_matrices(transforms[:, lanes_of(slot)])
            apply_some(0, CX // 2)
            settle()
        own = weighted(t, own, got_x, copies)
        stat_y[t] = closed(own)
        copies = exchange(t, stat_y, got_y, send_y, recv_y, lambda step: (0, step))
        for copy in reversed(copies):
            copy.start()
        if t == 1:
            apply_some(CX // 2, CX)
        spread, weights = transform_parts(weighted(t, own, got_y, copies))
        own_ref[t] = closed(opened(spread, weights))
        landing = nearby if t == 0 else blend_ref
        copies = {}
        for k, (a, b) in enumerate(BLEND_STEPS):
            there = slot_of(-a, -b)
            copies[(-a, -b)] = pltpu.make_async_remote_copy(
                src_ref=own_ref.at[t],
                dst_ref=landing.at[there],
                send_sem=send_t.at[t, k],
                recv_sem=recv_t.at[t, there],
                device_id=at(a, b),
                device_id_type=MESH,
            )
        for copy in copies.values():
            copy.start()
        own = slot_of(0, 0)
        if t == 0:
            transforms[:, lanes_of(own)] = (weights + spread).astype(BF16)

            @pl.loop(0, OBS // PART)
            def _(q):
                lanes = pl.ds(pl.multiple_of(q * PART, PART), PART)
                for slot in range(9):
                    part = rows[3 + slot : 4 + slot, lanes] * deviations[:, lanes]
                    scaled[lanes_of(slot), lanes] = part.astype(BF16)

        else:
            settle()
            middle_ref[K : 2 * K] = full_matrices((weights + spread).astype(BF16))
        near, far = BLEND_STEPS[6:], BLEND_STEPS[:6]
        for step in near:
            copies[step].wait_recv()
        for step in near:
            slot = slot_of(*step)
            if t == 0:
                transforms[:, lanes_of(slot)] = unpack_transform(nearby[slot])
            else:
                here = (step[1] + 1) * K
                middle_ref[here : here + K] = full_matrices(unpack_transform(blend_ref[slot]))
        if t == 0:
            for q in range(OBS // QUART):
                lanes = slice(q * QUART, (q + 1) * QUART)
                part = mm(transforms[:, : 3 * K], scaled[: 3 * K, lanes])
                deviations[:, lanes] = rows[2:3, lanes] + part
        for step in far:
            copies[step].wait_recv()
        if t == 0:
            for step in far:
                slot = slot_of(*step)
                transforms[:, lanes_of(slot)] = unpack_transform(nearby[slot])
        pending.extend(copies.values())
    settle()


def last_kernel(nearby, middle, ens, out_any, applied, matrices, stationary, store_sem):
    def ready(slots):
        for slot in slots:
            matrices[slot * K : (slot + 1) * K] = full_matrices(unpack_transform(nearby[slot]))

    def store(i):
        return pltpu.make_async_copy(column(applied, i), column(out_any, i), store_sem.at[i])

    def matrix_of(slot):
        if 3 <= slot < 6:
            return middle[(slot - 3) * K : (slot - 2) * K]
        return matrices[slot * K : (slot + 1) * K]

    ready(range(3))
    blend_column(0, 0, matrix_of, stationary)
    for i in range(CX):
        apply_column(i, i % SLOTS, ens, applied, stationary)
        if i + 1 < CX:
            blend_column(i + 1, (i + 1) % SLOTS, matrix_of, stationary)
        store(i).start()
        if i == 1:
            ready(range(6, 9))

    for i in range(CX):
        store(i).wait()


def shards(ensemble, obs_cell, obs_value, obs_weight, obs_count):
    flat = ensemble.reshape(ROWS, K)
    anywhere = pl.BlockSpec(memory_space=pl.ANY)
    fixed = pl.BlockSpec(memory_space=pltpu.HBM)
    dma = pltpu.SemaphoreType.DMA
    following, blend, middle = pl.pallas_call(
        first_kernel,
        out_shape=(
            jax.ShapeDtypeStruct((ROWS, K), BF16),
            jax.ShapeDtypeStruct((9, PACKED, K), BF16),
            jax.ShapeDtypeStruct((3 * K, K), F32),
        ),
        in_specs=[fixed] * 5,
        out_specs=(pl.BlockSpec(memory_space=pltpu.VMEM),) * 3,
        scratch_shapes=[
            pltpu.SMEM((BX, BY), jnp.int32),
            pltpu.SMEM((1, OBS), jnp.int32),
            pltpu.VMEM((2, 1, OBS), F32),
            pltpu.VMEM((1, OBS), jnp.int32),
            pltpu.VMEM((ROWS, K), BF16),
            pltpu.VMEM((ROWS, K), F32),
            pltpu.VMEM((OBS, K), F32),
            pltpu.VMEM((16, OBS), F32),
            pltpu.VMEM((K, OBS), F32),
            pltpu.VMEM((9 * K, OBS), BF16),
            pltpu.VMEM((9 * K, K), F32),
            pltpu.VMEM((2, 3 * K, 2 * K), BF16),
            pltpu.VMEM((ITERS, PACKED, K), BF16),
            pltpu.VMEM((ITERS, PACKED, K), BF16),
            pltpu.VMEM((ITERS, 4, PACKED, K), BF16),
            pltpu.VMEM((ITERS, 4, PACKED, K), BF16),
            pltpu.VMEM((9, PACKED, K), BF16),
            pltpu.VMEM((K, 9 * K), BF16),
            pltpu.VMEM((ITERS, PACKED, K), BF16),
            dma((5,)),
            dma((CX,)),
            dma((ITERS, 4)),
            dma((ITERS, 4)),
            dma((ITERS, 4)),
            dma((ITERS, 4)),
            dma((ITERS, 8)),
            dma((ITERS, 9)),
        ],
        compiler_params=pltpu.CompilerParams(
            collective_id=0, has_side_effects=True, vmem_limit_bytes=44 * 1024 * 1024
        ),
        name="analyse",
    )(
        *(
            pltpu.with_memory_space_constraint(array, pltpu.HBM)
            for array in (
                obs_count,
                obs_cell.reshape(1, OBS),
                obs_value.reshape(1, OBS),
                obs_weight.reshape(1, OBS),
                flat,
            )
        )
    )
    out = pl.pallas_call(
        last_kernel,
        out_shape=jax.ShapeDtypeStruct((ROWS, K), BF16),
        in_specs=[pl.BlockSpec(memory_space=pltpu.VMEM)] * 3,
        out_specs=fixed,
        scratch_shapes=[
            pltpu.VMEM((ROWS, K), BF16),
            pltpu.VMEM((9 * K, K), F32),
            pltpu.VMEM((SLOTS, 3 * K, 2 * K), BF16),
            dma((CX,)),
        ],
        compiler_params=pltpu.CompilerParams(vmem_limit_bytes=44 * 1024 * 1024),
        name="blend",
    )(blend, middle, following)
    return out.reshape(ensemble.shape)


def solution(mesh):
    placed = (
        P("gx", "gy", None, None),
        P("gx", "gy", None),
        P("gx", "gy", None),
        P("gx", "gy", None),
        P(),
    )
    return jax.shard_map(
        shards, mesh=mesh, in_specs=placed, out_specs=P("gx", "gy", None, None), check_vma=False
    )
```
